32 devices in a mesh: seq: 8 (over z, y), mp: 4 (over x, core).
Axes of the slice: x: 2, y: 2, z: 4, core: 2. Of those that a mesh axis runs over, the one named last changes fastest.
Arguments:
- fresh_queries: bfloat16 [512, 2048], P('seq', 'mp'), may hold values from -120 to 120
- fresh_keys: bfloat16 [512, 1024], P('seq', 'mp'), may hold values from -6 to 6
- fresh_values: bfloat16 [512, 1024], P('seq', 'mp'), may hold values from -6 to 6
- cache: bfloat16 [2, 512, 1024], P(None, 'seq', 'mp'), may hold values from -6 to 6
- pool_root: int32 [8, 32], replicated, may hold values from 0 to 1
- branch_owner: int32 [8], replicated, may hold values from 0 to 7, each once
- branch_len: int32 [8], replicated, may hold values from 1 to 32, 128 in all
- branch_root: int32 [8], replicated, may hold values from 0 to 1
- request_branch: int32 [8, 4], P('seq'), may hold values from 0 to 7
- token_request: int32 [8, 64], P('seq'), may hold values from 0 to 3, never falling along the last dimension, each value on 1 to 32 neighbouring positions
- residual: bfloat16 [512, 2048], P('seq'), may hold values from -1.5 to 1.5
- wo_t: bfloat16 [2048, 2048], P('seq', 'mp'), may hold values from -0.125 to 0.125
- norm_gain: float32 [2048], replicated, may hold values from 0.1 to 1.9
- w_qkv: bfloat16 [2048, 4096], P('seq', 'mp'), may hold values from -0.125 to 0.125
Outputs:
- attn: bfloat16 [512, 2048], P('seq', 'mp')
- stream: bfloat16 [512, 2048], P('seq')
- qkv_next: bfloat16 [512, 4096], P('seq', 'mp')
The draws below stay inside these ranges and needn't reach their ends.
Inputs may be any that keep to these rules, and one draw needn't show every extreme that they name: `token_request`: in each index's row the request number never falls, and each request has 1 to 32 tokens. `branch_owner`: each index of seq holds exactly one branch. `branch_len`: the longest branch has 32 rows.
All inputs are finite; a program needn't handle non-finite values.
Results may differ from the reference program's by a relative error of at most 0.018.
Values may be sent and summed in bfloat16 or wider, within the bound.
No kernel may reach another device: no remote copies, remote signals or barrier semaphores. Data moves between devices by JAX's collectives and lax.ppermute only.
A program may use at most 64 MiB of HBM per device.

```python
import math
import jax
import jax.numpy as jnp
import numpy as np
from jax import lax

D = 2048
QUERY_HEADS = 16
KEY_VALUE_HEADS = 8
HEAD_SIZE = 128
TOKENS_PER_SEQ = 64
REQ_DEV = 4
ROOT_DEV = 32
BRANCH_CAP = 32
NEW_TOKENS = 512
BRANCHES = 8
ROOTS = 2
CACHED_ROWS = 512
QKVW = 4096
N_SEQ = 8


def drawn_draws(key):
    base_offset = jnp.clip(jax.random.normal(jax.random.fold_in(key, 101), (NEW_TOKENS, KEY_VALUE_HEADS, HEAD_SIZE), jnp.float32), -6.0, 6.0)
    drawn = jnp.clip(jax.random.normal(jax.random.fold_in(key, 102), (NEW_TOKENS, QUERY_HEADS * HEAD_SIZE), jnp.float32), -6.0, 6.0)
    query_rows = drawn
    key_row_block = base_offset.reshape(NEW_TOKENS, KEY_VALUE_HEADS * HEAD_SIZE)
    return (query_rows, key_row_block)


def draw_fresh_queries(key, part):
    query_rows, key_row_block = drawn_draws(key)
    return query_rows.astype(jnp.bfloat16)


def draw_fresh_keys(key, part):
    query_rows, key_row_block = drawn_draws(key)
    return key_row_block.astype(jnp.bfloat16)


def place_ends(values, key, low, largest):
    spot = [jax.random.randint(jax.random.fold_in(key, axis), (), 0, length) for axis, length in enumerate(values.shape)]
    widest = values.shape.index(max(values.shape))
    neighbour = spot[:widest] + [(spot[widest] + 1) % values.shape[widest]] + spot[widest + 1:]
    return values.at[tuple(spot)].set(low).at[tuple(neighbour)].set(largest)


def levels(key, extent, split, low, largest):
    gain = 1.0
    for dim, blocks in split:
        heights = jax.random.uniform(jax.random.fold_in(jax.random.fold_in(key, 6), dim), (blocks,), jnp.float32, low / len(split), largest / len(split))
        gain = gain * jnp.repeat(jnp.exp(heights), extent[dim] // blocks).reshape((-1,) + (1,) * (len(extent) - 1 - dim))
    return gain


def cumulative_ranks(amount, slope):
    portions = [(1 << 20) // math.isqrt(grade ** slope) + 1 for grade in range(1, amount + 1)]
    deviation = 1 + sum(portions) // (1 << 30)
    return np.cumsum(np.array([max(1, weight // deviation) for weight in portions]))


def ranked_ids(rng, shape, amount, skew):
    listing = cumulative_ranks(amount, skew)
    ticket = jax.random.randint(jax.random.fold_in(rng, 1), shape, 0, int(listing[amount - 1]))
    grade = jnp.searchsorted(jnp.asarray(listing, jnp.int32), ticket, side="right")
    return jax.random.permutation(jax.random.fold_in(rng, 2), amount)[grade].astype(jnp.int32)


def profile(amount, total, most, lean):
    portions = [(1 << 20) // math.isqrt(grade ** lean) + 1 for grade in range(2, amount + 1)]
    spare, given = total - most - (amount - 1), [1] * (amount - 1)
    while spare > 0:
        movable = [i for i in range(amount - 1) if given[i] < most]
        whole, left = sum([portions[i] for i in movable]), spare
        for i in movable:
            extra = min(most - given[i], max(1, left * portions[i] // whole), spare)
            given[i] = given[i] + extra
            spare = spare - extra
    return np.array([most] + given)


def uneven(key, amount, total, bound, slope):
    if amount == 2:
        one = jax.random.randint(key, (), max(1, total - bound), min(bound, total - 1) + 1)
        return jnp.stack([one, total - one])
    lengths = jnp.asarray(profile(amount, total, bound, slope), jnp.int32)
    pairs = (amount - 1) // 2
    donor, sink = lengths[1:1 + 2 * pairs:2], lengths[2:2 + 2 * pairs:2]
    slack = jnp.minimum(donor - 1, bound - sink)
    moved = jax.random.randint(jax.random.fold_in(key, 1), (pairs,), 0, 1 << 20) % (slack + 1)
    lengths = lengths.at[1:1 + 2 * pairs:2].set(donor - moved).at[2:2 + 2 * pairs:2].set(sink + moved)
    return lengths[jax.random.permutation(jax.random.fold_in(key, 2), amount)]


def normal_values(stream_key, extent, scale, most, split=(), kind=jnp.bfloat16):
    values = jax.random.normal(stream_key, extent, jnp.float32) * scale
    if len(split) > 0:
        values = levels(stream_key, extent, split, -0.22, 0.18) * values
    return jnp.clip(values, min=-most, max=most).astype(kind)


def setup_inputs(seed: int = 0) -> dict:
    key_list = jax.random.split(jax.random.key(seed), 15)
    fresh_queries = draw_fresh_queries(jax.random.fold_in(key_list[14], 71), 0)
    fresh_keys = draw_fresh_keys(jax.random.fold_in(key_list[14], 71), 0)
    fresh_values = normal_values(key_list[2], (NEW_TOKENS, KEY_VALUE_HEADS * HEAD_SIZE), 1.0, 6.0, ((0, 8), (1, 4)))
    cache = normal_values(key_list[3], (2, CACHED_ROWS, KEY_VALUE_HEADS * HEAD_SIZE), 1.0, 6.0, ((1, 8), (2, 4)))
    pool_root = place_ends(ranked_ids(key_list[4], (N_SEQ, ROOT_DEV), ROOTS, 2), jax.random.fold_in(key_list[4], 3), 0, ROOTS - 1).astype(jnp.int32)
    branch_owner = jax.random.permutation(key_list[5], BRANCHES).astype(jnp.int32)
    branch_len = uneven(key_list[6], BRANCHES, BRANCHES * BRANCH_CAP // 2, BRANCH_CAP, 2).astype(jnp.int32)
    branch_root = place_ends(jax.random.randint(key_list[7], (BRANCHES,), 0, ROOTS), jax.random.fold_in(key_list[7], 1), 0, ROOTS - 1).astype(jnp.int32)
    request_branch = place_ends(ranked_ids(key_list[8], (N_SEQ, REQ_DEV), BRANCHES, 2), jax.random.fold_in(key_list[8], 3), 0, BRANCHES - 1).astype(jnp.int32)
    token_request = jax.vmap(lambda own: jnp.searchsorted(jnp.cumsum(uneven(own, REQ_DEV, TOKENS_PER_SEQ, TOKENS_PER_SEQ // 2, 2)), jnp.arange(TOKENS_PER_SEQ), side="right"))(jax.random.split(key_list[9], N_SEQ)).reshape((N_SEQ, TOKENS_PER_SEQ)).astype(jnp.int32)
    residual = normal_values(key_list[10], (NEW_TOKENS, D), 0.25, 1.5, ((0, 8),))
    wo_t = normal_values(key_list[11], (D, QUERY_HEADS * HEAD_SIZE), (QUERY_HEADS * HEAD_SIZE) ** -0.5, 0.125, ((0, 8), (1, 4)))
    norm_gain = jnp.clip(1.0 + 0.18 * jax.random.normal(key_list[12], (D,), jnp.float32), 0.1, 1.9)
    w_qkv = normal_values(key_list[13], (D, QKVW), D ** -0.5, 0.125, ((0, 8), (1, 4)))
    return {"fresh_queries": fresh_queries, "fresh_keys": fresh_keys, "fresh_values": fresh_values, "cache": cache, "pool_root": pool_root, "branch_owner": branch_owner, "branch_len": branch_len, "branch_root": branch_root, "request_branch": request_branch, "token_request": token_request, "residual": residual, "wo_t": wo_t, "norm_gain": norm_gain, "w_qkv": w_qkv}


def cache_tags(pool_root, branch_owner, branch_len, root_count, slot_count):
    owner_count = pool_root.shape[0]
    branch_count = branch_owner.shape[0]
    branch_ids = jnp.arange(branch_count, dtype=jnp.int32)
    owner_ids = jnp.arange(owner_count, dtype=jnp.int32)
    owned = lax.optimization_barrier(jnp.sum(jnp.where(branch_owner[None, :] == owner_ids[:, None], branch_ids[None, :], 0), axis=1))
    owned_length = lax.optimization_barrier(jnp.sum(jnp.where(branch_ids[None, :] == owned[:, None], branch_len[None, :], 0), axis=1))
    slot_ids = jnp.arange(slot_count, dtype=jnp.int32)
    branch_tags = jnp.where(slot_ids[None, :] < owned_length[:, None], root_count + owned[:, None], -1)
    return jnp.concatenate([pool_root, branch_tags.astype(jnp.int32)], axis=1).reshape(-1)

def device_attention(index, fresh_queries, fresh_keys, fresh_values, cached_keys, cached_values, tags, token_request, request_branch, branch_root):
    query_groups = QUERY_HEADS // KEY_VALUE_HEADS
    begin_index = index * TOKENS_PER_SEQ
    query_rows = lax.dynamic_slice_in_dim(fresh_queries, begin_index, TOKENS_PER_SEQ, 0).astype(jnp.float32).reshape(TOKENS_PER_SEQ, KEY_VALUE_HEADS, query_groups, HEAD_SIZE)
    incoming_keys = lax.dynamic_slice_in_dim(fresh_keys, begin_index, TOKENS_PER_SEQ, 0).astype(jnp.float32).reshape(TOKENS_PER_SEQ, KEY_VALUE_HEADS, HEAD_SIZE)
    incoming_values = lax.dynamic_slice_in_dim(fresh_values, begin_index, TOKENS_PER_SEQ, 0).astype(jnp.float32).reshape(TOKENS_PER_SEQ, KEY_VALUE_HEADS, HEAD_SIZE)
    requests = lax.dynamic_index_in_dim(token_request, index, 0, keepdims=False)
    branches_here = lax.dynamic_index_in_dim(request_branch, index, 0, keepdims=False)
    token_branch = jnp.take(branches_here, requests)
    token_root = jnp.take(branch_root, token_branch)
    all_keys = jnp.concatenate([cached_keys, incoming_keys], axis=0)
    all_values = jnp.concatenate([cached_values, incoming_values], axis=0)
    scores = jnp.einsum('tkgd,rkd->tkgr', query_rows, all_keys) * HEAD_SIZE ** (-0.5)
    pool_seen = (tags[None, :] == token_root[:, None]) | (tags[None, :] == ROOTS + token_branch[:, None])
    positions = jnp.arange(TOKENS_PER_SEQ, dtype=jnp.int32)
    own_seen = (requests[None, :] == requests[:, None]) & (positions[None, :] <= positions[:, None])
    seen = jnp.concatenate([pool_seen, own_seen], axis=1)[:, None, None, :]
    peak = lax.optimization_barrier(jnp.max(jnp.where(seen, scores, -jnp.inf), axis=-1, keepdims=True))
    prob = jnp.where(seen, jnp.exp(scores - peak), 0.0)
    total = lax.optimization_barrier(jnp.sum(prob, axis=-1))
    weight = prob.astype(jnp.bfloat16).astype(jnp.float32)
    mixed = jnp.einsum('tkgr,rkd->tkgd', weight, all_values) / total[..., None]
    return mixed.reshape(TOKENS_PER_SEQ, QUERY_HEADS * HEAD_SIZE).astype(jnp.bfloat16)

def reference(fresh_queries, fresh_keys, fresh_values, cache, pool_root, branch_owner, branch_len, branch_root, request_branch, token_request, residual, wo_t, norm_gain, w_qkv):
    tags = cache_tags(pool_root, branch_owner, branch_len, ROOTS, BRANCH_CAP)
    cached_keys = cache[0].astype(jnp.float32).reshape(CACHED_ROWS, KEY_VALUE_HEADS, HEAD_SIZE)
    cached_values = cache[1].astype(jnp.float32).reshape(CACHED_ROWS, KEY_VALUE_HEADS, HEAD_SIZE)

    def one_device(index):
        return device_attention(index, fresh_queries, fresh_keys, fresh_values, cached_keys, cached_values, tags, token_request, request_branch, branch_root)
    blocks = lax.map(one_device, jnp.arange(N_SEQ, dtype=jnp.int32))
    attn = blocks.reshape(NEW_TOKENS, QUERY_HEADS * HEAD_SIZE)
    projected = lax.dot_general(attn, wo_t, (((1,), (1,)), ((), ())), preferred_element_type=jnp.float32)
    stream = (residual.astype(jnp.float32) + projected).astype(jnp.bfloat16)
    widened = stream.astype(jnp.float32)
    mean_square = lax.optimization_barrier(jnp.mean(widened * widened, axis=-1, keepdims=True))
    normed = (widened * lax.rsqrt(mean_square + 1e-06) * norm_gain[None, :]).astype(jnp.bfloat16)
    qkv_next = jnp.dot(normed, w_qkv, preferred_element_type=jnp.float32).astype(jnp.bfloat16)
    return (attn, stream, qkv_next)
```

```python
import functools

import jax
import jax.numpy as jnp
from jax import lax
from jax.experimental import pallas as pl
from jax.experimental.pallas import tpu as pltpu
from jax.sharding import PartitionSpec as P

QUERY_HEADS = 16
KEY_VALUE_HEADS = 8
HEAD_SIZE = 128
NT = (((1,), (1,)), ((), ()))
TN = (((0,), (0,)), ((), ()))
F32 = jnp.float32
BF16 = jnp.bfloat16


def cache_tags(pool_root, branch_owner, branch_len, root_count, slot_count, owner_ids):
    branch_count = branch_owner.shape[0]
    branch_ids = jnp.arange(branch_count, dtype=jnp.int32)
    owned = jnp.sum(
        jnp.where(branch_owner[None, :] == owner_ids[:, None], branch_ids[None, :], 0), axis=1
    )
    owned_length = jnp.sum(
        jnp.where(branch_ids[None, :] == owned[:, None], branch_len[None, :], 0), axis=1
    )
    slot_ids = jnp.arange(slot_count, dtype=jnp.int32)
    branch_tags = jnp.where(
        slot_ids[None, :] < owned_length[:, None], root_count + owned[:, None], -1
    )
    return jnp.concatenate([pool_root, branch_tags], axis=1).reshape(-1)


def token_nodes(request_branch, token_request, branch_root):
    requests = token_request[0]
    local_branches = request_branch[0]
    request_ids = jnp.arange(local_branches.shape[0], dtype=jnp.int32)
    token_branch = jnp.sum(
        jnp.where(requests[:, None] == request_ids[None, :], local_branches[None, :], 0), axis=1
    )
    branch_ids = jnp.arange(branch_root.shape[0], dtype=jnp.int32)
    token_root = jnp.sum(
        jnp.where(token_branch[:, None] == branch_ids[None, :], branch_root[None, :], 0), axis=1
    )
    return requests, token_branch, token_root


def attend_kernel(*refs):
    q_ref, kf_ref, vf_ref, bias_ref = refs[:4]
    cache_refs, out_ref = refs[4:-1], refs[-1]
    tok = q_ref.shape[0]
    bias = bias_ref[...]
    for k in range(kf_ref.shape[1] // HEAD_SIZE):
        lanes = slice(k * HEAD_SIZE, (k + 1) * HEAD_SIZE)
        first = slice(2 * k * HEAD_SIZE, (2 * k + 1) * HEAD_SIZE)
        second = slice((2 * k + 1) * HEAD_SIZE, (2 * k + 2) * HEAD_SIZE)
        keys = jnp.concatenate([kf_ref[:, lanes]] + [c[0, :, lanes] for c in cache_refs], axis=0)
        values = jnp.concatenate([vf_ref[:, lanes]] + [c[1, :, lanes] for c in cache_refs], axis=0)
        queries = jnp.concatenate([q_ref[:, first], q_ref[:, second]], axis=0)
        scores = (
            lax.dot_general(keys, queries, NT, preferred_element_type=F32) * HEAD_SIZE**-0.5 + bias
        )
        peak = jnp.max(scores, axis=0, keepdims=True)
        prob = jnp.exp(scores - peak)
        total = jnp.sum(prob, axis=0, keepdims=True)
        mixed = lax.dot_general(values, prob.astype(BF16), TN, preferred_element_type=F32)
        attn = (mixed / total).T.astype(BF16)
        out_ref[:, first] = attn[:tok]
        out_ref[:, second] = attn[tok:]


def project_kernel(a0, a1, a2, a3, own_ref, par_ref, o0, o1, o2, o3, hold):
    m = lax.axis_index("mp")
    attn = jnp.concatenate([a0[...], a1[...], a2[...], a3[...]], axis=0)
    half = own_ref.shape[0]
    hold[:, :half] = lax.dot_general(attn, own_ref[...], NT, preferred_element_type=F32)
    hold[:, half:] = lax.dot_general(attn, par_ref[...], NT, preferred_element_type=F32)
    width = o0.shape[1]
    for j, out in enumerate((o0, o1, o2, o3)):
        at = pl.multiple_of((m ^ j) * width, width)
        out[...] = hold[:, pl.ds(at, width)].astype(out.dtype)


def residual_offset(e, k, half, width):
    return pl.multiple_of((e ^ (k // 2)) * half + (k % 2) * width, width)


def pick_kernel(res_ref, o1, o2, o3):
    e, m = lax.axis_index("seq"), lax.axis_index("mp")
    width = o1.shape[1]
    for s, out in ((1, o1), (2, o2), (3, o3)):
        at = residual_offset(e ^ (2 * s), m, 2 * width, width)
        out[...] = res_ref[:, pl.ds(at, width)]


def combine_kernel(r0, r1, r2, r3, res_ref, s1, s2, s3, out, t0, t1, t2, t3):
    e, m = lax.axis_index("seq"), lax.axis_index("mp")
    width = out.shape[1]
    tok = res_ref.shape[0]
    at = residual_offset(e, m, 2 * width, width)
    rest = jnp.concatenate([res_ref[:, pl.ds(at, width)], s1[...], s2[...], s3[...]], axis=0)
    total = r0[...] + r1[...].astype(F32) + r2[...].astype(F32) + r3[...].astype(F32)
    stream = (rest.astype(F32) + total).astype(BF16)
    out[...] = stream
    for s, part in enumerate((t0, t1, t2, t3)):
        part[...] = stream[s * tok : (s + 1) * tok]


def qkv_kernel(
    x0, x1, x2, x3, gain_ref, own_ref, par_ref, t0, t1, t2, t3, o0, o1, o2, o3, piece, hold
):
    e, m = lax.axis_index("seq"), lax.axis_index("mp")
    width = x0.shape[1]
    half = 2 * width
    tok = o0.shape[0]
    for j, part in enumerate((x0, x1, x2, x3)):
        k = m ^ j
        gain = gain_ref[:, pl.ds(residual_offset(e, k, half, width), width)]
        hold[:, pl.ds(pl.multiple_of(k * width, width), width)] = (
            part[...].astype(F32) * gain
        ).astype(BF16)
    for s, part in enumerate((t0, t1, t2, t3)):
        piece[:, s * width : (s + 1) * width] = part[...]
    for s, out in enumerate((o1, o2, o3, o0)):
        rows = slice(((s + 1) % 4) * tok, ((s + 1) % 4 + 1) * tok)
        out[...] = (
            jnp.dot(hold[rows, :half], own_ref[...], preferred_element_type=F32)
            + jnp.dot(hold[rows, half:], par_ref[...], preferred_element_type=F32)
        ).astype(out.dtype)


def finish_kernel(y0, y1, y2, y3, p0, p1, p2, p3, qkv_ref, stream_ref):
    e, m = lax.axis_index("seq"), lax.axis_index("mp")
    width = p0.shape[1] // 4
    squares = jnp.zeros((p0.shape[0], width), F32)
    for j, part in enumerate((p0, p1, p2, p3)):
        for s in range(4):
            block = part[:, s * width : (s + 1) * width]
            wide = block.astype(F32)
            squares = squares + wide * wide
            at = residual_offset(e ^ (2 * s), m ^ j, 2 * width, width)
            stream_ref[:, pl.ds(at, width)] = block
    mean_square = jnp.sum(squares, axis=1, keepdims=True) / stream_ref.shape[1]
    total = y0[...] + y1[...].astype(F32) + y2[...].astype(F32) + y3[...].astype(F32)
    qkv_ref[...] = (total * lax.rsqrt(mean_square + 1e-06)).astype(BF16)


def call(kernel, out_shape, args, scratch=(), flops=0, moved=1 << 20):
    return pl.pallas_call(
        kernel,
        out_shape=out_shape,
        in_specs=[pl.BlockSpec(memory_space=pltpu.VMEM)] * len(args),
        out_specs=jax.tree.map(lambda _: pl.BlockSpec(memory_space=pltpu.VMEM), out_shape),
        scratch_shapes=list(scratch),
        compiler_params=pltpu.CompilerParams(vmem_limit_bytes=24 << 20),
        cost_estimate=pl.CostEstimate(flops=flops, bytes_accessed=moved, transcendentals=0),
    )(*args)


def swap(value, axis, count, bits):
    return lax.ppermute(value, axis, [(i, i ^ bits) for i in range(count)])


def on_block(
    fresh_queries,
    fresh_keys,
    fresh_values,
    cache,
    pool_root,
    branch_owner,
    branch_len,
    branch_root,
    request_branch,
    token_request,
    residual,
    wo_t,
    norm_gain,
    w_qkv,
):
    seq_count = lax.axis_size("seq")
    root_count = seq_count // 4
    tok = fresh_queries.shape[0]
    e = lax.axis_index("seq")

    blocks = [cache] + [swap(cache, "seq", 8, s) for s in range(1, 8)]
    wo_pair = swap(wo_t, "seq", 8, 1)
    width = wo_t.shape[0] // 2
    sds = jax.ShapeDtypeStruct
    picked = call(pick_kernel, [sds((tok, width), BF16)] * 3, (residual,))
    beside = [swap(picked[s - 1], "seq", 8, 2 * s) for s in range(1, 4)]
    wq_pair = swap(w_qkv, "seq", 8, 1)

    relative = e ^ jnp.arange(seq_count, dtype=jnp.int32)
    rows = jnp.arange(seq_count, dtype=jnp.int32)
    pool_relative = jnp.sum(
        jnp.where(relative[:, None, None] == rows[None, :, None], pool_root[None], 0), axis=1
    )
    slot_count = cache.shape[1] - pool_root.shape[1]
    tags = cache_tags(pool_relative, branch_owner, branch_len, root_count, slot_count, relative)
    requests, token_branch, token_root = token_nodes(request_branch, token_request, branch_root)
    positions = jnp.arange(tok, dtype=jnp.int32)
    own_seen = (requests[None, :] == requests[:, None]) & (
        positions[:, None] <= positions[None, :]
    )
    pool_seen = (tags[:, None] == token_root[None, :]) | (
        tags[:, None] == root_count + token_branch[None, :]
    )
    seen = jnp.concatenate([own_seen, pool_seen], axis=0)
    bias = jnp.where(jnp.concatenate([seen, seen], axis=1), 0.0, -1e30).astype(F32)

    attn = call(
        attend_kernel,
        sds(fresh_queries.shape, BF16),
        (fresh_queries, fresh_keys, fresh_values, bias, *blocks),
        flops=1 << 26,
    )
    attns = [attn] + [swap(attn, "seq", 8, 2 * s) for s in range(1, 4)]
    sums = call(
        project_kernel,
        [sds((4 * tok, width), F32)] + [sds((4 * tok, width), BF16)] * 3,
        (*attns, wo_t, wo_pair),
        scratch=[pltpu.VMEM((4 * tok, 4 * width), F32)],
        flops=1 << 27,
    )
    sums = [sums[0]] + [swap(sums[j], "mp", 4, j) for j in range(1, 4)]
    made = call(
        combine_kernel,
        [sds((4 * tok, width), BF16)] + [sds((tok, width), BF16)] * 4,
        (*sums, residual, *beside),
    )
    stream_parts = [made[0]] + [swap(made[0], "mp", 4, j) for j in range(1, 4)]
    home = [made[1]] + [swap(made[1 + s], "seq", 8, 2 * s) for s in range(1, 4)]
    columns = w_qkv.shape[1]
    partial = call(
        qkv_kernel,
        [sds((tok, columns), F32)]
        + [sds((tok, columns), BF16)] * 3
        + [sds((tok, 4 * width), BF16)],
        (*stream_parts, norm_gain[None, :], w_qkv, wq_pair, *home),
        scratch=[pltpu.VMEM((4 * tok, 4 * width), BF16)],
        flops=1 << 28,
    )
    back = [partial[0]] + [swap(partial[s], "seq", 8, 2 * s) for s in range(1, 4)]
    pieces = [partial[4]] + [swap(partial[4], "mp", 4, j) for j in range(1, 4)]
    qkv_next, stream = call(
        finish_kernel,
        [sds((tok, columns), BF16), sds(residual.shape, BF16)],
        (*back, *pieces),
    )
    return attn, stream, qkv_next


def absorb(running, query_rows, key_row_block, value_rows, visible, score_scale):
    peak_old, total, mixed = running
    scores = (
        jnp.einsum("tkgd,rkd->tkgr", query_rows, key_row_block, preferred_element_type=jnp.float32)
        * score_scale
    )
    seen = visible[:, None, None, :]
    peak_new = jnp.maximum(peak_old, jnp.max(jnp.where(seen, scores, -jnp.inf), axis=-1))
    factor = jnp.exp(peak_old - peak_new)
    weights_full = jnp.where(seen, jnp.exp(scores - peak_new[..., None]), 0.0)
    total = total * factor + jnp.sum(weights_full, axis=-1)
    mixed = mixed * factor[..., None] + jnp.einsum(
        "tkgr,rkd->tkgd",
        weights_full.astype(jnp.bfloat16),
        value_rows,
        preferred_element_type=jnp.float32,
    )
    return (peak_new, total, mixed)


def on_device(
    fresh_queries,
    fresh_keys,
    fresh_values,
    cache,
    pool_root,
    branch_owner,
    branch_len,
    branch_root,
    request_branch,
    token_request,
    residual,
    wo_t,
    norm_gain,
    w_qkv,
):
    seq_count = lax.axis_size("seq")
    root_count = seq_count // 4
    tok_rows = fresh_queries.shape[0]
    kv_local = fresh_keys.shape[1] // HEAD_SIZE
    query_groups = QUERY_HEADS // KEY_VALUE_HEADS
    score_scale = HEAD_SIZE ** (-0.5)
    slot_count = cache.shape[1] - pool_root.shape[1]
    owner_ids = jnp.arange(seq_count, dtype=jnp.int32)
    tags = cache_tags(pool_root, branch_owner, branch_len, root_count, slot_count, owner_ids)
    requests, token_branch, token_root = token_nodes(request_branch, token_request, branch_root)
    query_rows = fresh_queries.reshape(tok_rows, kv_local, query_groups, HEAD_SIZE)
    incoming_keys = fresh_keys.reshape(tok_rows, kv_local, HEAD_SIZE)
    incoming_values = fresh_values.reshape(tok_rows, kv_local, HEAD_SIZE)
    positions = jnp.arange(tok_rows, dtype=jnp.int32)
    own_visible = (requests[None, :] == requests[:, None]) & (
        positions[None, :] <= positions[:, None]
    )
    start_state = (
        jnp.full((tok_rows, kv_local, query_groups), -jnp.inf, jnp.float32),
        jnp.zeros((tok_rows, kv_local, query_groups), jnp.float32),
        jnp.zeros((tok_rows, kv_local, query_groups, HEAD_SIZE), jnp.float32),
    )
    state = absorb(
        start_state, query_rows, incoming_keys, incoming_values, own_visible, score_scale
    )
    piece = lax.all_gather(cache, "seq", axis=1, tiled=True)
    rows = piece.shape[1]
    block = 512 if rows > 512 and rows % 512 == 0 else rows
    key_blocks = piece[0].reshape(rows // block, block, kv_local, HEAD_SIZE)
    value_blocks = piece[1].reshape(rows // block, block, kv_local, HEAD_SIZE)
    tag_blocks = tags.reshape(rows // block, block)

    def one_block(running, parts):
        key_row_block, value_rows, tag_rows = parts
        visible = (tag_rows[None, :] == token_root[:, None]) | (
            tag_rows[None, :] == root_count + token_branch[:, None]
        )
        updated = absorb(running, query_rows, key_row_block, value_rows, visible, score_scale)
        return (updated, None)

    state, unused = lax.scan(one_block, state, (key_blocks, value_blocks, tag_blocks))
    peak_final, total_final, mixed_final = state
    attn = (
        (mixed_final / total_final[..., None])
        .reshape(tok_rows, kv_local * query_groups * HEAD_SIZE)
        .astype(jnp.bfloat16)
    )
    partial_value = lax.dot_general(
        attn,
        lax.all_gather(wo_t, "seq", axis=0, tiled=True),
        (((1,), (1,)), ((), ())),
        preferred_element_type=jnp.float32,
    )
    summed = lax.psum(partial_value.astype(jnp.bfloat16), "mp").astype(jnp.float32)
    stream = (residual.astype(jnp.float32) + summed).astype(jnp.bfloat16)
    widened = stream.astype(jnp.float32)
    mean_square = jnp.mean(widened * widened, axis=-1, keepdims=True)
    normed = (widened * lax.rsqrt(mean_square + 1e-06) * norm_gain[None, :]).astype(jnp.bfloat16)
    qkv_sum = jnp.dot(
        normed, lax.all_gather(w_qkv, "seq", axis=0, tiled=True), preferred_element_type=jnp.float32
    )
    return (attn, stream, qkv_sum.astype(jnp.bfloat16))


def solution(mesh):
    small = mesh.shape["seq"] == 8 and mesh.shape["mp"] == 4
    return jax.shard_map(
        on_block if small else on_device,
        mesh=mesh,
        in_specs=(
            P("seq", "mp"),
            P("seq", "mp"),
            P("seq", "mp"),
            P(None, "seq", "mp"),
            P(),
            P(),
            P(),
            P(),
            P("seq", None),
            P("seq", None),
            P("seq", None),
            P("seq", "mp"),
            P(),
            P("seq", "mp"),
        ),
        out_specs=(P("seq", "mp"), P("seq", None), P("seq", "mp")),
        check_vma=False,
    )
```

```python
import jax
import jax.numpy as jnp
from jax import lax
from jax.experimental import pallas as pl
from jax.experimental.pallas import tpu as pltpu
from jax.sharding import PartitionSpec as P

QUERY_HEADS = 16
KEY_VALUE_HEADS = 8
HEAD_SIZE = 128
NT = (((1,), (1,)), ((), ()))
TN = (((0,), (0,)), ((), ()))
F32 = jnp.float32
HIDDEN = -1e30
BF16 = jnp.bfloat16


def cache_tags(pool_root, branch_owner, branch_len, root_count, slot_count, owner_ids):
    branch_count = branch_owner.shape[0]
    branch_ids = jnp.arange(branch_count, dtype=jnp.int32)
    owned = jnp.sum(
        jnp.where(branch_owner[None, :] == owner_ids[:, None], branch_ids[None, :], 0), axis=1
    )
    owned_length = jnp.sum(
        jnp.where(branch_ids[None, :] == owned[:, None], branch_len[None, :], 0), axis=1
    )
    slot_ids = jnp.arange(slot_count, dtype=jnp.int32)
    branch_tags = jnp.where(
        slot_ids[None, :] < owned_length[:, None], root_count + owned[:, None], -1
    )
    return jnp.concatenate([pool_root, branch_tags], axis=1).reshape(-1)


def token_nodes(request_branch, token_request, branch_root):
    requests = token_request[0]
    local_branches = request_branch[0]
    request_ids = jnp.arange(local_branches.shape[0], dtype=jnp.int32)
    token_branch = jnp.sum(
        jnp.where(requests[:, None] == request_ids[None, :], local_branches[None, :], 0), axis=1
    )
    branch_ids = jnp.arange(branch_root.shape[0], dtype=jnp.int32)
    token_root = jnp.sum(
        jnp.where(token_branch[:, None] == branch_ids[None, :], branch_root[None, :], 0), axis=1
    )
    return requests, token_branch, token_root


def feature_offset(e, half):
    return pl.multiple_of(e * half, half)


def distances(c):
    return (1 - c, c, 3 - c, 2 + c)


def head_lanes(h):
    return slice(h * HEAD_SIZE, (h + 1) * HEAD_SIZE)


def softmax_part(q_ref, k, keys, values, bias):
    queries = jnp.concatenate([q_ref[:, head_lanes(2 * k)], q_ref[:, head_lanes(2 * k + 1)]], axis=0)
    scores = (
        lax.dot_general(keys, queries, NT, preferred_element_type=F32) * HEAD_SIZE**-0.5 + bias
    )
    peak = jnp.max(scores, axis=0, keepdims=True)
    prob = jnp.exp(scores - peak)
    total = jnp.sum(prob, axis=0, keepdims=True)
    mixed = lax.dot_general(values, prob.astype(BF16), TN, preferred_element_type=F32)
    log_sum = jnp.broadcast_to(peak + jnp.log(total), mixed.shape)
    return (mixed / total).T, log_sum.T


def lend_kernel(ask_ref, tags_ref, roots_ref, c0, c1, c2, c3, out_ref):
    tok = ask_ref.shape[0]
    caches = (c0, c1, c2, c3)
    heads = 2 * c0.shape[2] // HEAD_SIZE
    wide = heads * HEAD_SIZE
    lane = lax.broadcasted_iota(jnp.int32, (tok, HEAD_SIZE), 1)
    facts = ask_ref[:, wide:].astype(F32)
    request = facts[:, :1].astype(jnp.int32) + 1
    branch = jnp.sum(jnp.where(lane == request, facts, 0.0), axis=1, keepdims=True)
    branch = branch.astype(jnp.int32)
    root_count = lax.axis_size("seq") // 4
    ids = lax.broadcasted_iota(jnp.int32, (tok, roots_ref.shape[1]), 1)
    root = jnp.sum(
        jnp.where(ids == branch, roots_ref[...].astype(F32), 0.0), axis=1, keepdims=True
    ).astype(jnp.int32)
    seen = (tags_ref[...] == root) | (tags_ref[...] == root_count + branch)
    bias = jnp.where(seen, 0.0, HIDDEN).astype(F32).T
    bias = jnp.concatenate([bias, bias], axis=1)
    stats = jnp.zeros((tok, HEAD_SIZE), F32)
    for k in range(heads // 2):
        keys = jnp.concatenate([c[0, :, head_lanes(k)] for c in caches], axis=0)
        values = jnp.concatenate([c[1, :, head_lanes(k)] for c in caches], axis=0)
        mixed, log_sum = softmax_part(ask_ref, k, keys, values, bias)
        for g in range(2):
            h, rows = 2 * k + g, slice(g * tok, (g + 1) * tok)
            out_ref[:, head_lanes(h)] = mixed[rows].astype(BF16)
            rest = log_sum[rows]
            for i in range(3):
                digit = rest.astype(BF16).astype(F32)
                stats = jnp.where(lane == i * heads + h, digit, stats)
                rest = rest - digit
    out_ref[:, wide:] = stats.astype(BF16)


def own_kernel(q_ref, kf_ref, vf_ref, bias_ref, c0, c1, c2, c3, out_ref, log_ref):
    tok = q_ref.shape[0]
    caches = (c0, c1, c2, c3)
    bias = bias_ref[...]
    lane = lax.broadcasted_iota(jnp.int32, (tok, HEAD_SIZE), 1)
    logs = jnp.zeros((tok, HEAD_SIZE), F32)
    for k in range(kf_ref.shape[1] // HEAD_SIZE):
        lanes = head_lanes(k)
        keys = jnp.concatenate([kf_ref[:, lanes]] + [c[0, :, lanes] for c in caches], axis=0)
        values = jnp.concatenate([vf_ref[:, lanes]] + [c[1, :, lanes] for c in caches], axis=0)
        mixed, log_sum = softmax_part(q_ref, k, keys, values, bias)
        for g in range(2):
            h, rows = 2 * k + g, slice(g * tok, (g + 1) * tok)
            out_ref[:, head_lanes(h)] = mixed[rows]
            logs = jnp.where(lane == h, log_sum[rows], logs)
    log_ref[...] = logs


def merge_kernel(mine_ref, log_ref, lent_ref, res_ref, out_ref, s1, s2, s3, s4):
    e, m = lax.axis_index("seq"), lax.axis_index("mp")
    wide = mine_ref.shape[1]
    heads = wide // HEAD_SIZE
    sends = (s1, s2, s3, s4)
    digits = lent_ref[:, wide:].astype(F32)
    for h in range(heads):
        mine = log_ref[:, h : h + 1]
        lent = (digits[:, h : h + 1] + digits[:, heads + h : heads + h + 1]) + digits[
            :, 2 * heads + h : 2 * heads + h + 1
        ]
        top = jnp.maximum(mine, lent)
        mine, lent = jnp.exp(mine - top), jnp.exp(lent - top)
        both = mine * mine_ref[:, head_lanes(h)] + lent * lent_ref[:, head_lanes(h)].astype(F32)
        attn = (both / (mine + lent)).astype(BF16)
        for ref in (out_ref, *sends):
            ref[:, head_lanes(h)] = attn
    quarter = s1.shape[1] - wide
    for s, ref in zip(distances(m % 2), sends):
        at = feature_offset(e ^ (2 * s) ^ (m // 2), 2 * quarter) + (m % 2) * quarter
        ref[:, wide:] = res_ref[:, pl.ds(pl.multiple_of(at, quarter), quarter)]


def project_kernel(g1, g2, g3, g4, own_ref, y_ref, core_ref, both_ref, out_ref, hold):
    m = lax.axis_index("mp")
    half, wide = own_ref.shape
    tok = g1.shape[0]
    quarter = half // 2
    mine = jnp.concatenate([g2[:, :wide], g4[:, :wide]], axis=0)
    other = jnp.concatenate([g1[:, :wide], g3[:, :wide]], axis=0)
    for h, (w_mine, w_other) in enumerate(((own_ref, core_ref), (y_ref, both_ref))):
        hold[:, h * half : (h + 1) * half] = lax.dot_general(
            mine, w_mine[...], NT, preferred_element_type=F32
        ) + lax.dot_general(other, w_other[...], NT, preferred_element_type=F32)
    for k, (first, second) in ((m, (g2, g4)), (m ^ 1, (g1, g3))):
        at = pl.ds(pl.multiple_of(k * quarter, quarter), quarter)
        hold[:tok, at] += first[:, wide:].astype(F32)
        hold[tok:, at] += second[:, wide:].astype(F32)
    out_ref[...] = hold[...].astype(BF16)


def qkv_kernel(stream_ref, gain_ref, own_ref, y_ref, core_ref, both_ref, o1, o2, o3, o4):
    e = lax.axis_index("seq")
    half = own_ref.shape[0]
    tok = o1.shape[0]
    stream = stream_ref[...].astype(F32)
    near = gain_ref[:, pl.ds(feature_offset(e, half), half)]
    far = gain_ref[:, pl.ds(feature_offset(e ^ 1, half), half)]
    left = (stream[:, :half] * near).astype(BF16)
    right = (stream[:, half:] * far).astype(BF16)
    for first, second, w_left, w_right in ((o1, o3, core_ref, both_ref), (o2, o4, own_ref, y_ref)):
        product = jnp.dot(left, w_left[...], preferred_element_type=F32) + jnp.dot(
            right, w_right[...], preferred_element_type=F32
        )
        first[...] = product[:tok].astype(BF16)
        second[...] = product[tok:].astype(BF16)


def pack_kernel(h1, h2, out_ref):
    width = h1.shape[1]
    out_ref[:, :width] = h1[...]
    out_ref[:, width:] = h2[...]


def add_kernel(a_ref, b_ref, out_ref, first_ref, second_ref):
    tok = first_ref.shape[0]
    stream = (a_ref[...].astype(F32) + b_ref[...].astype(F32)).astype(BF16)
    out_ref[...] = stream
    first_ref[...] = stream[:tok]
    second_ref[...] = stream[tok:]


def finish_kernel(y1, y2, y3, y4, near_ref, far_ref, qkv_ref, stream_ref):
    e, m = lax.axis_index("seq"), lax.axis_index("mp")
    half = near_ref.shape[1] // 4
    tok, width = stream_ref.shape
    squares = jnp.zeros((tok, half), F32)
    for ref, c in ((near_ref, m % 2), (far_ref, 1 - m % 2)):
        for i, s in enumerate((c, 2 + c)):
            for y in range(2):
                block = ref[:, (2 * i + y) * half : (2 * i + y + 1) * half]
                stream_ref[:, pl.ds(feature_offset(e ^ (2 * s) ^ y, half), half)] = block
                wide = block.astype(F32)
                squares = squares + wide * wide
    mean_square = jnp.sum(squares, axis=1, keepdims=True) / width
    total = (y1[...].astype(F32) + y2[...].astype(F32)) + (
        y3[...].astype(F32) + y4[...].astype(F32)
    )
    qkv_ref[...] = (total * lax.rsqrt(mean_square + 1e-06)).astype(BF16)


def call(kernel, out_shape, args, scratch=(), flops=0, moved=1 << 20):
    return pl.pallas_call(
        kernel,
        out_shape=out_shape,
        in_specs=[pl.BlockSpec(memory_space=pltpu.VMEM)] * len(args),
        out_specs=jax.tree.map(lambda _: pl.BlockSpec(memory_space=pltpu.VMEM), out_shape),
        scratch_shapes=list(scratch),
        compiler_params=pltpu.CompilerParams(vmem_limit_bytes=24 << 20),
        cost_estimate=pl.CostEstimate(flops=flops, bytes_accessed=moved, transcendentals=0),
    )(*args)


def swap(value, axis, count, bits):
    return lax.ppermute(value, axis, [(i, i ^ bits) for i in range(count)])


def routes():
    made = []
    for order in range(4):
        pairs = []
        for e in range(8):
            for m in range(4):
                s = distances(m % 2)[order]
                target = (e ^ (2 * s)) * 4 + (m & 2) + s % 2
                pairs.append((e * 4 + m, target))
        made.append(pairs)
    return made


def on_block(
    fresh_queries,
    fresh_keys,
    fresh_values,
    cache,
    pool_root,
    branch_owner,
    branch_len,
    branch_root,
    request_branch,
    token_request,
    residual,
    wo_t,
    norm_gain,
    w_qkv,
):
    seq_count = lax.axis_size("seq")
    root_count = seq_count // 4
    tok, wide = fresh_queries.shape
    half = wo_t.shape[0]
    columns = w_qkv.shape[1]
    e = lax.axis_index("seq")
    sds = jax.ShapeDtypeStruct
    out_routes = routes()
    home_routes = [[(b, a) for a, b in pairs] for pairs in out_routes]

    z2, z3, z1 = (swap(cache, "seq", 8, 2 * s) for s in (2, 3, 1))
    facts = jnp.concatenate(
        [token_request.reshape(tok, 1), jnp.broadcast_to(request_branch, (tok, request_branch.shape[1]))],
        axis=1,
    ).astype(BF16)
    facts = jnp.pad(facts, ((0, 0), (0, HEAD_SIZE - facts.shape[1])))
    ask = swap(jnp.concatenate([fresh_queries, facts], axis=1), "seq", 8, 1)

    near_ids = e ^ (2 * jnp.arange(seq_count // 2, dtype=jnp.int32))
    rows = jnp.arange(seq_count, dtype=jnp.int32)
    near_pool = jnp.sum(
        jnp.where(near_ids[:, None, None] == rows[None, :, None], pool_root[None], 0), axis=1
    )
    slot_count = cache.shape[1] - pool_root.shape[1]
    tags = cache_tags(near_pool, branch_owner, branch_len, root_count, slot_count, near_ids)
    requests, token_branch, token_root = token_nodes(request_branch, token_request, branch_root)
    positions = jnp.arange(tok, dtype=jnp.int32)
    own_seen = (requests[None, :] == requests[:, None]) & (
        positions[:, None] <= positions[None, :]
    )
    near_seen = (tags[:, None] == token_root[None, :]) | (
        tags[:, None] == root_count + token_branch[None, :]
    )
    seen = jnp.concatenate([own_seen, near_seen], axis=0)
    bias = jnp.where(jnp.concatenate([seen, seen], axis=1), 0.0, HIDDEN).astype(F32)

    wo_y = swap(wo_t, "seq", 8, 1)
    near_cache = [cache, z1, z2, z3]
    lend = call(
        lend_kernel,
        sds((tok, wide + HEAD_SIZE), BF16),
        (ask, tags[None, :], branch_root[None, :], *near_cache),
        flops=1 << 25,
    )
    lend, bias = lax.optimization_barrier((lend, bias))
    lent = swap(lend, "seq", 8, 1)
    mine, mine_log = call(
        own_kernel,
        [sds((tok, wide), F32), sds((tok, HEAD_SIZE), F32)],
        (fresh_queries, fresh_keys, fresh_values, bias, *near_cache),
        flops=1 << 25,
    )
    mine, wo_y, wo_later, wq_later = lax.optimization_barrier((mine, wo_y, wo_t, w_qkv))
    wo_core = swap(wo_later, "mp", 4, 1)
    wo_both = swap(wo_y, "mp", 4, 1)
    wq_core = swap(wq_later, "mp", 4, 1)
    wq_y = swap(wq_later, "seq", 8, 1)
    lent, wo_core, wo_both, wq_core = lax.optimization_barrier((lent, wo_core, wo_both, wq_core))
    attn, *sends = call(
        merge_kernel,
        [sds((tok, wide), BF16)] + [sds((tok, wide + half // 2), BF16)] * 4,
        (mine, mine_log, lent, residual),
    )
    g3, g4, g1, g2 = (
        lax.ppermute(sends[i], ("seq", "mp"), out_routes[i]) for i in (2, 3, 0, 1)
    )
    wq_y, g1, g2, g3, g4 = lax.optimization_barrier((wq_y, g1, g2, g3, g4))
    wq_both = swap(wq_y, "mp", 4, 1)
    part = call(
        project_kernel,
        sds((2 * tok, 2 * half), BF16),
        (g1, g2, g3, g4, wo_t, wo_y, wo_core, wo_both),
        scratch=[pltpu.VMEM((2 * tok, 2 * half), F32)],
        flops=1 << 27,
    )
    part_x = swap(part, "mp", 4, 2)
    stream_part, first, second = call(
        add_kernel,
        [sds((2 * tok, 2 * half), BF16)] + [sds((tok, 2 * half), BF16)] * 2,
        (part, part_x),
    )
    home = [
        lax.ppermute(v, ("seq", "mp"), r) for v, r in zip((first, second), home_routes[1::2])
    ]
    made = call(
        qkv_kernel,
        [sds((tok, columns), BF16)] * 4,
        (stream_part, norm_gain[None, :], w_qkv, wq_y, wq_core, wq_both),
        flops=1 << 28,
    )
    back = [lax.ppermute(made[i], ("seq", "mp"), home_routes[i]) for i in (2, 3, 0, 1)]
    home, made = lax.optimization_barrier((home, made))
    near = call(pack_kernel, sds((tok, 4 * half), BF16), tuple(home))
    far = swap(near, "mp", 4, 1)
    qkv_next, stream = call(
        finish_kernel,
        [sds((tok, columns), BF16), sds(residual.shape, BF16)],
        (*back, near, far),
    )
    return attn, stream, qkv_next


def absorb(running, query_rows, key_row_block, value_rows, visible, score_scale):
    peak_old, total, mixed = running
    scores = (
        jnp.einsum("tkgd,rkd->tkgr", query_rows, key_row_block, preferred_element_type=jnp.float32)
        * score_scale
    )
    seen = visible[:, None, None, :]
    peak_new = jnp.maximum(peak_old, jnp.max(jnp.where(seen, scores, -jnp.inf), axis=-1))
    factor = jnp.exp(peak_old - peak_new)
    weights_full = jnp.where(seen, jnp.exp(scores - peak_new[..., None]), 0.0)
    total = total * factor + jnp.sum(weights_full, axis=-1)
    mixed = mixed * factor[..., None] + jnp.einsum(
        "tkgr,rkd->tkgd",
        weights_full.astype(jnp.bfloat16),
        value_rows,
        preferred_element_type=jnp.float32,
    )
    return (peak_new, total, mixed)


def on_device(
    fresh_queries,
    fresh_keys,
    fresh_values,
    cache,
    pool_root,
    branch_owner,
    branch_len,
    branch_root,
    request_branch,
    token_request,
    residual,
    wo_t,
    norm_gain,
    w_qkv,
):
    seq_count = lax.axis_size("seq")
    root_count = seq_count // 4
    tok_rows = fresh_queries.shape[0]
    kv_local = fresh_keys.shape[1] // HEAD_SIZE
    query_groups = QUERY_HEADS // KEY_VALUE_HEADS
    score_scale = HEAD_SIZE ** (-0.5)
    slot_count = cache.shape[1] - pool_root.shape[1]
    owner_ids = jnp.arange(seq_count, dtype=jnp.int32)
    tags = cache_tags(pool_root, branch_owner, branch_len, root_count, slot_count, owner_ids)
    requests, token_branch, token_root = token_nodes(request_branch, token_request, branch_root)
    query_rows = fresh_queries.reshape(tok_rows, kv_local, query_groups, HEAD_SIZE)
    incoming_keys = fresh_keys.reshape(tok_rows, kv_local, HEAD_SIZE)
    incoming_values = fresh_values.reshape(tok_rows, kv_local, HEAD_SIZE)
    positions = jnp.arange(tok_rows, dtype=jnp.int32)
    own_visible = (requests[None, :] == requests[:, None]) & (
        positions[None, :] <= positions[:, None]
    )
    start_state = (
        jnp.full((tok_rows, kv_local, query_groups), -jnp.inf, jnp.float32),
        jnp.zeros((tok_rows, kv_local, query_groups), jnp.float32),
        jnp.zeros((tok_rows, kv_local, query_groups, HEAD_SIZE), jnp.float32),
    )
    state = absorb(
        start_state, query_rows, incoming_keys, incoming_values, own_visible, score_scale
    )
    piece = lax.all_gather(cache, "seq", axis=1, tiled=True)
    rows = piece.shape[1]
    block = 512 if rows > 512 and rows % 512 == 0 else rows
    key_blocks = piece[0].reshape(rows // block, block, kv_local, HEAD_SIZE)
    value_blocks = piece[1].reshape(rows // block, block, kv_local, HEAD_SIZE)
    tag_blocks = tags.reshape(rows // block, block)

    def one_block(running, parts):
        key_row_block, value_rows, tag_rows = parts
        visible = (tag_rows[None, :] == token_root[:, None]) | (
            tag_rows[None, :] == root_count + token_branch[:, None]
        )
        updated = absorb(running, query_rows, key_row_block, value_rows, visible, score_scale)
        return (updated, None)

    state, unused = lax.scan(one_block, state, (key_blocks, value_blocks, tag_blocks))
    peak_final, total_final, mixed_final = state
    attn = (
        (mixed_final / total_final[..., None])
        .reshape(tok_rows, kv_local * query_groups * HEAD_SIZE)
        .astype(jnp.bfloat16)
    )
    partial_value = lax.dot_general(
        attn,
        lax.all_gather(wo_t, "seq", axis=0, tiled=True),
        (((1,), (1,)), ((), ())),
        preferred_element_type=jnp.float32,
    )
    summed = lax.psum(partial_value.astype(jnp.bfloat16), "mp").astype(jnp.float32)
    stream = (residual.astype(jnp.float32) + summed).astype(jnp.bfloat16)
    widened = stream.astype(jnp.float32)
    mean_square = jnp.mean(widened * widened, axis=-1, keepdims=True)
    normed = (widened * lax.rsqrt(mean_square + 1e-06) * norm_gain[None, :]).astype(jnp.bfloat16)
    qkv_sum = jnp.dot(
        normed, lax.all_gather(w_qkv, "seq", axis=0, tiled=True), preferred_element_type=jnp.float32
    )
    return (attn, stream, qkv_sum.astype(jnp.bfloat16))


def solution(mesh):
    small = mesh.shape["seq"] == 8 and mesh.shape["mp"] == 4
    return jax.shard_map(
        on_block if small else on_device,
        mesh=mesh,
        in_specs=(
            P("seq", "mp"),
            P("seq", "mp"),
            P("seq", "mp"),
            P(None, "seq", "mp"),
            P(),
            P(),
            P(),
            P(),
            P("seq", None),
            P("seq", None),
            P("seq", None),
            P("seq", "mp"),
            P(),
            P("seq", "mp"),
        ),
        out_specs=(P("seq", "mp"), P("seq", None), P("seq", "mp")),
        check_vma=False,
    )
```

```python
import jax
import jax.numpy as jnp
from jax import lax
from jax.experimental import pallas as pl
from jax.experimental.pallas import tpu as pltpu
from jax.sharding import Mesh
from jax.sharding import PartitionSpec as P

QUERY_HEADS = 16
KEY_VALUE_HEADS = 8
HEAD_SIZE = 128
NT = (((1,), (1,)), ((), ()))
TN = (((0,), (0,)), ((), ()))
F32 = jnp.float32
HIDDEN = -1e30
BF16 = jnp.bfloat16


def cache_tags(pool_root, branch_owner, branch_len, root_count, slot_count, owner_ids):
    branch_count = branch_owner.shape[0]
    branch_ids = jnp.arange(branch_count, dtype=jnp.int32)
    owned = jnp.sum(
        jnp.where(branch_owner[None, :] == owner_ids[:, None], branch_ids[None, :], 0), axis=1
    )
    owned_length = jnp.sum(
        jnp.where(branch_ids[None, :] == owned[:, None], branch_len[None, :], 0), axis=1
    )
    slot_ids = jnp.arange(slot_count, dtype=jnp.int32)
    branch_tags = jnp.where(
        slot_ids[None, :] < owned_length[:, None], root_count + owned[:, None], -1
    )
    return jnp.concatenate([pool_root, branch_tags], axis=1).reshape(-1)


def token_nodes(request_branch, token_request, branch_root):
    requests = token_request[0]
    local_branches = request_branch[0]
    request_ids = jnp.arange(local_branches.shape[0], dtype=jnp.int32)
    token_branch = jnp.sum(
        jnp.where(requests[:, None] == request_ids[None, :], local_branches[None, :], 0), axis=1
    )
    branch_ids = jnp.arange(branch_root.shape[0], dtype=jnp.int32)
    token_root = jnp.sum(
        jnp.where(token_branch[:, None] == branch_ids[None, :], branch_root[None, :], 0), axis=1
    )
    return requests, token_branch, token_root


def feature_offset(e, half):
    return pl.multiple_of(e * half, half)


def head_lanes(h):
    return slice(h * HEAD_SIZE, (h + 1) * HEAD_SIZE)


def seq_index():
    return 2 * lax.axis_index("z") + lax.axis_index("y")


def own_nodes(request, branches_ref, roots_ref):
    branch, root = jnp.zeros_like(request), jnp.zeros_like(request)
    for r in range(branches_ref.shape[1]):
        b = branches_ref[0, r]
        branch = jnp.where(request == r, b, branch)
        root = jnp.where(request == r, roots_ref[b], root)
    return branch, root


def cache_bias(branch, root, pool_ref, owner_ref, length_ref, root_count):
    e = seq_index()
    owners, slots = pool_ref.shape
    by_row = pool_ref[...].astype(F32).T
    lane = lax.broadcasted_iota(jnp.int32, by_row.shape, 1)
    slot = lax.broadcasted_iota(jnp.int32, (slots, branch.shape[1]), 0)
    pieces = []
    for s in range(owners // 2):
        holder = e ^ (2 * s)
        held = jnp.sum(jnp.where(lane == holder, by_row, 0.0), axis=1, keepdims=True)
        owned, length = 0, 0
        for b in range(owners):
            here = owner_ref[b] == holder
            owned = jnp.where(here, b, owned)
            length = jnp.where(here, length_ref[b], length)
        pieces.append(held.astype(jnp.int32) == root)
        pieces.append((slot < length) & (branch == owned))
    return jnp.concatenate([jnp.where(seen, 0.0, HIDDEN) for seen in pieces], axis=0)


def softmax_part(q_ref, k, keys, values, bias):
    tok = bias.shape[1] // 2
    queries = jnp.concatenate(
        [q_ref[:tok, head_lanes(2 * k)], q_ref[:tok, head_lanes(2 * k + 1)]], axis=0
    )
    scores = (
        lax.dot_general(keys, queries, NT, preferred_element_type=F32) * HEAD_SIZE**-0.5 + bias
    )
    peak = jnp.max(scores, axis=0, keepdims=True)
    prob = jnp.exp(scores - peak)
    total = jnp.sum(prob, axis=0, keepdims=True)
    mixed = lax.dot_general(values, prob.astype(BF16), TN, preferred_element_type=F32)
    log_sum = jnp.broadcast_to(peak + jnp.log(total), mixed.shape)
    return (mixed / total).T, log_sum.T


def ask_kernel(q_ref, request_ref, branches_ref, roots_ref, out_ref):
    tok = q_ref.shape[0]
    branch, root = own_nodes(request_ref[...], branches_ref, roots_ref)
    rows = out_ref.shape[0] - tok
    which = lax.broadcasted_iota(jnp.int32, (rows, tok), 0)
    out_ref[:tok, :] = q_ref[...]
    out_ref[tok:, :tok] = jnp.where(which == 0, branch, root).astype(F32).astype(BF16)


def lend_kernel(ask_ref, pool_ref, owner_ref, length_ref, c0, c1, c2, c3, out_ref):
    tok = out_ref.shape[0]
    caches = (c0, c1, c2, c3)
    heads = 2 * c0.shape[2] // HEAD_SIZE
    wide = heads * HEAD_SIZE
    nodes = ask_ref[tok:, :tok].astype(F32).astype(jnp.int32)
    root_count = lax.axis_size("z") * lax.axis_size("y") // 4
    bias = cache_bias(nodes[:1], nodes[1:2], pool_ref, owner_ref, length_ref, root_count)
    bias = jnp.concatenate([bias, bias], axis=1)
    lane = lax.broadcasted_iota(jnp.int32, (tok, HEAD_SIZE), 1)
    stats = jnp.zeros((tok, HEAD_SIZE), F32)
    for k in range(heads // 2):
        keys = jnp.concatenate([c[0, :, head_lanes(k)] for c in caches], axis=0)
        values = jnp.concatenate([c[1, :, head_lanes(k)] for c in caches], axis=0)
        mixed, log_sum = softmax_part(ask_ref, k, keys, values, bias)
        for g in range(2):
            h, rows = 2 * k + g, slice(g * tok, (g + 1) * tok)
            out_ref[:, head_lanes(h)] = mixed[rows].astype(BF16)
            rest = log_sum[rows]
            for i in range(3):
                digit = rest.astype(BF16).astype(F32)
                stats = jnp.where(lane == i * heads + h, digit, stats)
                rest = rest - digit
    out_ref[:, wide:] = stats.astype(BF16)


def own_kernel(
    q_ref, kf_ref, vf_ref, request_ref, branches_ref, roots_ref, pool_ref, owner_ref, length_ref,
    c0, c1, c2, c3, lend_ref, out_ref, log_ref,
):
    tok = q_ref.shape[0]
    caches = (c0, c1, c2, c3)
    request = request_ref[...]
    branch, root = own_nodes(request, branches_ref, roots_ref)
    root_count = lax.axis_size("z") * lax.axis_size("y") // 4
    down = jnp.broadcast_to(request.astype(F32), (8, tok)).T[:, :1].astype(jnp.int32)
    key_at = lax.broadcasted_iota(jnp.int32, (tok, tok), 0)
    token_at = lax.broadcasted_iota(jnp.int32, (tok, tok), 1)
    fresh = jnp.where((down == request) & (key_at <= token_at), 0.0, HIDDEN)
    bias = jnp.concatenate(
        [fresh, cache_bias(branch, root, pool_ref, owner_ref, length_ref, root_count)], axis=0
    )
    bias = jnp.concatenate([bias, bias], axis=1)
    lane = lax.broadcasted_iota(jnp.int32, (tok, HEAD_SIZE), 1)
    logs = jnp.zeros((tok, HEAD_SIZE), F32)
    for k in range(kf_ref.shape[1] // HEAD_SIZE):
        lanes = head_lanes(k)
        keys = jnp.concatenate([kf_ref[:, lanes]] + [c[0, :, lanes] for c in caches], axis=0)
        values = jnp.concatenate([vf_ref[:, lanes]] + [c[1, :, lanes] for c in caches], axis=0)
        mixed, log_sum = softmax_part(q_ref, k, keys, values, bias)
        for g in range(2):
            h, rows = 2 * k + g, slice(g * tok, (g + 1) * tok)
            out_ref[:, head_lanes(h)] = mixed[rows]
            logs = jnp.where(lane == h, log_sum[rows], logs)
    log_ref[...] = logs


def merge_kernel(mine_ref, log_ref, lent_ref, res_ref, out_ref, send_ref):
    y, m = lax.axis_index("y"), 2 * lax.axis_index("x") + lax.axis_index("c")
    tok, wide = mine_ref.shape
    heads = wide // HEAD_SIZE
    part = tok // 2
    digits = lent_ref[:, wide:].astype(F32)
    for h in range(heads):
        mine = log_ref[:, h : h + 1]
        lent = (digits[:, h : h + 1] + digits[:, heads + h : heads + h + 1]) + digits[
            :, 2 * heads + h : 2 * heads + h + 1
        ]
        top = jnp.maximum(mine, lent)
        mine, lent = jnp.exp(mine - top), jnp.exp(lent - top)
        both = mine * mine_ref[:, head_lanes(h)] + lent * lent_ref[:, head_lanes(h)].astype(F32)
        attn = (both / (mine + lent)).astype(BF16)
        out_ref[:, head_lanes(h)] = attn
        for to in range(send_ref.shape[0]):
            c = to % 2
            send_ref[to, :, head_lanes(h)] = attn[c * part : (c + 1) * part]
    quarter = send_ref.shape[2] - wide
    for z in range(send_ref.shape[0] // 2):
        at = feature_offset((2 * z + y) ^ (m // 2), 2 * quarter) + (m % 2) * quarter
        block = res_ref[:, pl.ds(pl.multiple_of(at, quarter), quarter)]
        for c in range(2):
            send_ref[2 * z + c, :, wide:] = block[c * part : (c + 1) * part]


def project_kernel(g_ref, own_ref, y_ref, core_ref, both_ref, out_ref, hold):
    x, c = lax.axis_index("x"), lax.axis_index("c")
    half, wide = own_ref.shape
    part = g_ref.shape[1]
    quarter = half // 2
    chips = g_ref.shape[0] // 2
    mine = jnp.concatenate([g_ref[2 * z + c, :, :wide] for z in range(chips)], axis=0)
    other = jnp.concatenate([g_ref[2 * z + 1 - c, :, :wide] for z in range(chips)], axis=0)
    for h, (w_mine, w_other) in enumerate(((own_ref, core_ref), (y_ref, both_ref))):
        hold[:, h * half : (h + 1) * half] = lax.dot_general(
            mine, w_mine[...], NT, preferred_element_type=F32
        ) + lax.dot_general(other, w_other[...], NT, preferred_element_type=F32)
    for core in range(2):
        at = pl.ds(pl.multiple_of((2 * x + core) * quarter, quarter), quarter)
        for z in range(chips):
            hold[z * part : (z + 1) * part, at] += g_ref[2 * z + core, :, wide:].astype(F32)
    out_ref[...] = hold[...].astype(BF16)


def qkv_kernel(a_ref, b_ref, gain_ref, own_ref, y_ref, core_ref, both_ref, out_ref):
    e, c = seq_index(), lax.axis_index("c")
    half, columns = own_ref.shape
    part = out_ref.shape[1]
    whole = (a_ref[...].astype(F32) + b_ref[...].astype(F32)).astype(BF16)
    stream = whole.astype(F32)
    near = gain_ref[:, pl.ds(feature_offset(e, half), half)]
    far = gain_ref[:, pl.ds(feature_offset(e ^ 1, half), half)]
    left = (stream[:, :half] * near).astype(BF16)
    right = (stream[:, half:] * far).astype(BF16)
    for core, w_left, w_right in ((c, own_ref, y_ref), (1 - c, core_ref, both_ref)):
        product = jnp.dot(left, w_left[...], preferred_element_type=F32) + jnp.dot(
            right, w_right[...], preferred_element_type=F32
        )
        for z in range(out_ref.shape[0] // 2):
            rows = slice(z * part, (z + 1) * part)
            out_ref[2 * z + core, :, :columns] = product[rows].astype(BF16)
            out_ref[2 * z + core, :, columns:] = whole[rows]


def finish_kernel(got_ref, qkv_ref, stream_ref):
    y = lax.axis_index("y")
    columns = qkv_ref.shape[1]
    part = got_ref.shape[1]
    half = (got_ref.shape[2] - columns) // 2
    for c in range(2):
        rows = slice(c * part, (c + 1) * part)
        squares = jnp.zeros((part, half), F32)
        total = jnp.zeros((part, columns), F32)
        for z in range(got_ref.shape[0] // 2):
            total = total + got_ref[2 * z + c, :, :columns].astype(F32)
            for side in range(2):
                at = columns + side * half
                block = got_ref[2 * z + c, :, at : at + half]
                stream_ref[rows, pl.ds(feature_offset(2 * z + (y ^ side), half), half)] = block
                wide = block.astype(F32)
                squares = squares + wide * wide
        mean_square = jnp.sum(squares, axis=1, keepdims=True) / stream_ref.shape[1]
        qkv_ref[rows, :] = (total * lax.rsqrt(mean_square + 1e-06)).astype(BF16)


def call(kernel, out_shape, args, scratch=(), scalars=(), flops=0, moved=1 << 20):
    vmem, smem = pl.BlockSpec(memory_space=pltpu.VMEM), pl.BlockSpec(memory_space=pltpu.SMEM)
    return pl.pallas_call(
        kernel,
        out_shape=out_shape,
        in_specs=[smem if i in scalars else vmem for i in range(len(args))],
        out_specs=jax.tree.map(lambda _: vmem, out_shape),
        scratch_shapes=list(scratch),
        compiler_params=pltpu.CompilerParams(vmem_limit_bytes=24 << 20),
        cost_estimate=pl.CostEstimate(flops=flops, bytes_accessed=moved, transcendentals=0),
    )(*args)


def swap(value, axis, bits=1):
    return lax.ppermute(value, axis, [(i, i ^ bits) for i in range(lax.axis_size(axis))])


def on_block(
    fresh_queries,
    fresh_keys,
    fresh_values,
    cache,
    pool_root,
    branch_owner,
    branch_len,
    branch_root,
    request_branch,
    token_request,
    residual,
    wo_t,
    norm_gain,
    w_qkv,
):
    tok, wide = fresh_queries.shape
    half = wo_t.shape[0]
    columns = w_qkv.shape[1]
    chips = lax.axis_size("z")
    sds = jax.ShapeDtypeStruct

    z1, z2, z3 = (swap(cache, "z", s) for s in (1, 2, 3))
    caches = (cache, z1, z2, z3)
    ask = swap(
        call(
            ask_kernel,
            sds((tok + 16, wide), BF16),
            (fresh_queries, token_request, request_branch, branch_root),
            scalars=(2, 3),
        ),
        "y",
    )
    wo_y = swap(wo_t, "y")
    lend = call(
        lend_kernel,
        sds((tok, wide + HEAD_SIZE), BF16),
        (ask, pool_root, branch_owner, branch_len, *caches),
        scalars=(2, 3),
        flops=1 << 25,
    )
    lent = swap(lend, "y")
    mine, mine_log = call(
        own_kernel,
        [sds((tok, wide), F32), sds((tok, HEAD_SIZE), F32)],
        (
            fresh_queries, fresh_keys, fresh_values, token_request, request_branch, branch_root,
            pool_root, branch_owner, branch_len, *caches, lend,
        ),
        scalars=(4, 5, 7, 8),
        flops=1 << 25,
    )
    mine, wo_y, wo_later, wq_later = lax.optimization_barrier((mine, wo_y, wo_t, w_qkv))
    wo_core = swap(wo_later, "c")
    wo_both = swap(wo_y, "c")
    wq_core = swap(wq_later, "c")
    wq_y = swap(wq_later, "y")
    attn, send = call(
        merge_kernel,
        [sds((tok, wide), BF16), sds((2 * chips, tok // 2, wide + half // 2), BF16)],
        (mine, mine_log, lent, residual),
    )
    got = lax.all_to_all(send, ("z", "c"), 0, 0, tiled=True)
    part = call(
        project_kernel,
        sds((chips * tok // 2, 2 * half), BF16),
        (got, wo_t, wo_y, wo_core, wo_both),
        scratch=[pltpu.VMEM((chips * tok // 2, 2 * half), F32)],
        flops=1 << 27,
    )
    part_x = swap(part, "x")
    wq_y, part = lax.optimization_barrier((wq_y, part))
    wq_both = swap(wq_y, "c")
    made = call(
        qkv_kernel,
        sds((2 * chips, tok // 2, columns + 2 * half), BF16),
        (part, part_x, norm_gain[None, :], w_qkv, wq_y, wq_core, wq_both),
        flops=1 << 28,
    )
    back = lax.all_to_all(made, ("z", "c"), 0, 0, tiled=True)
    qkv_next, stream = call(
        finish_kernel,
        [sds((tok, columns), BF16), sds(residual.shape, BF16)],
        (back,),
    )
    return attn, stream, qkv_next


def absorb(running, query_rows, key_row_block, value_rows, visible, score_scale):
    peak_old, total, mixed = running
    scores = (
        jnp.einsum("tkgd,rkd->tkgr", query_rows, key_row_block, preferred_element_type=jnp.float32)
        * score_scale
    )
    seen = visible[:, None, None, :]
    peak_new = jnp.maximum(peak_old, jnp.max(jnp.where(seen, scores, -jnp.inf), axis=-1))
    factor = jnp.exp(peak_old - peak_new)
    weights_full = jnp.where(seen, jnp.exp(scores - peak_new[..., None]), 0.0)
    total = total * factor + jnp.sum(weights_full, axis=-1)
    mixed = mixed * factor[..., None] + jnp.einsum(
        "tkgr,rkd->tkgd",
        weights_full.astype(jnp.bfloat16),
        value_rows,
        preferred_element_type=jnp.float32,
    )
    return (peak_new, total, mixed)


def on_device(
    fresh_queries,
    fresh_keys,
    fresh_values,
    cache,
    pool_root,
    branch_owner,
    branch_len,
    branch_root,
    request_branch,
    token_request,
    residual,
    wo_t,
    norm_gain,
    w_qkv,
):
    seq_count = lax.axis_size("seq")
    root_count = seq_count // 4
    tok_rows = fresh_queries.shape[0]
    kv_local = fresh_keys.shape[1] // HEAD_SIZE
    query_groups = QUERY_HEADS // KEY_VALUE_HEADS
    score_scale = HEAD_SIZE ** (-0.5)
    slot_count = cache.shape[1] - pool_root.shape[1]
    owner_ids = jnp.arange(seq_count, dtype=jnp.int32)
    tags = cache_tags(pool_root, branch_owner, branch_len, root_count, slot_count, owner_ids)
    requests, token_branch, token_root = token_nodes(request_branch, token_request, branch_root)
    query_rows = fresh_queries.reshape(tok_rows, kv_local, query_groups, HEAD_SIZE)
    incoming_keys = fresh_keys.reshape(tok_rows, kv_local, HEAD_SIZE)
    incoming_values = fresh_values.reshape(tok_rows, kv_local, HEAD_SIZE)
    positions = jnp.arange(tok_rows, dtype=jnp.int32)
    own_visible = (requests[None, :] == requests[:, None]) & (
        positions[None, :] <= positions[:, None]
    )
    start_state = (
        jnp.full((tok_rows, kv_local, query_groups), -jnp.inf, jnp.float32),
        jnp.zeros((tok_rows, kv_local, query_groups), jnp.float32),
        jnp.zeros((tok_rows, kv_local, query_groups, HEAD_SIZE), jnp.float32),
    )
    state = absorb(
        start_state, query_rows, incoming_keys, incoming_values, own_visible, score_scale
    )
    piece = lax.all_gather(cache, "seq", axis=1, tiled=True)
    rows = piece.shape[1]
    block = 512 if rows > 512 and rows % 512 == 0 else rows
    key_blocks = piece[0].reshape(rows // block, block, kv_local, HEAD_SIZE)
    value_blocks = piece[1].reshape(rows // block, block, kv_local, HEAD_SIZE)
    tag_blocks = tags.reshape(rows // block, block)

    def one_block(running, parts):
        key_row_block, value_rows, tag_rows = parts
        visible = (tag_rows[None, :] == token_root[:, None]) | (
            tag_rows[None, :] == root_count + token_branch[:, None]
        )
        updated = absorb(running, query_rows, key_row_block, value_rows, visible, score_scale)
        return (updated, None)

    state, unused = lax.scan(one_block, state, (key_blocks, value_blocks, tag_blocks))
    peak_final, total_final, mixed_final = state
    attn = (
        (mixed_final / total_final[..., None])
        .reshape(tok_rows, kv_local * query_groups * HEAD_SIZE)
        .astype(jnp.bfloat16)
    )
    partial_value = lax.dot_general(
        attn,
        lax.all_gather(wo_t, "seq", axis=0, tiled=True),
        (((1,), (1,)), ((), ())),
        preferred_element_type=jnp.float32,
    )
    summed = lax.psum(partial_value.astype(jnp.bfloat16), "mp").astype(jnp.float32)
    stream = (residual.astype(jnp.float32) + summed).astype(jnp.bfloat16)
    widened = stream.astype(jnp.float32)
    mean_square = jnp.mean(widened * widened, axis=-1, keepdims=True)
    normed = (widened * lax.rsqrt(mean_square + 1e-06) * norm_gain[None, :]).astype(jnp.bfloat16)
    qkv_sum = jnp.dot(
        normed, lax.all_gather(w_qkv, "seq", axis=0, tiled=True), preferred_element_type=jnp.float32
    )
    return (attn, stream, qkv_sum.astype(jnp.bfloat16))


def solution(mesh):
    small = mesh.shape["seq"] == 8 and mesh.shape["mp"] == 4
    seq, mp = "seq", "mp"
    if small:
        mesh = Mesh(mesh.devices.reshape(4, 2, 2, 2), ("z", "y", "x", "c"))
        seq, mp = ("z", "y"), ("x", "c")
    return jax.shard_map(
        on_block if small else on_device,
        mesh=mesh,
        in_specs=(
            P(seq, mp),
            P(seq, mp),
            P(seq, mp),
            P(None, seq, mp),
            P(),
            P(),
            P(),
            P(),
            P(seq, None),
            P(seq, None),
            P(seq, None),
            P(seq, mp),
            P(),
            P(seq, mp),
        ),
        out_specs=(P(seq, mp), P(seq, None), P(seq, mp)),
        check_vma=False,
    )
```

```python
import jax
import jax.numpy as jnp
from jax import lax
from jax.experimental import pallas as pl
from jax.experimental.pallas import tpu as pltpu
from jax.sharding import Mesh
from jax.sharding import PartitionSpec as P

QUERY_HEADS = 16
KEY_VALUE_HEADS = 8
HEAD_SIZE = 128
NT = (((1,), (1,)), ((), ()))
TN = (((0,), (0,)), ((), ()))
F32 = jnp.float32
HIDDEN = -1e30
BF16 = jnp.bfloat16


def cache_tags(pool_root, branch_owner, branch_len, root_count, slot_count, owner_ids):
    branch_count = branch_owner.shape[0]
    branch_ids = jnp.arange(branch_count, dtype=jnp.int32)
    owned = jnp.sum(
        jnp.where(branch_owner[None, :] == owner_ids[:, None], branch_ids[None, :], 0), axis=1
    )
    owned_length = jnp.sum(
        jnp.where(branch_ids[None, :] == owned[:, None], branch_len[None, :], 0), axis=1
    )
    slot_ids = jnp.arange(slot_count, dtype=jnp.int32)
    branch_tags = jnp.where(
        slot_ids[None, :] < owned_length[:, None], root_count + owned[:, None], -1
    )
    return jnp.concatenate([pool_root, branch_tags], axis=1).reshape(-1)


def token_nodes(request_branch, token_request, branch_root):
    requests = token_request[0]
    local_branches = request_branch[0]
    request_ids = jnp.arange(local_branches.shape[0], dtype=jnp.int32)
    token_branch = jnp.sum(
        jnp.where(requests[:, None] == request_ids[None, :], local_branches[None, :], 0), axis=1
    )
    branch_ids = jnp.arange(branch_root.shape[0], dtype=jnp.int32)
    token_root = jnp.sum(
        jnp.where(token_branch[:, None] == branch_ids[None, :], branch_root[None, :], 0), axis=1
    )
    return requests, token_branch, token_root


def head_lanes(h):
    return slice(h * HEAD_SIZE, (h + 1) * HEAD_SIZE)


def seq_index():
    return 2 * lax.axis_index("z") + lax.axis_index("y")


def own_nodes(request, branches_ref, roots_ref):
    branch, root = jnp.zeros_like(request), jnp.zeros_like(request)
    for r in range(branches_ref.shape[1]):
        b = branches_ref[0, r]
        branch = jnp.where(request == r, b, branch)
        root = jnp.where(request == r, roots_ref[b], root)
    return branch, root


def cache_bias(branch, root, pool_ref, owner_ref, length_ref, root_count):
    e = seq_index()
    owners, slots = pool_ref.shape
    by_row = pool_ref[...].astype(F32).T
    lane = lax.broadcasted_iota(jnp.int32, by_row.shape, 1)
    slot = lax.broadcasted_iota(jnp.int32, (slots, branch.shape[1]), 0)
    pieces = []
    for s in range(owners):
        holder = e ^ s
        held = jnp.sum(jnp.where(lane == holder, by_row, 0.0), axis=1, keepdims=True)
        owned, length = 0, 0
        for b in range(owners):
            here = owner_ref[b] == holder
            owned = jnp.where(here, b, owned)
            length = jnp.where(here, length_ref[b], length)
        pieces.append(held.astype(jnp.int32) == root)
        pieces.append((slot < length) & (branch == owned))
    return jnp.concatenate([jnp.where(seen, 0.0, HIDDEN) for seen in pieces], axis=0)


def chunk_offset(e, k, width):
    return pl.multiple_of((e ^ (k // 2)) * (2 * width) + (k % 2) * width, width)


def mp_index():
    return 2 * lax.axis_index("x") + lax.axis_index("c")


def attend_kernel(
    q_ref, kf_ref, vf_ref, request_ref, branches_ref, roots_ref, pool_ref, owner_ref, length_ref,
    res_ref, *refs,
):
    caches, out_ref, sends = refs[:-5], refs[-5], refs[-4:]
    e, m = seq_index(), mp_index()
    tok, wide = q_ref.shape
    request = request_ref[...]
    branch, root = own_nodes(request, branches_ref, roots_ref)
    root_count = lax.axis_size("z") * lax.axis_size("y") // 4
    down = jnp.broadcast_to(request.astype(F32), (8, tok)).T[:, :1].astype(jnp.int32)
    key_at = lax.broadcasted_iota(jnp.int32, (tok, tok), 0)
    token_at = lax.broadcasted_iota(jnp.int32, (tok, tok), 1)
    fresh = jnp.where((down == request) & (key_at <= token_at), 0.0, HIDDEN)
    bias = jnp.concatenate(
        [fresh, cache_bias(branch, root, pool_ref, owner_ref, length_ref, root_count)], axis=0
    )
    bias = jnp.concatenate([bias, bias], axis=1)
    for k in range(kf_ref.shape[1] // HEAD_SIZE):
        lanes, first, second = head_lanes(k), head_lanes(2 * k), head_lanes(2 * k + 1)
        keys = jnp.concatenate([kf_ref[:, lanes]] + [c[0, :, lanes] for c in caches], axis=0)
        values = jnp.concatenate([vf_ref[:, lanes]] + [c[1, :, lanes] for c in caches], axis=0)
        queries = jnp.concatenate([q_ref[:, first], q_ref[:, second]], axis=0)
        scores = (
            lax.dot_general(keys, queries, NT, preferred_element_type=F32) * HEAD_SIZE**-0.5 + bias
        )
        peak = jnp.max(scores, axis=0, keepdims=True)
        prob = jnp.exp(scores - peak)
        total = jnp.sum(prob, axis=0, keepdims=True)
        mixed = lax.dot_general(values, prob.astype(BF16), TN, preferred_element_type=F32)
        attn = (mixed / total).T.astype(BF16)
        for ref in (out_ref, *sends):
            ref[:, first] = attn[:tok]
            ref[:, second] = attn[tok:]
    width = sends[0].shape[1] - wide
    for s, ref in enumerate(sends):
        ref[:, wide:] = res_ref[:, pl.ds(chunk_offset(e ^ (2 * s), m, width), width)]


def project_kernel(a0, a1, a2, a3, own_ref, par_ref, o0, o1, o2, o3, hold):
    m = mp_index()
    half, wide = own_ref.shape
    blocks = (a0, a1, a2, a3)
    attn = jnp.concatenate([a[:, :wide] for a in blocks], axis=0)
    rest = jnp.concatenate([a[:, wide:] for a in blocks], axis=0)
    hold[:, :half] = lax.dot_general(attn, own_ref[...], NT, preferred_element_type=F32)
    hold[:, half:] = lax.dot_general(attn, par_ref[...], NT, preferred_element_type=F32)
    width = o0.shape[1]
    for j, out in enumerate((o0, o1, o2, o3)):
        chunk = hold[:, pl.ds(pl.multiple_of((m ^ j) * width, width), width)]
        out[...] = chunk + rest.astype(F32) if j == 0 else chunk.astype(BF16)


def combine_kernel(r0, r1, r2, r3, out, t0, t1, t2, t3):
    tok = t0.shape[0]
    stream = (
        r0[...] + r1[...].astype(F32) + r2[...].astype(F32) + r3[...].astype(F32)
    ).astype(BF16)
    out[...] = stream
    for s, part in enumerate((t0, t1, t2, t3)):
        part[...] = stream[s * tok : (s + 1) * tok]


def qkv_kernel(x0, x1, x2, x3, gain_ref, own_ref, par_ref, o0, o1, o2, o3, hold):
    e, m = seq_index(), mp_index()
    width = x0.shape[1]
    half = 2 * width
    tok = o0.shape[0]
    for j, part in enumerate((x0, x1, x2, x3)):
        k = m ^ j
        gain = gain_ref[:, pl.ds(chunk_offset(e, k, width), width)]
        hold[:, pl.ds(pl.multiple_of(k * width, width), width)] = (
            part[...].astype(F32) * gain
        ).astype(BF16)
    product = jnp.dot(hold[:, :half], own_ref[...], preferred_element_type=F32) + jnp.dot(
        hold[:, half:], par_ref[...], preferred_element_type=F32
    )
    for s, out in enumerate((o0, o1, o2, o3)):
        out[...] = product[s * tok : (s + 1) * tok].astype(out.dtype)


def pack_kernel(t0, t1, t2, t3, out_ref):
    width = t0.shape[1]
    for s, part in enumerate((t0, t1, t2, t3)):
        out_ref[:, s * width : (s + 1) * width] = part[...]


def finish_kernel(y0, y1, y2, y3, p0, p1, p2, p3, qkv_ref, stream_ref):
    e, m = seq_index(), mp_index()
    width = p0.shape[1] // 4
    squares = jnp.zeros((p0.shape[0], width), F32)
    for j, part in enumerate((p0, p1, p2, p3)):
        for s in range(4):
            block = part[:, s * width : (s + 1) * width]
            wide = block.astype(F32)
            squares = squares + wide * wide
            stream_ref[:, pl.ds(chunk_offset(e ^ (2 * s), m ^ j, width), width)] = block
    mean_square = jnp.sum(squares, axis=1, keepdims=True) / stream_ref.shape[1]
    total = y0[...] + y1[...].astype(F32) + y2[...].astype(F32) + y3[...].astype(F32)
    qkv_ref[...] = (total * lax.rsqrt(mean_square + 1e-06)).astype(BF16)


def call(kernel, out_shape, args, scratch=(), scalars=(), flops=0, moved=1 << 20):
    vmem, smem = pl.BlockSpec(memory_space=pltpu.VMEM), pl.BlockSpec(memory_space=pltpu.SMEM)
    return pl.pallas_call(
        kernel,
        out_shape=out_shape,
        in_specs=[smem if i in scalars else vmem for i in range(len(args))],
        out_specs=jax.tree.map(lambda _: vmem, out_shape),
        scratch_shapes=list(scratch),
        compiler_params=pltpu.CompilerParams(vmem_limit_bytes=24 << 20),
        cost_estimate=pl.CostEstimate(flops=flops, bytes_accessed=moved, transcendentals=0),
    )(*args)


def swap(value, axes, bits):
    count = lax.axis_size(axes)
    return lax.ppermute(value, axes, [(i, i ^ bits) for i in range(count)])


def on_block(
    fresh_queries,
    fresh_keys,
    fresh_values,
    cache,
    pool_root,
    branch_owner,
    branch_len,
    branch_root,
    request_branch,
    token_request,
    residual,
    wo_t,
    norm_gain,
    w_qkv,
):
    tok, wide = fresh_queries.shape
    width = wo_t.shape[0] // 2
    columns = w_qkv.shape[1]
    sds = jax.ShapeDtypeStruct
    seq, mp = ("z", "y"), ("x", "c")

    far = {s: swap(cache, seq, s) for s in (4, 6, 5, 7, 2, 3, 1)}
    blocks = [cache] + [far[s] for s in range(1, 8)]
    blocks, wo_later = lax.optimization_barrier((blocks, wo_t))
    wo_pair = swap(wo_later, "y", 1)
    attn, *sends = call(
        attend_kernel,
        [sds((tok, wide), BF16)] + [sds((tok, wide + width), BF16)] * 4,
        (
            fresh_queries, fresh_keys, fresh_values, token_request, request_branch, branch_root,
            pool_root, branch_owner, branch_len, residual, *blocks,
        ),
        scalars=(4, 5, 7, 8),
        flops=1 << 26,
    )
    own_send, wq_later = lax.optimization_barrier((sends[0], w_qkv))
    wq_pair = swap(wq_later, "y", 1)
    a2, a3, a1 = (swap(sends[s], "z", s) for s in (2, 3, 1))
    sums = call(
        project_kernel,
        [sds((4 * tok, width), F32)] + [sds((4 * tok, width), BF16)] * 3,
        (own_send, a1, a2, a3, wo_t, wo_pair),
        scratch=[pltpu.VMEM((4 * tok, 4 * width), F32)],
        flops=1 << 27,
    )
    sums = [sums[0]] + [swap(sums[j], mp, j) for j in range(1, 4)]
    made = call(
        combine_kernel,
        [sds((4 * tok, width), BF16)] + [sds((tok, width), BF16)] * 4,
        tuple(sums),
    )
    slices = [made[0]] + [swap(made[0], mp, j) for j in range(1, 4)]
    home = [made[1]] + [swap(made[1 + s], "z", s) for s in range(1, 4)]
    partial = call(
        qkv_kernel,
        [sds((tok, columns), F32)] + [sds((tok, columns), BF16)] * 3,
        (*slices, norm_gain[None, :], w_qkv, wq_pair),
        scratch=[pltpu.VMEM((4 * tok, 4 * width), BF16)],
        flops=1 << 28,
    )
    y1, y2, y3 = (swap(partial[s], "z", s) for s in (1, 2, 3))
    home, y1 = lax.optimization_barrier((home, y1))
    packed = call(pack_kernel, sds((tok, 4 * width), BF16), tuple(home))
    pieces = [packed] + [swap(packed, mp, j) for j in range(1, 4)]
    qkv_next, stream = call(
        finish_kernel,
        [sds((tok, columns), BF16), sds(residual.shape, BF16)],
        (partial[0], y1, y2, y3, *pieces),
    )
    return attn, stream, qkv_next


def absorb(running, query_rows, key_row_block, value_rows, visible, score_scale):
    peak_old, total, mixed = running
    scores = (
        jnp.einsum("tkgd,rkd->tkgr", query_rows, key_row_block, preferred_element_type=jnp.float32)
        * score_scale
    )
    seen = visible[:, None, None, :]
    peak_new = jnp.maximum(peak_old, jnp.max(jnp.where(seen, scores, -jnp.inf), axis=-1))
    factor = jnp.exp(peak_old - peak_new)
    weights_full = jnp.where(seen, jnp.exp(scores - peak_new[..., None]), 0.0)
    total = total * factor + jnp.sum(weights_full, axis=-1)
    mixed = mixed * factor[..., None] + jnp.einsum(
        "tkgr,rkd->tkgd",
        weights_full.astype(jnp.bfloat16),
        value_rows,
        preferred_element_type=jnp.float32,
    )
    return (peak_new, total, mixed)


def on_device(
    fresh_queries,
    fresh_keys,
    fresh_values,
    cache,
    pool_root,
    branch_owner,
    branch_len,
    branch_root,
    request_branch,
    token_request,
    residual,
    wo_t,
    norm_gain,
    w_qkv,
):
    seq_count = lax.axis_size("seq")
    root_count = seq_count // 4
    tok_rows = fresh_queries.shape[0]
    kv_local = fresh_keys.shape[1] // HEAD_SIZE
    query_groups = QUERY_HEADS // KEY_VALUE_HEADS
    score_scale = HEAD_SIZE ** (-0.5)
    slot_count = cache.shape[1] - pool_root.shape[1]
    owner_ids = jnp.arange(seq_count, dtype=jnp.int32)
    tags = cache_tags(pool_root, branch_owner, branch_len, root_count, slot_count, owner_ids)
    requests, token_branch, token_root = token_nodes(request_branch, token_request, branch_root)
    query_rows = fresh_queries.reshape(tok_rows, kv_local, query_groups, HEAD_SIZE)
    incoming_keys = fresh_keys.reshape(tok_rows, kv_local, HEAD_SIZE)
    incoming_values = fresh_values.reshape(tok_rows, kv_local, HEAD_SIZE)
    positions = jnp.arange(tok_rows, dtype=jnp.int32)
    own_visible = (requests[None, :] == requests[:, None]) & (
        positions[None, :] <= positions[:, None]
    )
    start_state = (
        jnp.full((tok_rows, kv_local, query_groups), -jnp.inf, jnp.float32),
        jnp.zeros((tok_rows, kv_local, query_groups), jnp.float32),
        jnp.zeros((tok_rows, kv_local, query_groups, HEAD_SIZE), jnp.float32),
    )
    state = absorb(
        start_state, query_rows, incoming_keys, incoming_values, own_visible, score_scale
    )
    piece = lax.all_gather(cache, "seq", axis=1, tiled=True)
    rows = piece.shape[1]
    block = 512 if rows > 512 and rows % 512 == 0 else rows
    key_blocks = piece[0].reshape(rows // block, block, kv_local, HEAD_SIZE)
    value_blocks = piece[1].reshape(rows // block, block, kv_local, HEAD_SIZE)
    tag_blocks = tags.reshape(rows // block, block)

    def one_block(running, parts):
        key_row_block, value_rows, tag_rows = parts
        visible = (tag_rows[None, :] == token_root[:, None]) | (
            tag_rows[None, :] == root_count + token_branch[:, None]
        )
        updated = absorb(running, query_rows, key_row_block, value_rows, visible, score_scale)
        return (updated, None)

    state, unused = lax.scan(one_block, state, (key_blocks, value_blocks, tag_blocks))
    peak_final, total_final, mixed_final = state
    attn = (
        (mixed_final / total_final[..., None])
        .reshape(tok_rows, kv_local * query_groups * HEAD_SIZE)
        .astype(jnp.bfloat16)
    )
    partial_value = lax.dot_general(
        attn,
        lax.all_gather(wo_t, "seq", axis=0, tiled=True),
        (((1,), (1,)), ((), ())),
        preferred_element_type=jnp.float32,
    )
    summed = lax.psum(partial_value.astype(jnp.bfloat16), "mp").astype(jnp.float32)
    stream = (residual.astype(jnp.float32) + summed).astype(jnp.bfloat16)
    widened = stream.astype(jnp.float32)
    mean_square = jnp.mean(widened * widened, axis=-1, keepdims=True)
    normed = (widened * lax.rsqrt(mean_square + 1e-06) * norm_gain[None, :]).astype(jnp.bfloat16)
    qkv_sum = jnp.dot(
        normed, lax.all_gather(w_qkv, "seq", axis=0, tiled=True), preferred_element_type=jnp.float32
    )
    return (attn, stream, qkv_sum.astype(jnp.bfloat16))


def solution(mesh):
    small = mesh.shape["seq"] == 8 and mesh.shape["mp"] == 4
    seq, mp = "seq", "mp"
    if small:
        mesh = Mesh(mesh.devices.reshape(4, 2, 2, 2), ("z", "y", "x", "c"))
        seq, mp = ("z", "y"), ("x", "c")
    return jax.shard_map(
        on_block if small else on_device,
        mesh=mesh,
        in_specs=(
            P(seq, mp),
            P(seq, mp),
            P(seq, mp),
            P(None, seq, mp),
            P(),
            P(),
            P(),
            P(),
            P(seq, None),
            P(seq, None),
            P(seq, None),
            P(seq, mp),
            P(),
            P(seq, mp),
        ),
        out_specs=(P(seq, mp), P(seq, None), P(seq, mp)),
        check_vma=False,
    )
```

```python
import jax
import jax.numpy as jnp
from jax import lax
from jax.experimental import pallas as pl
from jax.experimental.pallas import tpu as pltpu
from jax.sharding import Mesh
from jax.sharding import PartitionSpec as P

QUERY_HEADS = 16
KEY_VALUE_HEADS = 8
HEAD_SIZE = 128
NT = (((1,), (1,)), ((), ()))
TN = (((0,), (0,)), ((), ()))
F32 = jnp.float32
HIDDEN = -1e30
BF16 = jnp.bfloat16


def cache_tags(pool_root, branch_owner, branch_len, root_count, slot_count, owner_ids):
    branch_count = branch_owner.shape[0]
    branch_ids = jnp.arange(branch_count, dtype=jnp.int32)
    owned = jnp.sum(
        jnp.where(branch_owner[None, :] == owner_ids[:, None], branch_ids[None, :], 0), axis=1
    )
    owned_length = jnp.sum(
        jnp.where(branch_ids[None, :] == owned[:, None], branch_len[None, :], 0), axis=1
    )
    slot_ids = jnp.arange(slot_count, dtype=jnp.int32)
    branch_tags = jnp.where(
        slot_ids[None, :] < owned_length[:, None], root_count + owned[:, None], -1
    )
    return jnp.concatenate([pool_root, branch_tags], axis=1).reshape(-1)


def token_nodes(request_branch, token_request, branch_root):
    requests = token_request[0]
    local_branches = request_branch[0]
    request_ids = jnp.arange(local_branches.shape[0], dtype=jnp.int32)
    token_branch = jnp.sum(
        jnp.where(requests[:, None] == request_ids[None, :], local_branches[None, :], 0), axis=1
    )
    branch_ids = jnp.arange(branch_root.shape[0], dtype=jnp.int32)
    token_root = jnp.sum(
        jnp.where(token_branch[:, None] == branch_ids[None, :], branch_root[None, :], 0), axis=1
    )
    return requests, token_branch, token_root


def head_lanes(h):
    return slice(h * HEAD_SIZE, (h + 1) * HEAD_SIZE)


def seq_index():
    return 2 * lax.axis_index("z") + lax.axis_index("y")


def chunk_offset(e, k, width):
    return pl.multiple_of((e ^ (k // 2)) * (2 * width) + (k % 2) * width, width)


def mp_index():
    return 2 * lax.axis_index("x") + lax.axis_index("c")


def attend_kernel(q_ref, kf_ref, vf_ref, res_ref, bias_ref, *refs):
    caches, out_ref, sends = refs[:-5], refs[-5], refs[-4:]
    e, m = seq_index(), mp_index()
    tok, wide = q_ref.shape
    bias = bias_ref[...]
    for k in range(kf_ref.shape[1] // HEAD_SIZE):
        lanes, first, second = head_lanes(k), head_lanes(2 * k), head_lanes(2 * k + 1)
        keys = jnp.concatenate([kf_ref[:, lanes]] + [c[0, :, lanes] for c in caches], axis=0)
        values = jnp.concatenate([vf_ref[:, lanes]] + [c[1, :, lanes] for c in caches], axis=0)
        queries = jnp.concatenate([q_ref[:, first], q_ref[:, second]], axis=0)
        scores = (
            lax.dot_general(keys, queries, NT, preferred_element_type=F32) * HEAD_SIZE**-0.5 + bias
        )
        peak = jnp.max(scores, axis=0, keepdims=True)
        prob = jnp.exp(scores - peak)
        total = jnp.sum(prob, axis=0, keepdims=True)
        mixed = lax.dot_general(values, prob.astype(BF16), TN, preferred_element_type=F32)
        attn = (mixed / total).T.astype(BF16)
        for ref in (out_ref, *sends):
            ref[:, first] = attn[:tok]
            ref[:, second] = attn[tok:]
    width = sends[0].shape[1] - wide
    for s, ref in enumerate(sends):
        ref[:, wide:] = res_ref[:, pl.ds(chunk_offset(e ^ (2 * s), m, width), width)]


def project_kernel(a0, a1, a2, a3, own_ref, par_ref, o0, o1, o2, o3, hold):
    m = mp_index()
    half, wide = own_ref.shape
    blocks = (a0, a1, a2, a3)
    attn = jnp.concatenate([a[:, :wide] for a in blocks], axis=0)
    rest = jnp.concatenate([a[:, wide:] for a in blocks], axis=0)
    hold[:, :half] = lax.dot_general(attn, own_ref[...], NT, preferred_element_type=F32)
    hold[:, half:] = lax.dot_general(attn, par_ref[...], NT, preferred_element_type=F32)
    width = o0.shape[1]
    for j, out in enumerate((o0, o1, o2, o3)):
        chunk = hold[:, pl.ds(pl.multiple_of((m ^ j) * width, width), width)]
        out[...] = chunk + rest.astype(F32) if j == 0 else chunk.astype(BF16)


def combine_kernel(r0, r1, r2, r3, out, t0, t1, t2, t3):
    tok = t0.shape[0]
    stream = (
        r0[...] + r1[...].astype(F32) + r2[...].astype(F32) + r3[...].astype(F32)
    ).astype(BF16)
    out[...] = stream
    for s, part in enumerate((t0, t1, t2, t3)):
        part[...] = stream[s * tok : (s + 1) * tok]


def qkv_kernel(x0, x1, x2, x3, gain_ref, own_ref, par_ref, t0, t1, t2, t3, o0, o1, o2, o3, packed_ref, hold):
    e, m = seq_index(), mp_index()
    width = x0.shape[1]
    half = 2 * width
    tok = o0.shape[0]
    for j, part in enumerate((x0, x1, x2, x3)):
        k = m ^ j
        gain = gain_ref[:, pl.ds(chunk_offset(e, k, width), width)]
        hold[:, pl.ds(pl.multiple_of(k * width, width), width)] = (
            part[...].astype(F32) * gain
        ).astype(BF16)
    product = jnp.dot(hold[:, :half], own_ref[...], preferred_element_type=F32) + jnp.dot(
        hold[:, half:], par_ref[...], preferred_element_type=F32
    )
    for s, part in enumerate((t0, t1, t2, t3)):
        packed_ref[:, s * width : (s + 1) * width] = part[...]
    for s, out in enumerate((o0, o1, o2, o3)):
        out[...] = product[s * tok : (s + 1) * tok].astype(out.dtype)


def finish_kernel(y0, y1, y2, y3, p0, p1, p2, p3, qkv_ref, stream_ref):
    e, m = seq_index(), mp_index()
    width = p0.shape[1] // 4
    squares = jnp.zeros((p0.shape[0], width), F32)
    for j, part in enumerate((p0, p1, p2, p3)):
        for s in range(4):
            block = part[:, s * width : (s + 1) * width]
            wide = block.astype(F32)
            squares = squares + wide * wide
            stream_ref[:, pl.ds(chunk_offset(e ^ (2 * s), m ^ j, width), width)] = block
    mean_square = jnp.sum(squares, axis=1, keepdims=True) / stream_ref.shape[1]
    total = y0[...] + y1[...].astype(F32) + y2[...].astype(F32) + y3[...].astype(F32)
    qkv_ref[...] = (total * lax.rsqrt(mean_square + 1e-06)).astype(BF16)


def call(kernel, out_shape, args, scratch=(), flops=0, moved=1 << 20):
    vmem = pl.BlockSpec(memory_space=pltpu.VMEM)
    return pl.pallas_call(
        kernel,
        out_shape=out_shape,
        in_specs=[vmem] * len(args),
        out_specs=jax.tree.map(lambda _: vmem, out_shape),
        scratch_shapes=list(scratch),
        compiler_params=pltpu.CompilerParams(vmem_limit_bytes=24 << 20),
        cost_estimate=pl.CostEstimate(flops=flops, bytes_accessed=moved, transcendentals=0),
    )(*args)


def swap(value, axes, bits):
    count = lax.axis_size(axes)
    return lax.ppermute(value, axes, [(i, i ^ bits) for i in range(count)])


def on_block(
    fresh_queries,
    fresh_keys,
    fresh_values,
    cache,
    pool_root,
    branch_owner,
    branch_len,
    branch_root,
    request_branch,
    token_request,
    residual,
    wo_t,
    norm_gain,
    w_qkv,
):
    tok, wide = fresh_queries.shape
    width = wo_t.shape[0] // 2
    columns = w_qkv.shape[1]
    sds = jax.ShapeDtypeStruct
    seq, mp = ("z", "y"), ("x", "c")

    far = {s: swap(cache, seq, s) for s in (4, 6, 5, 7, 2, 3, 1)}
    blocks = [cache] + [far[s] for s in range(1, 8)]
    wo_pair = swap(wo_t, "y", 1)

    holders = pool_root.shape[0]
    root_count = holders // 4
    rows = jnp.arange(holders, dtype=jnp.int32)
    relative = seq_index() ^ rows
    pool_relative = jnp.sum(
        jnp.where(relative[:, None, None] == rows[None, :, None], pool_root[None], 0), axis=1
    )
    slot_count = cache.shape[1] - pool_root.shape[1]
    tags = cache_tags(pool_relative, branch_owner, branch_len, root_count, slot_count, relative)
    requests, token_branch, token_root = token_nodes(request_branch, token_request, branch_root)
    positions = jnp.arange(tok, dtype=jnp.int32)
    own_seen = (requests[None, :] == requests[:, None]) & (
        positions[:, None] <= positions[None, :]
    )
    pool_seen = (tags[:, None] == token_root[None, :]) | (
        tags[:, None] == root_count + token_branch[None, :]
    )
    seen = jnp.concatenate([own_seen, pool_seen], axis=0)
    bias = jnp.where(jnp.concatenate([seen, seen], axis=1), 0.0, HIDDEN).astype(F32)

    blocks, wo_pair = lax.optimization_barrier((blocks, wo_pair))
    attn, *sends = call(
        attend_kernel,
        [sds((tok, wide), BF16)] + [sds((tok, wide + width), BF16)] * 4,
        (fresh_queries, fresh_keys, fresh_values, residual, bias, *blocks),
        flops=1 << 26,
    )
    own_send, wq_later = lax.optimization_barrier((sends[0], w_qkv))
    wq_pair = swap(wq_later, "y", 1)
    a2, a3, a1 = (swap(sends[s], "z", s) for s in (2, 3, 1))
    sums = call(
        project_kernel,
        [sds((4 * tok, width), F32)] + [sds((4 * tok, width), BF16)] * 3,
        (own_send, a1, a2, a3, wo_t, wo_pair),
        scratch=[pltpu.VMEM((4 * tok, 4 * width), F32)],
        flops=1 << 27,
    )
    sums = [sums[0]] + [swap(sums[j], mp, j) for j in range(1, 4)]
    made = call(
        combine_kernel,
        [sds((4 * tok, width), BF16)] + [sds((tok, width), BF16)] * 4,
        tuple(sums),
    )
    made, wq_pair = lax.optimization_barrier((made, wq_pair))
    slices = [made[0]] + [swap(made[0], mp, j) for j in range(1, 4)]
    home = [made[1]] + [swap(made[1 + s], "z", s) for s in range(1, 4)]
    *partial, packed = call(
        qkv_kernel,
        [sds((tok, columns), F32)]
        + [sds((tok, columns), BF16)] * 3
        + [sds((tok, 4 * width), BF16)],
        (*slices, norm_gain[None, :], w_qkv, wq_pair, *home),
        scratch=[pltpu.VMEM((4 * tok, 4 * width), BF16)],
        flops=1 << 28,
    )
    y1, y2, y3 = (swap(partial[s], "z", s) for s in (1, 2, 3))
    packed, y1 = lax.optimization_barrier((packed, y1))
    pieces = [packed] + [swap(packed, mp, j) for j in range(1, 4)]
    qkv_next, stream = call(
        finish_kernel,
        [sds((tok, columns), BF16), sds(residual.shape, BF16)],
        (partial[0], y1, y2, y3, *pieces),
    )
    return attn, stream, qkv_next


def absorb(running, query_rows, key_row_block, value_rows, visible, score_scale):
    peak_old, total, mixed = running
    scores = (
        jnp.einsum("tkgd,rkd->tkgr", query_rows, key_row_block, preferred_element_type=jnp.float32)
        * score_scale
    )
    seen = visible[:, None, None, :]
    peak_new = jnp.maximum(peak_old, jnp.max(jnp.where(seen, scores, -jnp.inf), axis=-1))
    factor = jnp.exp(peak_old - peak_new)
    weights_full = jnp.where(seen, jnp.exp(scores - peak_new[..., None]), 0.0)
    total = total * factor + jnp.sum(weights_full, axis=-1)
    mixed = mixed * factor[..., None] + jnp.einsum(
        "tkgr,rkd->tkgd",
        weights_full.astype(jnp.bfloat16),
        value_rows,
        preferred_element_type=jnp.float32,
    )
    return (peak_new, total, mixed)


def on_device(
    fresh_queries,
    fresh_keys,
    fresh_values,
    cache,
    pool_root,
    branch_owner,
    branch_len,
    branch_root,
    request_branch,
    token_request,
    residual,
    wo_t,
    norm_gain,
    w_qkv,
):
    seq_count = lax.axis_size("seq")
    root_count = seq_count // 4
    tok_rows = fresh_queries.shape[0]
    kv_local = fresh_keys.shape[1] // HEAD_SIZE
    query_groups = QUERY_HEADS // KEY_VALUE_HEADS
    score_scale = HEAD_SIZE ** (-0.5)
    slot_count = cache.shape[1] - pool_root.shape[1]
    owner_ids = jnp.arange(seq_count, dtype=jnp.int32)
    tags = cache_tags(pool_root, branch_owner, branch_len, root_count, slot_count, owner_ids)
    requests, token_branch, token_root = token_nodes(request_branch, token_request, branch_root)
    query_rows = fresh_queries.reshape(tok_rows, kv_local, query_groups, HEAD_SIZE)
    incoming_keys = fresh_keys.reshape(tok_rows, kv_local, HEAD_SIZE)
    incoming_values = fresh_values.reshape(tok_rows, kv_local, HEAD_SIZE)
    positions = jnp.arange(tok_rows, dtype=jnp.int32)
    own_visible = (requests[None, :] == requests[:, None]) & (
        positions[None, :] <= positions[:, None]
    )
    start_state = (
        jnp.full((tok_rows, kv_local, query_groups), -jnp.inf, jnp.float32),
        jnp.zeros((tok_rows, kv_local, query_groups), jnp.float32),
        jnp.zeros((tok_rows, kv_local, query_groups, HEAD_SIZE), jnp.float32),
    )
    state = absorb(
        start_state, query_rows, incoming_keys, incoming_values, own_visible, score_scale
    )
    piece = lax.all_gather(cache, "seq", axis=1, tiled=True)
    rows = piece.shape[1]
    block = 512 if rows > 512 and rows % 512 == 0 else rows
    key_blocks = piece[0].reshape(rows // block, block, kv_local, HEAD_SIZE)
    value_blocks = piece[1].reshape(rows // block, block, kv_local, HEAD_SIZE)
    tag_blocks = tags.reshape(rows // block, block)

    def one_block(running, parts):
        key_row_block, value_rows, tag_rows = parts
        visible = (tag_rows[None, :] == token_root[:, None]) | (
            tag_rows[None, :] == root_count + token_branch[:, None]
        )
        updated = absorb(running, query_rows, key_row_block, value_rows, visible, score_scale)
        return (updated, None)

    state, unused = lax.scan(one_block, state, (key_blocks, value_blocks, tag_blocks))
    peak_final, total_final, mixed_final = state
    attn = (
        (mixed_final / total_final[..., None])
        .reshape(tok_rows, kv_local * query_groups * HEAD_SIZE)
        .astype(jnp.bfloat16)
    )
    partial_value = lax.dot_general(
        attn,
        lax.all_gather(wo_t, "seq", axis=0, tiled=True),
        (((1,), (1,)), ((), ())),
        preferred_element_type=jnp.float32,
    )
    summed = lax.psum(partial_value.astype(jnp.bfloat16), "mp").astype(jnp.float32)
    stream = (residual.astype(jnp.float32) + summed).astype(jnp.bfloat16)
    widened = stream.astype(jnp.float32)
    mean_square = jnp.mean(widened * widened, axis=-1, keepdims=True)
    normed = (widened * lax.rsqrt(mean_square + 1e-06) * norm_gain[None, :]).astype(jnp.bfloat16)
    qkv_sum = jnp.dot(
        normed, lax.all_gather(w_qkv, "seq", axis=0, tiled=True), preferred_element_type=jnp.float32
    )
    return (attn, stream, qkv_sum.astype(jnp.bfloat16))


def solution(mesh):
    small = mesh.shape["seq"] == 8 and mesh.shape["mp"] == 4
    seq, mp = "seq", "mp"
    if small:
        mesh = Mesh(mesh.devices.reshape(4, 2, 2, 2), ("z", "y", "x", "c"))
        seq, mp = ("z", "y"), ("x", "c")
    return jax.shard_map(
        on_block if small else on_device,
        mesh=mesh,
        in_specs=(
            P(seq, mp),
            P(seq, mp),
            P(seq, mp),
            P(None, seq, mp),
            P(),
            P(),
            P(),
            P(),
            P(seq, None),
            P(seq, None),
            P(seq, None),
            P(seq, mp),
            P(),
            P(seq, mp),
        ),
        out_specs=(P(seq, mp), P(seq, None), P(seq, mp)),
        check_vma=False,
    )
```

```python
import jax
import jax.numpy as jnp
from jax import lax
from jax.experimental import pallas as pl
from jax.experimental.pallas import tpu as pltpu
from jax.sharding import Mesh
from jax.sharding import PartitionSpec as P

QUERY_HEADS = 16
KEY_VALUE_HEADS = 8
HEAD_SIZE = 128
NT = (((1,), (1,)), ((), ()))
TN = (((0,), (0,)), ((), ()))
F32 = jnp.float32
HIDDEN = -1e30
BF16 = jnp.bfloat16


def cache_tags(pool_root, branch_owner, branch_len, root_count, slot_count, owner_ids):
    branch_count = branch_owner.shape[0]
    branch_ids = jnp.arange(branch_count, dtype=jnp.int32)
    owned = jnp.sum(
        jnp.where(branch_owner[None, :] == owner_ids[:, None], branch_ids[None, :], 0), axis=1
    )
    owned_length = jnp.sum(
        jnp.where(branch_ids[None, :] == owned[:, None], branch_len[None, :], 0), axis=1
    )
    slot_ids = jnp.arange(slot_count, dtype=jnp.int32)
    branch_tags = jnp.where(
        slot_ids[None, :] < owned_length[:, None], root_count + owned[:, None], -1
    )
    return jnp.concatenate([pool_root, branch_tags], axis=1).reshape(-1)


def token_branches(request_branch, token_request):
    requests = token_request[0]
    local_branches = request_branch[0]
    request_ids = jnp.arange(local_branches.shape[0], dtype=jnp.int32)
    token_branch = jnp.sum(
        jnp.where(requests[:, None] == request_ids[None, :], local_branches[None, :], 0), axis=1
    )
    return requests, token_branch


def head_lanes(h):
    return slice(h * HEAD_SIZE, (h + 1) * HEAD_SIZE)


def seq_index():
    return 2 * lax.axis_index("z") + lax.axis_index("y")


def chunk_offset(e, k, width):
    return pl.multiple_of((e ^ (k // 2)) * (2 * width) + (k % 2) * width, width)


def mp_index():
    return 2 * lax.axis_index("x") + lax.axis_index("c")


def attend_kernel(local_ref, res_ref, bias_ref, *refs):
    caches, out_ref, sends = refs[:-5], refs[-5], refs[-4:]
    e, m = seq_index(), mp_index()
    tok, wide = out_ref.shape
    kv = caches[0].shape[2]
    q_ref, kf_ref, vf_ref = (
        local_ref.at[:, :wide],
        local_ref.at[:, wide : wide + kv],
        local_ref.at[:, wide + kv :],
    )
    rows = caches[0].shape[1]
    bias = jnp.concatenate(
        [bias_ref[:tok]]
        + [
            bias_ref[pl.ds(pl.multiple_of(tok + (e ^ s) * rows, rows), rows), :]
            for s in range(len(caches))
        ],
        axis=0,
    )
    for k in range(kf_ref.shape[1] // HEAD_SIZE):
        lanes, first, second = head_lanes(k), head_lanes(2 * k), head_lanes(2 * k + 1)
        keys = jnp.concatenate([kf_ref[:, lanes]] + [c[0, :, lanes] for c in caches], axis=0)
        values = jnp.concatenate([vf_ref[:, lanes]] + [c[1, :, lanes] for c in caches], axis=0)
        queries = jnp.concatenate([q_ref[:, first], q_ref[:, second]], axis=0)
        scores = (
            lax.dot_general(keys, queries, NT, preferred_element_type=F32) * HEAD_SIZE**-0.5 + bias
        )
        peak = jnp.max(scores, axis=0, keepdims=True)
        prob = jnp.exp(scores - peak)
        total = jnp.sum(prob, axis=0, keepdims=True)
        mixed = lax.dot_general(values, prob.astype(BF16), TN, preferred_element_type=F32)
        attn = (mixed / total).T.astype(BF16)
        for ref in (out_ref, *sends):
            ref[:, first] = attn[:tok]
            ref[:, second] = attn[tok:]
    width = sends[0].shape[1] - wide
    for s, ref in enumerate(sends):
        ref[:, wide:] = res_ref[:, pl.ds(chunk_offset(e ^ (2 * s), m, width), width)]


def project_kernel(a0, a1, a2, a3, own_ref, par_ref, o0, o1, o2, o3, hold):
    m = mp_index()
    half, wide = own_ref.shape
    blocks = (a0, a1, a2, a3)
    attn = jnp.concatenate([a[:, :wide] for a in blocks], axis=0)
    rest = jnp.concatenate([a[:, wide:] for a in blocks], axis=0)
    hold[:, :half] = lax.dot_general(attn, own_ref[...], NT, preferred_element_type=F32)
    hold[:, half:] = lax.dot_general(attn, par_ref[...], NT, preferred_element_type=F32)
    width = o0.shape[1]
    for j, out in enumerate((o0, o1, o2, o3)):
        chunk = hold[:, pl.ds(pl.multiple_of((m ^ j) * width, width), width)]
        out[...] = chunk + rest.astype(F32) if j == 0 else chunk.astype(BF16)


def combine_kernel(r0, r1, r2, r3, out, t0, t1, t2, t3):
    tok = t0.shape[0]
    stream = (
        r0[...] + r1[...].astype(F32) + r2[...].astype(F32) + r3[...].astype(F32)
    ).astype(BF16)
    out[...] = stream
    for s, part in enumerate((t0, t1, t2, t3)):
        part[...] = stream[s * tok : (s + 1) * tok]


def qkv_kernel(x0, x1, x2, x3, gain_ref, own_ref, par_ref, o0, o1, o2, o3, hold):
    e, m = seq_index(), mp_index()
    width = x0.shape[1]
    half = 2 * width
    tok = o0.shape[0]
    for j, part in enumerate((x0, x1, x2, x3)):
        k = m ^ j
        gain = gain_ref[:, pl.ds(chunk_offset(e, k, width), width)]
        hold[:, pl.ds(pl.multiple_of(k * width, width), width)] = (
            part[...].astype(F32) * gain
        ).astype(BF16)
    product = jnp.dot(hold[:, :half], own_ref[...], preferred_element_type=F32) + jnp.dot(
        hold[:, half:], par_ref[...], preferred_element_type=F32
    )
    for s, out in enumerate((o0, o1, o2, o3)):
        out[...] = product[s * tok : (s + 1) * tok].astype(out.dtype)


def pack_kernel(t0, t1, t2, t3, out_ref):
    width = t0.shape[1]
    for s, part in enumerate((t0, t1, t2, t3)):
        out_ref[:, s * width : (s + 1) * width] = part[...]


def finish_kernel(y0, y1, y2, y3, p0, p1, p2, p3, qkv_ref, stream_ref):
    e, m = seq_index(), mp_index()
    width = p0.shape[1] // 4
    squares = jnp.zeros((p0.shape[0], width), F32)
    for j, part in enumerate((p0, p1, p2, p3)):
        for s in range(4):
            block = part[:, s * width : (s + 1) * width]
            wide = block.astype(F32)
            squares = squares + wide * wide
            stream_ref[:, pl.ds(chunk_offset(e ^ (2 * s), m ^ j, width), width)] = block
    mean_square = jnp.sum(squares, axis=1, keepdims=True) / stream_ref.shape[1]
    total = y0[...] + y1[...].astype(F32) + y2[...].astype(F32) + y3[...].astype(F32)
    qkv_ref[...] = (total * lax.rsqrt(mean_square + 1e-06)).astype(BF16)


def call(kernel, out_shape, args, scratch=(), flops=0, moved=1 << 20):
    vmem = pl.BlockSpec(memory_space=pltpu.VMEM)
    return pl.pallas_call(
        kernel,
        out_shape=out_shape,
        in_specs=[vmem] * len(args),
        out_specs=jax.tree.map(lambda _: vmem, out_shape),
        scratch_shapes=list(scratch),
        compiler_params=pltpu.CompilerParams(vmem_limit_bytes=24 << 20),
        cost_estimate=pl.CostEstimate(flops=flops, bytes_accessed=moved, transcendentals=0),
    )(*args)


def swap(value, axes, bits):
    count = lax.axis_size(axes)
    return lax.ppermute(value, axes, [(i, i ^ bits) for i in range(count)])


def on_block(
    fresh_queries,
    fresh_keys,
    fresh_values,
    cache,
    pool_root,
    branch_owner,
    branch_len,
    branch_root,
    request_branch,
    token_request,
    residual,
    wo_t,
    norm_gain,
    w_qkv,
):
    tok, wide = fresh_queries.shape
    width = wo_t.shape[0] // 2
    columns = w_qkv.shape[1]
    sds = jax.ShapeDtypeStruct
    mp = ("x", "c")

    along = [cache] + [swap(cache, "z", s) for s in range(1, 4)]
    beside = swap(cache, "y", 1)

    holders = pool_root.shape[0]
    requests, token_branch = token_branches(request_branch, token_request)
    branch_ids = jnp.arange(branch_root.shape[0], dtype=jnp.int32)
    chosen = token_branch[:, None] == branch_ids[None, :]
    token_root, token_owner, token_length = (
        jnp.sum(jnp.where(chosen, per_branch[None, :], 0), axis=1)
        for per_branch in (branch_root, branch_owner, branch_len)
    )
    positions = jnp.arange(tok, dtype=jnp.int32)
    own_seen = (requests[None, :] == requests[:, None]) & (
        positions[:, None] <= positions[None, :]
    )
    slot_count = cache.shape[1] - pool_root.shape[1]
    slots = jnp.arange(slot_count, dtype=jnp.int32)
    at = jnp.arange(holders, dtype=jnp.int32)
    root_seen = pool_root[:, :, None] == token_root[None, None, :]
    branch_seen = (token_owner[None, None, :] == at[:, None, None]) & (
        slots[None, :, None] < token_length[None, None, :]
    )
    pool_seen = jnp.concatenate([root_seen, branch_seen], axis=1).reshape(-1, tok)
    seen = jnp.concatenate([own_seen, pool_seen], axis=0)
    bias = jnp.where(jnp.concatenate([seen, seen], axis=1), 0.0, HIDDEN).astype(F32)

    local = jnp.concatenate([fresh_queries, fresh_keys, fresh_values], axis=1)
    along[1:], bias, local = lax.optimization_barrier((along[1:], bias, local))
    across = [beside] + [swap(mine, "y", 1) for mine in along[1:]]
    blocks = [block for pair in zip(along, across) for block in pair]
    blocks, wo_later = lax.optimization_barrier((blocks, wo_t))
    wo_pair = swap(wo_later, "y", 1)
    attn, *sends = call(
        attend_kernel,
        [sds((tok, wide), BF16)] + [sds((tok, wide + width), BF16)] * 4,
        (local, residual, bias, *blocks),
        flops=1 << 26,
    )
    a2, a3, a1 = (swap(sends[s], "z", s) for s in (2, 3, 1))
    sums = call(
        project_kernel,
        [sds((4 * tok, width), F32)] + [sds((4 * tok, width), BF16)] * 3,
        (sends[0], a1, a2, a3, wo_t, wo_pair),
        scratch=[pltpu.VMEM((4 * tok, 4 * width), F32)],
        flops=1 << 27,
    )
    own_sum, wq_later = lax.optimization_barrier((sums[0], w_qkv))
    wq_pair = swap(wq_later, "y", 1)
    sums = [own_sum] + [swap(sums[j], mp, j) for j in range(1, 4)]
    made = call(
        combine_kernel,
        [sds((4 * tok, width), BF16)] + [sds((tok, width), BF16)] * 4,
        tuple(sums),
    )
    slices = [made[0]] + [swap(made[0], mp, j) for j in range(1, 4)]
    home = [made[1]] + [swap(made[1 + s], "z", s) for s in range(1, 4)]
    partial = call(
        qkv_kernel,
        [sds((tok, columns), F32)] + [sds((tok, columns), BF16)] * 3,
        (*slices, norm_gain[None, :], w_qkv, wq_pair),
        scratch=[pltpu.VMEM((4 * tok, 4 * width), BF16)],
        flops=1 << 28,
    )
    y1, y2, y3 = (swap(partial[s], "z", s) for s in (1, 2, 3))
    home, own_partial = lax.optimization_barrier((home, partial[0]))
    packed = call(pack_kernel, sds((tok, 4 * width), BF16), tuple(home))
    pieces = [packed] + [swap(packed, mp, j) for j in range(1, 4)]
    qkv_next, stream = call(
        finish_kernel,
        [sds((tok, columns), BF16), sds(residual.shape, BF16)],
        (own_partial, y1, y2, y3, *pieces),
    )
    return attn, stream, qkv_next


def absorb(running, query_rows, key_row_block, value_rows, visible, score_scale):
    peak_old, total, mixed = running
    scores = (
        jnp.einsum("tkgd,rkd->tkgr", query_rows, key_row_block, preferred_element_type=jnp.float32)
        * score_scale
    )
    seen = visible[:, None, None, :]
    peak_new = jnp.maximum(peak_old, jnp.max(jnp.where(seen, scores, -jnp.inf), axis=-1))
    factor = jnp.exp(peak_old - peak_new)
    weights_full = jnp.where(seen, jnp.exp(scores - peak_new[..., None]), 0.0)
    total = total * factor + jnp.sum(weights_full, axis=-1)
    mixed = mixed * factor[..., None] + jnp.einsum(
        "tkgr,rkd->tkgd",
        weights_full.astype(jnp.bfloat16),
        value_rows,
        preferred_element_type=jnp.float32,
    )
    return (peak_new, total, mixed)


def on_device(
    fresh_queries,
    fresh_keys,
    fresh_values,
    cache,
    pool_root,
    branch_owner,
    branch_len,
    branch_root,
    request_branch,
    token_request,
    residual,
    wo_t,
    norm_gain,
    w_qkv,
):
    seq_count = lax.axis_size("seq")
    root_count = seq_count // 4
    tok_rows = fresh_queries.shape[0]
    kv_local = fresh_keys.shape[1] // HEAD_SIZE
    query_groups = QUERY_HEADS // KEY_VALUE_HEADS
    score_scale = HEAD_SIZE ** (-0.5)
    slot_count = cache.shape[1] - pool_root.shape[1]
    owner_ids = jnp.arange(seq_count, dtype=jnp.int32)
    tags = cache_tags(pool_root, branch_owner, branch_len, root_count, slot_count, owner_ids)
    requests, token_branch = token_branches(request_branch, token_request)
    branch_ids = jnp.arange(branch_root.shape[0], dtype=jnp.int32)
    token_root = jnp.sum(
        jnp.where(token_branch[:, None] == branch_ids[None, :], branch_root[None, :], 0), axis=1
    )
    query_rows = fresh_queries.reshape(tok_rows, kv_local, query_groups, HEAD_SIZE)
    incoming_keys = fresh_keys.reshape(tok_rows, kv_local, HEAD_SIZE)
    incoming_values = fresh_values.reshape(tok_rows, kv_local, HEAD_SIZE)
    positions = jnp.arange(tok_rows, dtype=jnp.int32)
    own_visible = (requests[None, :] == requests[:, None]) & (
        positions[None, :] <= positions[:, None]
    )
    start_state = (
        jnp.full((tok_rows, kv_local, query_groups), -jnp.inf, jnp.float32),
        jnp.zeros((tok_rows, kv_local, query_groups), jnp.float32),
        jnp.zeros((tok_rows, kv_local, query_groups, HEAD_SIZE), jnp.float32),
    )
    state = absorb(
        start_state, query_rows, incoming_keys, incoming_values, own_visible, score_scale
    )
    piece = lax.all_gather(cache, "seq", axis=1, tiled=True)
    rows = piece.shape[1]
    block = 512 if rows > 512 and rows % 512 == 0 else rows
    key_blocks = piece[0].reshape(rows // block, block, kv_local, HEAD_SIZE)
    value_blocks = piece[1].reshape(rows // block, block, kv_local, HEAD_SIZE)
    tag_blocks = tags.reshape(rows // block, block)

    def one_block(running, parts):
        key_row_block, value_rows, tag_rows = parts
        visible = (tag_rows[None, :] == token_root[:, None]) | (
            tag_rows[None, :] == root_count + token_branch[:, None]
        )
        updated = absorb(running, query_rows, key_row_block, value_rows, visible, score_scale)
        return (updated, None)

    state, unused = lax.scan(one_block, state, (key_blocks, value_blocks, tag_blocks))
    peak_final, total_final, mixed_final = state
    attn = (
        (mixed_final / total_final[..., None])
        .reshape(tok_rows, kv_local * query_groups * HEAD_SIZE)
        .astype(jnp.bfloat16)
    )
    partial_value = lax.dot_general(
        attn,
        lax.all_gather(wo_t, "seq", axis=0, tiled=True),
        (((1,), (1,)), ((), ())),
        preferred_element_type=jnp.float32,
    )
    summed = lax.psum(partial_value.astype(jnp.bfloat16), "mp").astype(jnp.float32)
    stream = (residual.astype(jnp.float32) + summed).astype(jnp.bfloat16)
    widened = stream.astype(jnp.float32)
    mean_square = jnp.mean(widened * widened, axis=-1, keepdims=True)
    normed = (widened * lax.rsqrt(mean_square + 1e-06) * norm_gain[None, :]).astype(jnp.bfloat16)
    qkv_sum = jnp.dot(
        normed, lax.all_gather(w_qkv, "seq", axis=0, tiled=True), preferred_element_type=jnp.float32
    )
    return (attn, stream, qkv_sum.astype(jnp.bfloat16))


def solution(mesh):
    small = mesh.shape["seq"] == 8 and mesh.shape["mp"] == 4
    seq, mp = "seq", "mp"
    if small:
        mesh = Mesh(mesh.devices.reshape(4, 2, 2, 2), ("z", "y", "x", "c"))
        seq, mp = ("z", "y"), ("x", "c")
    return jax.shard_map(
        on_block if small else on_device,
        mesh=mesh,
        in_specs=(
            P(seq, mp),
            P(seq, mp),
            P(seq, mp),
            P(None, seq, mp),
            P(),
            P(),
            P(),
            P(),
            P(seq, None),
            P(seq, None),
            P(seq, None),
            P(seq, mp),
            P(),
            P(seq, mp),
        ),
        out_specs=(P(seq, mp), P(seq, None), P(seq, mp)),
        check_vma=False,
    )
```

```python
import jax
import jax.numpy as jnp
from jax import lax
from jax.experimental import pallas as pl
from jax.experimental.pallas import tpu as pltpu
from jax.sharding import Mesh
from jax.sharding import PartitionSpec as P

QUERY_HEADS = 16
KEY_VALUE_HEADS = 8
HEAD_SIZE = 128
NT = (((1,), (1,)), ((), ()))
TN = (((0,), (0,)), ((), ()))
F32 = jnp.float32
HIDDEN = -1e30
BF16 = jnp.bfloat16


def cache_tags(pool_root, branch_owner, branch_len, root_count, slot_count, owner_ids):
    branch_count = branch_owner.shape[0]
    branch_ids = jnp.arange(branch_count, dtype=jnp.int32)
    owned = jnp.sum(
        jnp.where(branch_owner[None, :] == owner_ids[:, None], branch_ids[None, :], 0), axis=1
    )
    owned_length = jnp.sum(
        jnp.where(branch_ids[None, :] == owned[:, None], branch_len[None, :], 0), axis=1
    )
    slot_ids = jnp.arange(slot_count, dtype=jnp.int32)
    branch_tags = jnp.where(
        slot_ids[None, :] < owned_length[:, None], root_count + owned[:, None], -1
    )
    return jnp.concatenate([pool_root, branch_tags], axis=1).reshape(-1)


def token_branches(request_branch, token_request):
    requests = token_request[0]
    local_branches = request_branch[0]
    request_ids = jnp.arange(local_branches.shape[0], dtype=jnp.int32)
    token_branch = jnp.sum(
        jnp.where(requests[:, None] == request_ids[None, :], local_branches[None, :], 0), axis=1
    )
    return requests, token_branch


def head_lanes(h):
    return slice(h * HEAD_SIZE, (h + 1) * HEAD_SIZE)


def seq_index():
    return 2 * lax.axis_index("z") + lax.axis_index("y")


def chunk_offset(e, k, width):
    return pl.multiple_of((e ^ (k // 2)) * (2 * width) + (k % 2) * width, width)


def mp_index():
    return 2 * lax.axis_index("x") + lax.axis_index("c")


def attend_kernel(local_ref, res_ref, bias_ref, *refs):
    caches, out_ref, sends = refs[:-5], refs[-5], refs[-4:]
    e, m = seq_index(), mp_index()
    tok, wide = out_ref.shape
    kv = caches[0].shape[2]
    q_ref, kf_ref, vf_ref = (
        local_ref.at[:, :wide],
        local_ref.at[:, wide : wide + kv],
        local_ref.at[:, wide + kv :],
    )
    rows = caches[0].shape[1]
    bias = jnp.concatenate(
        [bias_ref[:tok]]
        + [
            bias_ref[pl.ds(pl.multiple_of(tok + (e ^ s) * rows, rows), rows), :]
            for s in range(len(caches))
        ],
        axis=0,
    )
    for k in range(kf_ref.shape[1] // HEAD_SIZE):
        lanes, first, second = head_lanes(k), head_lanes(2 * k), head_lanes(2 * k + 1)
        keys = jnp.concatenate([kf_ref[:, lanes]] + [c[0, :, lanes] for c in caches], axis=0)
        values = jnp.concatenate([vf_ref[:, lanes]] + [c[1, :, lanes] for c in caches], axis=0)
        queries = jnp.concatenate([q_ref[:, first], q_ref[:, second]], axis=0)
        scores = (
            lax.dot_general(keys, queries, NT, preferred_element_type=F32) * HEAD_SIZE**-0.5 + bias
        )
        peak = jnp.max(scores, axis=0, keepdims=True)
        prob = jnp.exp(scores - peak)
        total = jnp.sum(prob, axis=0, keepdims=True)
        mixed = lax.dot_general(values, prob.astype(BF16), TN, preferred_element_type=F32)
        attn = (mixed / total).T.astype(BF16)
        for ref in (out_ref, *sends):
            ref[:, first] = attn[:tok]
            ref[:, second] = attn[tok:]
    width = sends[0].shape[1] - wide
    for s, ref in enumerate(sends):
        ref[:, wide:] = res_ref[:, pl.ds(chunk_offset(e ^ (2 * s), m, width), width)]


def project_kernel(a0, a1, a2, a3, own_ref, par_ref, o0, o1, o2, o3, hold):
    m = mp_index()
    half, wide = own_ref.shape
    blocks = (a0, a1, a2, a3)
    attn = jnp.concatenate([a[:, :wide] for a in blocks], axis=0)
    rest = jnp.concatenate([a[:, wide:] for a in blocks], axis=0)
    hold[:, :half] = lax.dot_general(attn, own_ref[...], NT, preferred_element_type=F32)
    hold[:, half:] = lax.dot_general(attn, par_ref[...], NT, preferred_element_type=F32)
    width = o0.shape[1]
    for j, out in enumerate((o0, o1, o2, o3)):
        chunk = hold[:, pl.ds(pl.multiple_of((m ^ j) * width, width), width)]
        out[...] = chunk + rest.astype(F32) if j == 0 else chunk.astype(BF16)


def combine_kernel(r0, r1, r2, r3, out, t0, t1, t2, t3):
    tok = t0.shape[0]
    stream = (
        r0[...] + r1[...].astype(F32) + r2[...].astype(F32) + r3[...].astype(F32)
    ).astype(BF16)
    out[...] = stream
    for s, part in enumerate((t0, t1, t2, t3)):
        part[...] = stream[s * tok : (s + 1) * tok]


def qkv_kernel(x0, x1, x2, x3, gain_ref, own_ref, par_ref, o0, o1, o2, o3, hold):
    e, m = seq_index(), mp_index()
    width = x0.shape[1]
    half = 2 * width
    tok = o0.shape[0]
    for j, part in enumerate((x0, x1, x2, x3)):
        k = m ^ j
        gain = gain_ref[:, pl.ds(chunk_offset(e, k, width), width)]
        hold[:, pl.ds(pl.multiple_of(k * width, width), width)] = (
            part[...].astype(F32) * gain
        ).astype(BF16)
    product = jnp.dot(hold[:, :half], own_ref[...], preferred_element_type=F32) + jnp.dot(
        hold[:, half:], par_ref[...], preferred_element_type=F32
    )
    for s, out in enumerate((o0, o1, o2, o3)):
        out[...] = product[s * tok : (s + 1) * tok].astype(out.dtype)


def pack_kernel(t0, t1, t2, t3, out_ref):
    width = t0.shape[1]
    for s, part in enumerate((t0, t1, t2, t3)):
        out_ref[:, s * width : (s + 1) * width] = part[...]


def finish_kernel(y0, y1, y2, y3, p0, p1, p2, p3, qkv_ref, stream_ref):
    e, m = seq_index(), mp_index()
    width = p0.shape[1] // 4
    squares = jnp.zeros((p0.shape[0], width), F32)
    for j, part in enumerate((p0, p1, p2, p3)):
        for s in range(4):
            block = part[:, s * width : (s + 1) * width]
            wide = block.astype(F32)
            squares = squares + wide * wide
            stream_ref[:, pl.ds(chunk_offset(e ^ (2 * s), m ^ j, width), width)] = block
    mean_square = jnp.sum(squares, axis=1, keepdims=True) / stream_ref.shape[1]
    total = y0[...] + y1[...].astype(F32) + y2[...].astype(F32) + y3[...].astype(F32)
    qkv_ref[...] = (total * lax.rsqrt(mean_square + 1e-06)).astype(BF16)


def call(kernel, out_shape, args, scratch=(), flops=0, moved=1 << 20):
    vmem = pl.BlockSpec(memory_space=pltpu.VMEM)
    return pl.pallas_call(
        kernel,
        out_shape=out_shape,
        in_specs=[vmem] * len(args),
        out_specs=jax.tree.map(lambda _: vmem, out_shape),
        scratch_shapes=list(scratch),
        compiler_params=pltpu.CompilerParams(vmem_limit_bytes=24 << 20),
        cost_estimate=pl.CostEstimate(flops=flops, bytes_accessed=moved, transcendentals=0),
    )(*args)


def swap(value, axes, bits):
    count = lax.axis_size(axes)
    return lax.ppermute(value, axes, [(i, i ^ bits) for i in range(count)])


def on_block(
    fresh_queries,
    fresh_keys,
    fresh_values,
    cache,
    pool_root,
    branch_owner,
    branch_len,
    branch_root,
    request_branch,
    token_request,
    residual,
    wo_t,
    norm_gain,
    w_qkv,
):
    tok, wide = fresh_queries.shape
    width = wo_t.shape[0] // 2
    columns = w_qkv.shape[1]
    sds = jax.ShapeDtypeStruct
    mp = ("x", "c")

    along = [cache] + [swap(cache, "z", s) for s in range(1, 4)]
    beside = swap(cache, "y", 1)

    holders = pool_root.shape[0]
    requests, token_branch = token_branches(request_branch, token_request)
    branch_ids = jnp.arange(branch_root.shape[0], dtype=jnp.int32)
    chosen = token_branch[:, None] == branch_ids[None, :]
    token_root, token_owner, token_length = (
        jnp.sum(jnp.where(chosen, per_branch[None, :], 0), axis=1)
        for per_branch in (branch_root, branch_owner, branch_len)
    )
    positions = jnp.arange(tok, dtype=jnp.int32)
    own_seen = (requests[None, :] == requests[:, None]) & (
        positions[:, None] <= positions[None, :]
    )
    slot_count = cache.shape[1] - pool_root.shape[1]
    slots = jnp.arange(slot_count, dtype=jnp.int32)
    at = jnp.arange(holders, dtype=jnp.int32)
    root_seen = pool_root[:, :, None] == token_root[None, None, :]
    branch_seen = (token_owner[None, None, :] == at[:, None, None]) & (
        slots[None, :, None] < token_length[None, None, :]
    )
    pool_seen = jnp.concatenate([root_seen, branch_seen], axis=1).reshape(-1, tok)
    seen = jnp.concatenate([own_seen, pool_seen], axis=0)
    bias = jnp.where(jnp.concatenate([seen, seen], axis=1), 0.0, HIDDEN).astype(F32)

    local = jnp.concatenate([fresh_queries, fresh_keys, fresh_values], axis=1)
    along[1:], bias, local = lax.optimization_barrier((along[1:], bias, local))
    across = [beside] + [swap(mine, "y", 1) for mine in along[1:]]
    blocks = [block for pair in zip(along, across) for block in pair]
    wo_pair = swap(wo_t, "y", 1)
    blocks, wo_pair, wq_later = lax.optimization_barrier((blocks, wo_pair, w_qkv))
    wq_pair = swap(wq_later, "y", 1)
    attn, *sends = call(
        attend_kernel,
        [sds((tok, wide), BF16)] + [sds((tok, wide + width), BF16)] * 4,
        (local, residual, bias, *blocks),
        flops=1 << 26,
    )
    a2, a3, a1 = (swap(sends[s], "z", s) for s in (2, 3, 1))
    sums = call(
        project_kernel,
        [sds((4 * tok, width), F32)] + [sds((4 * tok, width), BF16)] * 3,
        (sends[0], a1, a2, a3, wo_t, wo_pair),
        scratch=[pltpu.VMEM((4 * tok, 4 * width), F32)],
        flops=1 << 27,
    )
    sums = [sums[0]] + [swap(sums[j], mp, j) for j in range(1, 4)]
    made = call(
        combine_kernel,
        [sds((4 * tok, width), BF16)] + [sds((tok, width), BF16)] * 4,
        tuple(sums),
    )
    made, wq_pair = lax.optimization_barrier((made, wq_pair))
    slices = [made[0]] + [swap(made[0], mp, j) for j in range(1, 4)]
    home = [made[1]] + [swap(made[1 + s], "z", s) for s in range(1, 4)]
    partial = call(
        qkv_kernel,
        [sds((tok, columns), F32)] + [sds((tok, columns), BF16)] * 3,
        (*slices, norm_gain[None, :], w_qkv, wq_pair),
        scratch=[pltpu.VMEM((4 * tok, 4 * width), BF16)],
        flops=1 << 28,
    )
    y1, y2, y3 = (swap(partial[s], "z", s) for s in (1, 2, 3))
    home, own_partial = lax.optimization_barrier((home, partial[0]))
    packed = call(pack_kernel, sds((tok, 4 * width), BF16), tuple(home))
    pieces = [packed] + [swap(packed, mp, j) for j in range(1, 4)]
    qkv_next, stream = call(
        finish_kernel,
        [sds((tok, columns), BF16), sds(residual.shape, BF16)],
        (own_partial, y1, y2, y3, *pieces),
    )
    return attn, stream, qkv_next


def absorb(running, query_rows, key_row_block, value_rows, visible, score_scale):
    peak_old, total, mixed = running
    scores = (
        jnp.einsum("tkgd,rkd->tkgr", query_rows, key_row_block, preferred_element_type=jnp.float32)
        * score_scale
    )
    seen = visible[:, None, None, :]
    peak_new = jnp.maximum(peak_old, jnp.max(jnp.where(seen, scores, -jnp.inf), axis=-1))
    factor = jnp.exp(peak_old - peak_new)
    weights_full = jnp.where(seen, jnp.exp(scores - peak_new[..., None]), 0.0)
    total = total * factor + jnp.sum(weights_full, axis=-1)
    mixed = mixed * factor[..., None] + jnp.einsum(
        "tkgr,rkd->tkgd",
        weights_full.astype(jnp.bfloat16),
        value_rows,
        preferred_element_type=jnp.float32,
    )
    return (peak_new, total, mixed)


def on_device(
    fresh_queries,
    fresh_keys,
    fresh_values,
    cache,
    pool_root,
    branch_owner,
    branch_len,
    branch_root,
    request_branch,
    token_request,
    residual,
    wo_t,
    norm_gain,
    w_qkv,
):
    seq_count = lax.axis_size("seq")
    root_count = seq_count // 4
    tok_rows = fresh_queries.shape[0]
    kv_local = fresh_keys.shape[1] // HEAD_SIZE
    query_groups = QUERY_HEADS // KEY_VALUE_HEADS
    score_scale = HEAD_SIZE ** (-0.5)
    slot_count = cache.shape[1] - pool_root.shape[1]
    owner_ids = jnp.arange(seq_count, dtype=jnp.int32)
    tags = cache_tags(pool_root, branch_owner, branch_len, root_count, slot_count, owner_ids)
    requests, token_branch = token_branches(request_branch, token_request)
    branch_ids = jnp.arange(branch_root.shape[0], dtype=jnp.int32)
    token_root = jnp.sum(
        jnp.where(token_branch[:, None] == branch_ids[None, :], branch_root[None, :], 0), axis=1
    )
    query_rows = fresh_queries.reshape(tok_rows, kv_local, query_groups, HEAD_SIZE)
    incoming_keys = fresh_keys.reshape(tok_rows, kv_local, HEAD_SIZE)
    incoming_values = fresh_values.reshape(tok_rows, kv_local, HEAD_SIZE)
    positions = jnp.arange(tok_rows, dtype=jnp.int32)
    own_visible = (requests[None, :] == requests[:, None]) & (
        positions[None, :] <= positions[:, None]
    )
    start_state = (
        jnp.full((tok_rows, kv_local, query_groups), -jnp.inf, jnp.float32),
        jnp.zeros((tok_rows, kv_local, query_groups), jnp.float32),
        jnp.zeros((tok_rows, kv_local, query_groups, HEAD_SIZE), jnp.float32),
    )
    state = absorb(
        start_state, query_rows, incoming_keys, incoming_values, own_visible, score_scale
    )
    piece = lax.all_gather(cache, "seq", axis=1, tiled=True)
    rows = piece.shape[1]
    block = 512 if rows > 512 and rows % 512 == 0 else rows
    key_blocks = piece[0].reshape(rows // block, block, kv_local, HEAD_SIZE)
    value_blocks = piece[1].reshape(rows // block, block, kv_local, HEAD_SIZE)
    tag_blocks = tags.reshape(rows // block, block)

    def one_block(running, parts):
        key_row_block, value_rows, tag_rows = parts
        visible = (tag_rows[None, :] == token_root[:, None]) | (
            tag_rows[None, :] == root_count + token_branch[:, None]
        )
        updated = absorb(running, query_rows, key_row_block, value_rows, visible, score_scale)
        return (updated, None)

    state, unused = lax.scan(one_block, state, (key_blocks, value_blocks, tag_blocks))
    peak_final, total_final, mixed_final = state
    attn = (
        (mixed_final / total_final[..., None])
        .reshape(tok_rows, kv_local * query_groups * HEAD_SIZE)
        .astype(jnp.bfloat16)
    )
    partial_value = lax.dot_general(
        attn,
        lax.all_gather(wo_t, "seq", axis=0, tiled=True),
        (((1,), (1,)), ((), ())),
        preferred_element_type=jnp.float32,
    )
    summed = lax.psum(partial_value.astype(jnp.bfloat16), "mp").astype(jnp.float32)
    stream = (residual.astype(jnp.float32) + summed).astype(jnp.bfloat16)
    widened = stream.astype(jnp.float32)
    mean_square = jnp.mean(widened * widened, axis=-1, keepdims=True)
    normed = (widened * lax.rsqrt(mean_square + 1e-06) * norm_gain[None, :]).astype(jnp.bfloat16)
    qkv_sum = jnp.dot(
        normed, lax.all_gather(w_qkv, "seq", axis=0, tiled=True), preferred_element_type=jnp.float32
    )
    return (attn, stream, qkv_sum.astype(jnp.bfloat16))


def solution(mesh):
    small = mesh.shape["seq"] == 8 and mesh.shape["mp"] == 4
    seq, mp = "seq", "mp"
    if small:
        mesh = Mesh(mesh.devices.reshape(4, 2, 2, 2), ("z", "y", "x", "c"))
        seq, mp = ("z", "y"), ("x", "c")
    return jax.shard_map(
        on_block if small else on_device,
        mesh=mesh,
        in_specs=(
            P(seq, mp),
            P(seq, mp),
            P(seq, mp),
            P(None, seq, mp),
            P(),
            P(),
            P(),
            P(),
            P(seq, None),
            P(seq, None),
            P(seq, None),
            P(seq, mp),
            P(),
            P(seq, mp),
        ),
        out_specs=(P(seq, mp), P(seq, None), P(seq, mp)),
        check_vma=False,
    )
```

```python
import jax
import jax.numpy as jnp
from jax import lax
from jax.experimental import pallas as pl
from jax.experimental.pallas import tpu as pltpu
from jax.sharding import Mesh
from jax.sharding import PartitionSpec as P

QUERY_HEADS = 16
KEY_VALUE_HEADS = 8
HEAD_SIZE = 128
NT = (((1,), (1,)), ((), ()))
TN = (((0,), (0,)), ((), ()))
F32 = jnp.float32
HIDDEN = -1e30
BF16 = jnp.bfloat16


def cache_tags(pool_root, branch_owner, branch_len, root_count, slot_count, owner_ids):
    branch_count = branch_owner.shape[0]
    branch_ids = jnp.arange(branch_count, dtype=jnp.int32)
    owned = jnp.sum(
        jnp.where(branch_owner[None, :] == owner_ids[:, None], branch_ids[None, :], 0), axis=1
    )
    owned_length = jnp.sum(
        jnp.where(branch_ids[None, :] == owned[:, None], branch_len[None, :], 0), axis=1
    )
    slot_ids = jnp.arange(slot_count, dtype=jnp.int32)
    branch_tags = jnp.where(
        slot_ids[None, :] < owned_length[:, None], root_count + owned[:, None], -1
    )
    return jnp.concatenate([pool_root, branch_tags], axis=1).reshape(-1)


def token_branches(request_branch, token_request):
    requests = token_request[0]
    local_branches = request_branch[0]
    request_ids = jnp.arange(local_branches.shape[0], dtype=jnp.int32)
    token_branch = jnp.sum(
        jnp.where(requests[:, None] == request_ids[None, :], local_branches[None, :], 0), axis=1
    )
    return requests, token_branch


def head_lanes(h):
    return slice(h * HEAD_SIZE, (h + 1) * HEAD_SIZE)


def seq_index():
    return 2 * lax.axis_index("z") + lax.axis_index("y")


def chunk_offset(e, k, width):
    return pl.multiple_of((e ^ (k // 2)) * (2 * width) + (k % 2) * width, width)


def mp_index():
    return 2 * lax.axis_index("x") + lax.axis_index("c")


def attend_kernel(local_ref, res_ref, bias_ref, *refs):
    caches, out_ref, sends = refs[:-5], refs[-5], refs[-4:]
    e, m = seq_index(), mp_index()
    tok, wide = out_ref.shape
    kv = caches[0].shape[2]
    q_ref, kf_ref, vf_ref = (
        local_ref.at[:, :wide],
        local_ref.at[:, wide : wide + kv],
        local_ref.at[:, wide + kv :],
    )
    rows = caches[0].shape[1]
    bias = jnp.concatenate(
        [bias_ref[:tok]]
        + [
            bias_ref[pl.ds(pl.multiple_of(tok + (e ^ s) * rows, rows), rows), :]
            for s in range(len(caches))
        ],
        axis=0,
    )
    for k in range(kf_ref.shape[1] // HEAD_SIZE):
        lanes, first, second = head_lanes(k), head_lanes(2 * k), head_lanes(2 * k + 1)
        keys = jnp.concatenate([kf_ref[:, lanes]] + [c[0, :, lanes] for c in caches], axis=0)
        values = jnp.concatenate([vf_ref[:, lanes]] + [c[1, :, lanes] for c in caches], axis=0)
        queries = jnp.concatenate([q_ref[:, first], q_ref[:, second]], axis=0)
        scores = (
            lax.dot_general(keys, queries, NT, preferred_element_type=F32) * HEAD_SIZE**-0.5 + bias
        )
        peak = jnp.max(scores, axis=0, keepdims=True)
        prob = jnp.exp(scores - peak)
        total = jnp.sum(prob, axis=0, keepdims=True)
        mixed = lax.dot_general(values, prob.astype(BF16), TN, preferred_element_type=F32)
        attn = (mixed / total).T.astype(BF16)
        for ref in (out_ref, *sends):
            ref[:, first] = attn[:tok]
            ref[:, second] = attn[tok:]
    width = sends[0].shape[1] - wide
    for s, ref in enumerate(sends):
        ref[:, wide:] = res_ref[:, pl.ds(chunk_offset(e ^ (2 * s), m, width), width)]


def project_kernel(a2, a3, a1, a0, own_ref, par_ref, o0, o1, o2, o3, hold):
    m = mp_index()
    half, wide = own_ref.shape
    blocks = (a0, a1, a2, a3)
    attn = jnp.concatenate([a[:, :wide] for a in blocks], axis=0)
    rest = jnp.concatenate([a[:, wide:] for a in blocks], axis=0)
    hold[:, :half] = lax.dot_general(attn, own_ref[...], NT, preferred_element_type=F32)
    hold[:, half:] = lax.dot_general(attn, par_ref[...], NT, preferred_element_type=F32)
    width = o0.shape[1]
    for j, out in enumerate((o0, o1, o2, o3)):
        chunk = hold[:, pl.ds(pl.multiple_of((m ^ j) * width, width), width)]
        out[...] = chunk + rest.astype(F32) if j == 0 else chunk.astype(BF16)


def combine_kernel(r2, r3, r1, r0, out, t0, t1, t2, t3):
    tok = t0.shape[0]
    stream = (
        r0[...] + r1[...].astype(F32) + r2[...].astype(F32) + r3[...].astype(F32)
    ).astype(BF16)
    out[...] = stream
    for s, part in enumerate((t0, t1, t2, t3)):
        part[...] = stream[s * tok : (s + 1) * tok]


def qkv_kernel(x0, x1, x2, x3, gain_ref, own_ref, par_ref, o0, o1, o2, o3, hold):
    e, m = seq_index(), mp_index()
    width = x0.shape[1]
    half = 2 * width
    tok = o0.shape[0]
    for j, part in enumerate((x0, x1, x2, x3)):
        k = m ^ j
        gain = gain_ref[:, pl.ds(chunk_offset(e, k, width), width)]
        hold[:, pl.ds(pl.multiple_of(k * width, width), width)] = (
            part[...].astype(F32) * gain
        ).astype(BF16)
    product = jnp.dot(hold[:, :half], own_ref[...], preferred_element_type=F32) + jnp.dot(
        hold[:, half:], par_ref[...], preferred_element_type=F32
    )
    for s, out in enumerate((o0, o1, o2, o3)):
        out[...] = product[s * tok : (s + 1) * tok].astype(out.dtype)


def pack_kernel(t0, t1, t2, t3, out_ref):
    width = t0.shape[1]
    for s, part in enumerate((t0, t1, t2, t3)):
        out_ref[:, s * width : (s + 1) * width] = part[...]


def finish_kernel(p0, p1, p2, p3, y2, y3, y1, y0, qkv_ref, stream_ref):
    e, m = seq_index(), mp_index()
    width = p0.shape[1] // 4
    squares = jnp.zeros((p0.shape[0], width), F32)
    for j, part in enumerate((p0, p1, p2, p3)):
        for s in range(4):
            block = part[:, s * width : (s + 1) * width]
            wide = block.astype(F32)
            squares = squares + wide * wide
            stream_ref[:, pl.ds(chunk_offset(e ^ (2 * s), m ^ j, width), width)] = block
    mean_square = jnp.sum(squares, axis=1, keepdims=True) / stream_ref.shape[1]
    total = y0[...] + y1[...].astype(F32) + y2[...].astype(F32) + y3[...].astype(F32)
    qkv_ref[...] = (total * lax.rsqrt(mean_square + 1e-06)).astype(BF16)


def call(kernel, out_shape, args, scratch=(), flops=0, moved=1 << 20):
    vmem = pl.BlockSpec(memory_space=pltpu.VMEM)
    return pl.pallas_call(
        kernel,
        out_shape=out_shape,
        in_specs=[vmem] * len(args),
        out_specs=jax.tree.map(lambda _: vmem, out_shape),
        scratch_shapes=list(scratch),
        compiler_params=pltpu.CompilerParams(vmem_limit_bytes=24 << 20),
        cost_estimate=pl.CostEstimate(flops=flops, bytes_accessed=moved, transcendentals=0),
    )(*args)


def swap(value, axes, bits):
    count = lax.axis_size(axes)
    return lax.ppermute(value, axes, [(i, i ^ bits) for i in range(count)])


def on_block(
    fresh_queries,
    fresh_keys,
    fresh_values,
    cache,
    pool_root,
    branch_owner,
    branch_len,
    branch_root,
    request_branch,
    token_request,
    residual,
    wo_t,
    norm_gain,
    w_qkv,
):
    tok, wide = fresh_queries.shape
    width = wo_t.shape[0] // 2
    columns = w_qkv.shape[1]
    sds = jax.ShapeDtypeStruct
    mp = ("x", "c")

    along = [cache] + [swap(cache, "z", s) for s in range(1, 4)]
    beside = swap(cache, "y", 1)

    holders = pool_root.shape[0]
    requests, token_branch = token_branches(request_branch, token_request)
    branch_ids = jnp.arange(branch_root.shape[0], dtype=jnp.int32)
    chosen = token_branch[:, None] == branch_ids[None, :]
    token_root, token_owner, token_length = (
        jnp.sum(jnp.where(chosen, per_branch[None, :], 0), axis=1)
        for per_branch in (branch_root, branch_owner, branch_len)
    )
    positions = jnp.arange(tok, dtype=jnp.int32)
    own_seen = (requests[None, :] == requests[:, None]) & (
        positions[:, None] <= positions[None, :]
    )
    slot_count = cache.shape[1] - pool_root.shape[1]
    slots = jnp.arange(slot_count, dtype=jnp.int32)
    at = jnp.arange(holders, dtype=jnp.int32)
    root_seen = pool_root[:, :, None] == token_root[None, None, :]
    branch_seen = (token_owner[None, None, :] == at[:, None, None]) & (
        slots[None, :, None] < token_length[None, None, :]
    )
    pool_seen = jnp.concatenate([root_seen, branch_seen], axis=1).reshape(-1, tok)
    seen = jnp.concatenate([own_seen, pool_seen], axis=0)
    bias = jnp.where(jnp.concatenate([seen, seen], axis=1), 0.0, HIDDEN).astype(F32)

    local = jnp.concatenate([fresh_queries, fresh_keys, fresh_values], axis=1)
    along[1:], bias, local = lax.optimization_barrier((along[1:], bias, local))
    across = [beside] + [swap(mine, "y", 1) for mine in along[1:]]
    blocks = [block for pair in zip(along, across) for block in pair]
    wo_pair = swap(wo_t, "y", 1)
    blocks, wo_pair, wq_later = lax.optimization_barrier((blocks, wo_pair, w_qkv))
    wq_pair = swap(wq_later, "y", 1)
    attn, *sends = call(
        attend_kernel,
        [sds((tok, wide), BF16)] + [sds((tok, wide + width), BF16)] * 4,
        (local, residual, bias, *blocks),
        flops=1 << 26,
    )
    a2, a3, a1 = (swap(sends[s], "z", s) for s in (2, 3, 1))
    sums = call(
        project_kernel,
        [sds((4 * tok, width), F32)] + [sds((4 * tok, width), BF16)] * 3,
        (a2, a3, a1, sends[0], wo_t, wo_pair),
        scratch=[pltpu.VMEM((4 * tok, 4 * width), F32)],
        flops=1 << 27,
    )
    sums = [sums[0]] + [swap(sums[j], mp, j) for j in range(1, 4)]
    made = call(
        combine_kernel,
        [sds((4 * tok, width), BF16)] + [sds((tok, width), BF16)] * 4,
        (sums[2], sums[3], sums[1], sums[0]),
    )
    made, wq_pair = lax.optimization_barrier((made, wq_pair))
    slices = [made[0]] + [swap(made[0], mp, j) for j in range(1, 4)]
    home = [made[1]] + [swap(made[1 + s], "z", s) for s in range(1, 4)]
    partial = call(
        qkv_kernel,
        [sds((tok, columns), F32)] + [sds((tok, columns), BF16)] * 3,
        (*slices, norm_gain[None, :], w_qkv, wq_pair),
        scratch=[pltpu.VMEM((4 * tok, 4 * width), BF16)],
        flops=1 << 28,
    )
    y1, y2, y3 = (swap(partial[s], "z", s) for s in (1, 2, 3))
    home, own_partial = lax.optimization_barrier((home, partial[0]))
    packed = call(pack_kernel, sds((tok, 4 * width), BF16), tuple(home))
    pieces = [packed] + [swap(packed, mp, j) for j in range(1, 4)]
    qkv_next, stream = call(
        finish_kernel,
        [sds((tok, columns), BF16), sds(residual.shape, BF16)],
        (*pieces, y2, y3, y1, own_partial),
    )
    return attn, stream, qkv_next


def absorb(running, query_rows, key_row_block, value_rows, visible, score_scale):
    peak_old, total, mixed = running
    scores = (
        jnp.einsum("tkgd,rkd->tkgr", query_rows, key_row_block, preferred_element_type=jnp.float32)
        * score_scale
    )
    seen = visible[:, None, None, :]
    peak_new = jnp.maximum(peak_old, jnp.max(jnp.where(seen, scores, -jnp.inf), axis=-1))
    factor = jnp.exp(peak_old - peak_new)
    weights_full = jnp.where(seen, jnp.exp(scores - peak_new[..., None]), 0.0)
    total = total * factor + jnp.sum(weights_full, axis=-1)
    mixed = mixed * factor[..., None] + jnp.einsum(
        "tkgr,rkd->tkgd",
        weights_full.astype(jnp.bfloat16),
        value_rows,
        preferred_element_type=jnp.float32,
    )
    return (peak_new, total, mixed)


def on_device(
    fresh_queries,
    fresh_keys,
    fresh_values,
    cache,
    pool_root,
    branch_owner,
    branch_len,
    branch_root,
    request_branch,
    token_request,
    residual,
    wo_t,
    norm_gain,
    w_qkv,
):
    seq_count = lax.axis_size("seq")
    root_count = seq_count // 4
    tok_rows = fresh_queries.shape[0]
    kv_local = fresh_keys.shape[1] // HEAD_SIZE
    query_groups = QUERY_HEADS // KEY_VALUE_HEADS
    score_scale = HEAD_SIZE ** (-0.5)
    slot_count = cache.shape[1] - pool_root.shape[1]
    owner_ids = jnp.arange(seq_count, dtype=jnp.int32)
    tags = cache_tags(pool_root, branch_owner, branch_len, root_count, slot_count, owner_ids)
    requests, token_branch = token_branches(request_branch, token_request)
    branch_ids = jnp.arange(branch_root.shape[0], dtype=jnp.int32)
    token_root = jnp.sum(
        jnp.where(token_branch[:, None] == branch_ids[None, :], branch_root[None, :], 0), axis=1
    )
    query_rows = fresh_queries.reshape(tok_rows, kv_local, query_groups, HEAD_SIZE)
    incoming_keys = fresh_keys.reshape(tok_rows, kv_local, HEAD_SIZE)
    incoming_values = fresh_values.reshape(tok_rows, kv_local, HEAD_SIZE)
    positions = jnp.arange(tok_rows, dtype=jnp.int32)
    own_visible = (requests[None, :] == requests[:, None]) & (
        positions[None, :] <= positions[:, None]
    )
    start_state = (
        jnp.full((tok_rows, kv_local, query_groups), -jnp.inf, jnp.float32),
        jnp.zeros((tok_rows, kv_local, query_groups), jnp.float32),
        jnp.zeros((tok_rows, kv_local, query_groups, HEAD_SIZE), jnp.float32),
    )
    state = absorb(
        start_state, query_rows, incoming_keys, incoming_values, own_visible, score_scale
    )
    piece = lax.all_gather(cache, "seq", axis=1, tiled=True)
    rows = piece.shape[1]
    block = 512 if rows > 512 and rows % 512 == 0 else rows
    key_blocks = piece[0].reshape(rows // block, block, kv_local, HEAD_SIZE)
    value_blocks = piece[1].reshape(rows // block, block, kv_local, HEAD_SIZE)
    tag_blocks = tags.reshape(rows // block, block)

    def one_block(running, parts):
        key_row_block, value_rows, tag_rows = parts
        visible = (tag_rows[None, :] == token_root[:, None]) | (
            tag_rows[None, :] == root_count + token_branch[:, None]
        )
        updated = absorb(running, query_rows, key_row_block, value_rows, visible, score_scale)
        return (updated, None)

    state, unused = lax.scan(one_block, state, (key_blocks, value_blocks, tag_blocks))
    peak_final, total_final, mixed_final = state
    attn = (
        (mixed_final / total_final[..., None])
        .reshape(tok_rows, kv_local * query_groups * HEAD_SIZE)
        .astype(jnp.bfloat16)
    )
    partial_value = lax.dot_general(
        attn,
        lax.all_gather(wo_t, "seq", axis=0, tiled=True),
        (((1,), (1,)), ((), ())),
        preferred_element_type=jnp.float32,
    )
    summed = lax.psum(partial_value.astype(jnp.bfloat16), "mp").astype(jnp.float32)
    stream = (residual.astype(jnp.float32) + summed).astype(jnp.bfloat16)
    widened = stream.astype(jnp.float32)
    mean_square = jnp.mean(widened * widened, axis=-1, keepdims=True)
    normed = (widened * lax.rsqrt(mean_square + 1e-06) * norm_gain[None, :]).astype(jnp.bfloat16)
    qkv_sum = jnp.dot(
        normed, lax.all_gather(w_qkv, "seq", axis=0, tiled=True), preferred_element_type=jnp.float32
    )
    return (attn, stream, qkv_sum.astype(jnp.bfloat16))


def solution(mesh):
    small = mesh.shape["seq"] == 8 and mesh.shape["mp"] == 4
    seq, mp = "seq", "mp"
    if small:
        mesh = Mesh(mesh.devices.reshape(4, 2, 2, 2), ("z", "y", "x", "c"))
        seq, mp = ("z", "y"), ("x", "c")
    return jax.shard_map(
        on_block if small else on_device,
        mesh=mesh,
        in_specs=(
            P(seq, mp),
            P(seq, mp),
            P(seq, mp),
            P(None, seq, mp),
            P(),
            P(),
            P(),
            P(),
            P(seq, None),
            P(seq, None),
            P(seq, None),
            P(seq, mp),
            P(),
            P(seq, mp),
        ),
        out_specs=(P(seq, mp), P(seq, None), P(seq, mp)),
        check_vma=False,
    )
```

```python
import jax
import jax.numpy as jnp
from jax import lax
from jax.experimental import pallas as pl
from jax.experimental.pallas import tpu as pltpu
from jax.sharding import Mesh
from jax.sharding import PartitionSpec as P

QUERY_HEADS = 16
KEY_VALUE_HEADS = 8
HEAD_SIZE = 128
NT = (((1,), (1,)), ((), ()))
TN = (((0,), (0,)), ((), ()))
F32 = jnp.float32
HIDDEN = -1e30
BF16 = jnp.bfloat16


def cache_tags(pool_root, branch_owner, branch_len, root_count, slot_count, owner_ids):
    branch_count = branch_owner.shape[0]
    branch_ids = jnp.arange(branch_count, dtype=jnp.int32)
    owned = jnp.sum(
        jnp.where(branch_owner[None, :] == owner_ids[:, None], branch_ids[None, :], 0), axis=1
    )
    owned_length = jnp.sum(
        jnp.where(branch_ids[None, :] == owned[:, None], branch_len[None, :], 0), axis=1
    )
    slot_ids = jnp.arange(slot_count, dtype=jnp.int32)
    branch_tags = jnp.where(
        slot_ids[None, :] < owned_length[:, None], root_count + owned[:, None], -1
    )
    return jnp.concatenate([pool_root, branch_tags], axis=1).reshape(-1)


def token_branches(request_branch, token_request):
    requests = token_request[0]
    local_branches = request_branch[0]
    request_ids = jnp.arange(local_branches.shape[0], dtype=jnp.int32)
    token_branch = jnp.sum(
        jnp.where(requests[:, None] == request_ids[None, :], local_branches[None, :], 0), axis=1
    )
    return requests, token_branch


def head_lanes(h):
    return slice(h * HEAD_SIZE, (h + 1) * HEAD_SIZE)


def seq_index():
    return 2 * lax.axis_index("z") + lax.axis_index("y")


def chunk_offset(e, k, width):
    return pl.multiple_of((e ^ (k // 2)) * (2 * width) + (k % 2) * width, width)


def mp_index():
    return 2 * lax.axis_index("x") + lax.axis_index("c")


def attend_kernel(local_ref, res_ref, bias_ref, *refs):
    caches, out_ref, sends = refs[:-5], refs[-5], refs[-4:]
    e, m = seq_index(), mp_index()
    tok, wide = out_ref.shape
    kv = caches[0].shape[2]
    q_ref, kf_ref, vf_ref = (
        local_ref.at[:, :wide],
        local_ref.at[:, wide : wide + kv],
        local_ref.at[:, wide + kv :],
    )
    rows = caches[0].shape[1]
    bias = jnp.concatenate(
        [bias_ref[:tok]]
        + [
            bias_ref[pl.ds(pl.multiple_of(tok + (e ^ s) * rows, rows), rows), :]
            for s in range(len(caches))
        ],
        axis=0,
    )
    for k in range(kf_ref.shape[1] // HEAD_SIZE):
        lanes, first, second = head_lanes(k), head_lanes(2 * k), head_lanes(2 * k + 1)
        keys = jnp.concatenate([kf_ref[:, lanes]] + [c[0, :, lanes] for c in caches], axis=0)
        values = jnp.concatenate([vf_ref[:, lanes]] + [c[1, :, lanes] for c in caches], axis=0)
        queries = jnp.concatenate([q_ref[:, first], q_ref[:, second]], axis=0)
        scores = (
            lax.dot_general(keys, queries, NT, preferred_element_type=F32) * HEAD_SIZE**-0.5 + bias
        )
        peak = jnp.max(scores, axis=0, keepdims=True)
        prob = jnp.exp(scores - peak)
        total = jnp.sum(prob, axis=0, keepdims=True)
        mixed = lax.dot_general(values, prob.astype(BF16), TN, preferred_element_type=F32)
        attn = (mixed / total).T.astype(BF16)
        for ref in (out_ref, *sends):
            ref[:, first] = attn[:tok]
            ref[:, second] = attn[tok:]
    width = sends[0].shape[1] - wide
    for s, ref in enumerate(sends):
        ref[:, wide:] = res_ref[:, pl.ds(chunk_offset(e ^ (2 * s), m, width), width)]


def project_kernel(a2, a3, a1, a0, own_ref, par_ref, o0, o1, o2, o3, hold):
    m = mp_index()
    half, wide = own_ref.shape
    blocks = (a0, a1, a2, a3)
    attn = jnp.concatenate([a[:, :wide] for a in blocks], axis=0)
    rest = jnp.concatenate([a[:, wide:] for a in blocks], axis=0)
    hold[:, :half] = lax.dot_general(attn, own_ref[...], NT, preferred_element_type=F32)
    hold[:, half:] = lax.dot_general(attn, par_ref[...], NT, preferred_element_type=F32)
    width = o0.shape[1]
    for j, out in enumerate((o0, o1, o2, o3)):
        chunk = hold[:, pl.ds(pl.multiple_of((m ^ j) * width, width), width)]
        out[...] = chunk + rest.astype(F32) if j == 0 else chunk.astype(BF16)


def combine_kernel(r2, r3, r1, r0, out):
    out[...] = (
        r0[...] + r1[...].astype(F32) + r2[...].astype(F32) + r3[...].astype(F32)
    ).astype(BF16)


def qkv_kernel(x0, x1, x2, x3, gain_ref, own_ref, par_ref, o0, o1, o2, o3, hold, whole):
    e, m = seq_index(), mp_index()
    width = x0.shape[1]
    half, columns = own_ref.shape
    tok = o0.shape[0]
    for j, part in enumerate((x0, x1, x2, x3)):
        k = m ^ j
        gain = gain_ref[:, pl.ds(chunk_offset(e, k, width), width)]
        at = pl.ds(pl.multiple_of(k * width, width), width)
        whole[:, at] = part[...]
        hold[:, at] = (part[...].astype(F32) * gain).astype(BF16)
    product = jnp.dot(hold[:, :half], own_ref[...], preferred_element_type=F32) + jnp.dot(
        hold[:, half:], par_ref[...], preferred_element_type=F32
    )
    for s, out in enumerate((o0, o1, o2, o3)):
        rows = slice(s * tok, (s + 1) * tok)
        out[:, :columns] = product[rows].astype(BF16)
        out[:, columns:] = whole[rows]


def finish_kernel(y2, y3, y1, y0, qkv_ref, stream_ref):
    e = seq_index()
    tok, columns = qkv_ref.shape
    half = (y0.shape[1] - columns) // 2
    squares = jnp.zeros((tok, half), F32)
    for s, ref in enumerate((y0, y1, y2, y3)):
        for side in range(2):
            block = ref[:, columns + side * half : columns + (side + 1) * half]
            wide = block.astype(F32)
            squares = squares + wide * wide
            at = pl.multiple_of((e ^ (2 * s) ^ side) * half, half)
            stream_ref[:, pl.ds(at, half)] = block
    mean_square = jnp.sum(squares, axis=1, keepdims=True) / stream_ref.shape[1]
    total = (y0[:, :columns].astype(F32) + y1[:, :columns].astype(F32)) + (
        y2[:, :columns].astype(F32) + y3[:, :columns].astype(F32)
    )
    qkv_ref[...] = (total * lax.rsqrt(mean_square + 1e-06)).astype(BF16)


def call(kernel, out_shape, args, scratch=(), flops=0, moved=1 << 20):
    vmem = pl.BlockSpec(memory_space=pltpu.VMEM)
    return pl.pallas_call(
        kernel,
        out_shape=out_shape,
        in_specs=[vmem] * len(args),
        out_specs=jax.tree.map(lambda _: vmem, out_shape),
        scratch_shapes=list(scratch),
        compiler_params=pltpu.CompilerParams(vmem_limit_bytes=24 << 20),
        cost_estimate=pl.CostEstimate(flops=flops, bytes_accessed=moved, transcendentals=0),
    )(*args)


def swap(value, axes, bits):
    count = lax.axis_size(axes)
    return lax.ppermute(value, axes, [(i, i ^ bits) for i in range(count)])


def on_block(
    fresh_queries,
    fresh_keys,
    fresh_values,
    cache,
    pool_root,
    branch_owner,
    branch_len,
    branch_root,
    request_branch,
    token_request,
    residual,
    wo_t,
    norm_gain,
    w_qkv,
):
    tok, wide = fresh_queries.shape
    width = wo_t.shape[0] // 2
    columns = w_qkv.shape[1]
    sds = jax.ShapeDtypeStruct
    mp = ("x", "c")

    along = [cache] + [swap(cache, "z", s) for s in range(1, 4)]
    beside = swap(cache, "y", 1)
    holders = pool_root.shape[0]
    requests, token_branch = token_branches(request_branch, token_request)
    branch_ids = jnp.arange(branch_root.shape[0], dtype=jnp.int32)
    chosen = token_branch[:, None] == branch_ids[None, :]
    token_root, token_owner, token_length = (
        jnp.sum(jnp.where(chosen, per_branch[None, :], 0), axis=1)
        for per_branch in (branch_root, branch_owner, branch_len)
    )
    small = (requests, token_root, token_owner, token_length, pool_root)
    along[1:], small, mine = lax.optimization_barrier(
        (along[1:], small, (fresh_queries, fresh_keys, fresh_values))
    )
    requests, token_root, token_owner, token_length, pool_root = small
    across = [beside] + [swap(rows, "y", 1) for rows in along[1:]]
    blocks = [block for pair in zip(along, across) for block in pair]
    positions = jnp.arange(tok, dtype=jnp.int32)
    own_seen = (requests[None, :] == requests[:, None]) & (
        positions[:, None] <= positions[None, :]
    )
    slot_count = cache.shape[1] - pool_root.shape[1]
    slots = jnp.arange(slot_count, dtype=jnp.int32)
    at = jnp.arange(holders, dtype=jnp.int32)
    root_seen = pool_root[:, :, None] == token_root[None, None, :]
    branch_seen = (token_owner[None, None, :] == at[:, None, None]) & (
        slots[None, :, None] < token_length[None, None, :]
    )
    pool_seen = jnp.concatenate([root_seen, branch_seen], axis=1).reshape(-1, tok)
    seen = jnp.concatenate([own_seen, pool_seen], axis=0)
    bias = jnp.where(jnp.concatenate([seen, seen], axis=1), 0.0, HIDDEN).astype(F32)

    local = jnp.concatenate(mine, axis=1)
    blocks, wo_later = lax.optimization_barrier((blocks, wo_t))
    wo_pair = swap(wo_later, "y", 1)
    attn, *sends = call(
        attend_kernel,
        [sds((tok, wide), BF16)] + [sds((tok, wide + width), BF16)] * 4,
        (local, residual, bias, *blocks),
        flops=1 << 26,
    )
    a2, a3, a1 = (swap(sends[s], "z", s) for s in (2, 3, 1))
    sums = call(
        project_kernel,
        [sds((4 * tok, width), F32)] + [sds((4 * tok, width), BF16)] * 3,
        (a2, a3, a1, sends[0], wo_t, wo_pair),
        scratch=[pltpu.VMEM((4 * tok, 4 * width), F32)],
        flops=1 << 27,
    )
    own_sum, wq_later = lax.optimization_barrier((sums[0], w_qkv))
    wq_pair = swap(wq_later, "y", 1)
    sums = [own_sum] + [swap(sums[j], mp, j) for j in range(1, 4)]
    made = call(
        combine_kernel,
        sds((4 * tok, width), BF16),
        (sums[2], sums[3], sums[1], sums[0]),
    )
    slices = [made] + [swap(made, mp, j) for j in range(1, 4)]
    partial = call(
        qkv_kernel,
        [sds((tok, columns + 4 * width), BF16)] * 4,
        (*slices, norm_gain[None, :], w_qkv, wq_pair),
        scratch=[
            pltpu.VMEM((4 * tok, 4 * width), BF16),
            pltpu.VMEM((4 * tok, 4 * width), BF16),
        ],
        flops=1 << 28,
    )
    y2, y3, y1 = (swap(partial[s], "z", s) for s in (2, 3, 1))
    qkv_next, stream = call(
        finish_kernel,
        [sds((tok, columns), BF16), sds(residual.shape, BF16)],
        (y2, y3, y1, partial[0]),
    )
    return attn, stream, qkv_next


def absorb(running, query_rows, key_row_block, value_rows, visible, score_scale):
    peak_old, total, mixed = running
    scores = (
        jnp.einsum("tkgd,rkd->tkgr", query_rows, key_row_block, preferred_element_type=jnp.float32)
        * score_scale
    )
    seen = visible[:, None, None, :]
    peak_new = jnp.maximum(peak_old, jnp.max(jnp.where(seen, scores, -jnp.inf), axis=-1))
    factor = jnp.exp(peak_old - peak_new)
    weights_full = jnp.where(seen, jnp.exp(scores - peak_new[..., None]), 0.0)
    total = total * factor + jnp.sum(weights_full, axis=-1)
    mixed = mixed * factor[..., None] + jnp.einsum(
        "tkgr,rkd->tkgd",
        weights_full.astype(jnp.bfloat16),
        value_rows,
        preferred_element_type=jnp.float32,
    )
    return (peak_new, total, mixed)


def on_device(
    fresh_queries,
    fresh_keys,
    fresh_values,
    cache,
    pool_root,
    branch_owner,
    branch_len,
    branch_root,
    request_branch,
    token_request,
    residual,
    wo_t,
    norm_gain,
    w_qkv,
):
    seq_count = lax.axis_size("seq")
    root_count = seq_count // 4
    tok_rows = fresh_queries.shape[0]
    kv_local = fresh_keys.shape[1] // HEAD_SIZE
    query_groups = QUERY_HEADS // KEY_VALUE_HEADS
    score_scale = HEAD_SIZE ** (-0.5)
    slot_count = cache.shape[1] - pool_root.shape[1]
    owner_ids = jnp.arange(seq_count, dtype=jnp.int32)
    tags = cache_tags(pool_root, branch_owner, branch_len, root_count, slot_count, owner_ids)
    requests, token_branch = token_branches(request_branch, token_request)
    branch_ids = jnp.arange(branch_root.shape[0], dtype=jnp.int32)
    token_root = jnp.sum(
        jnp.where(token_branch[:, None] == branch_ids[None, :], branch_root[None, :], 0), axis=1
    )
    query_rows = fresh_queries.reshape(tok_rows, kv_local, query_groups, HEAD_SIZE)
    incoming_keys = fresh_keys.reshape(tok_rows, kv_local, HEAD_SIZE)
    incoming_values = fresh_values.reshape(tok_rows, kv_local, HEAD_SIZE)
    positions = jnp.arange(tok_rows, dtype=jnp.int32)
    own_visible = (requests[None, :] == requests[:, None]) & (
        positions[None, :] <= positions[:, None]
    )
    start_state = (
        jnp.full((tok_rows, kv_local, query_groups), -jnp.inf, jnp.float32),
        jnp.zeros((tok_rows, kv_local, query_groups), jnp.float32),
        jnp.zeros((tok_rows, kv_local, query_groups, HEAD_SIZE), jnp.float32),
    )
    state = absorb(
        start_state, query_rows, incoming_keys, incoming_values, own_visible, score_scale
    )
    piece = lax.all_gather(cache, "seq", axis=1, tiled=True)
    rows = piece.shape[1]
    block = 512 if rows > 512 and rows % 512 == 0 else rows
    key_blocks = piece[0].reshape(rows // block, block, kv_local, HEAD_SIZE)
    value_blocks = piece[1].reshape(rows // block, block, kv_local, HEAD_SIZE)
    tag_blocks = tags.reshape(rows // block, block)

    def one_block(running, parts):
        key_row_block, value_rows, tag_rows = parts
        visible = (tag_rows[None, :] == token_root[:, None]) | (
            tag_rows[None, :] == root_count + token_branch[:, None]
        )
        updated = absorb(running, query_rows, key_row_block, value_rows, visible, score_scale)
        return (updated, None)

    state, unused = lax.scan(one_block, state, (key_blocks, value_blocks, tag_blocks))
    peak_final, total_final, mixed_final = state
    attn = (
        (mixed_final / total_final[..., None])
        .reshape(tok_rows, kv_local * query_groups * HEAD_SIZE)
        .astype(jnp.bfloat16)
    )
    partial_value = lax.dot_general(
        attn,
        lax.all_gather(wo_t, "seq", axis=0, tiled=True),
        (((1,), (1,)), ((), ())),
        preferred_element_type=jnp.float32,
    )
    summed = lax.psum(partial_value.astype(jnp.bfloat16), "mp").astype(jnp.float32)
    stream = (residual.astype(jnp.float32) + summed).astype(jnp.bfloat16)
    widened = stream.astype(jnp.float32)
    mean_square = jnp.mean(widened * widened, axis=-1, keepdims=True)
    normed = (widened * lax.rsqrt(mean_square + 1e-06) * norm_gain[None, :]).astype(jnp.bfloat16)
    qkv_sum = jnp.dot(
        normed, lax.all_gather(w_qkv, "seq", axis=0, tiled=True), preferred_element_type=jnp.float32
    )
    return (attn, stream, qkv_sum.astype(jnp.bfloat16))


def solution(mesh):
    small = mesh.shape["seq"] == 8 and mesh.shape["mp"] == 4
    seq, mp = "seq", "mp"
    if small:
        mesh = Mesh(mesh.devices.reshape(4, 2, 2, 2), ("z", "y", "x", "c"))
        seq, mp = ("z", "y"), ("x", "c")
    return jax.shard_map(
        on_block if small else on_device,
        mesh=mesh,
        in_specs=(
            P(seq, mp),
            P(seq, mp),
            P(seq, mp),
            P(None, seq, mp),
            P(),
            P(),
            P(),
            P(),
            P(seq, None),
            P(seq, None),
            P(seq, None),
            P(seq, mp),
            P(),
            P(seq, mp),
        ),
        out_specs=(P(seq, mp), P(seq, None), P(seq, mp)),
        check_vma=False,
    )
```

```python
import jax
import jax.numpy as jnp
from jax import lax
from jax.experimental import pallas as pl
from jax.experimental.pallas import tpu as pltpu
from jax.sharding import Mesh
from jax.sharding import PartitionSpec as P

QUERY_HEADS = 16
KEY_VALUE_HEADS = 8
HEAD_SIZE = 128
NT = (((1,), (1,)), ((), ()))
TN = (((0,), (0,)), ((), ()))
F32 = jnp.float32
HIDDEN = -1e30
BF16 = jnp.bfloat16


def cache_tags(pool_root, branch_owner, branch_len, root_count, slot_count, owner_ids):
    branch_count = branch_owner.shape[0]
    branch_ids = jnp.arange(branch_count, dtype=jnp.int32)
    owned = jnp.sum(
        jnp.where(branch_owner[None, :] == owner_ids[:, None], branch_ids[None, :], 0), axis=1
    )
    owned_length = jnp.sum(
        jnp.where(branch_ids[None, :] == owned[:, None], branch_len[None, :], 0), axis=1
    )
    slot_ids = jnp.arange(slot_count, dtype=jnp.int32)
    branch_tags = jnp.where(
        slot_ids[None, :] < owned_length[:, None], root_count + owned[:, None], -1
    )
    return jnp.concatenate([pool_root, branch_tags], axis=1).reshape(-1)


def token_branches(request_branch, token_request):
    requests = token_request[0]
    local_branches = request_branch[0]
    request_ids = jnp.arange(local_branches.shape[0], dtype=jnp.int32)
    token_branch = jnp.sum(
        jnp.where(requests[:, None] == request_ids[None, :], local_branches[None, :], 0), axis=1
    )
    return requests, token_branch


def head_lanes(h):
    return slice(h * HEAD_SIZE, (h + 1) * HEAD_SIZE)


def seq_index():
    return 2 * lax.axis_index("z") + lax.axis_index("y")


def chunk_offset(e, k, width):
    return pl.multiple_of((e ^ (k // 2)) * (2 * width) + (k % 2) * width, width)


def mp_index():
    return 2 * lax.axis_index("x") + lax.axis_index("c")


def attend_kernel(local_ref, res_ref, bias_ref, *refs):
    caches, out_ref, sends = refs[:-5], refs[-5], refs[-4:]
    e, m = seq_index(), mp_index()
    tok, wide = out_ref.shape
    kv = caches[0].shape[2]
    q_ref, kf_ref, vf_ref = (
        local_ref.at[:, :wide],
        local_ref.at[:, wide : wide + kv],
        local_ref.at[:, wide + kv :],
    )
    rows = caches[0].shape[1]
    bias = jnp.concatenate(
        [bias_ref[:tok]]
        + [
            bias_ref[pl.ds(pl.multiple_of(tok + (e ^ s) * rows, rows), rows), :]
            for s in range(len(caches))
        ],
        axis=0,
    )
    for k in range(kf_ref.shape[1] // HEAD_SIZE):
        lanes, first, second = head_lanes(k), head_lanes(2 * k), head_lanes(2 * k + 1)
        keys = jnp.concatenate([kf_ref[:, lanes]] + [c[0, :, lanes] for c in caches], axis=0)
        values = jnp.concatenate([vf_ref[:, lanes]] + [c[1, :, lanes] for c in caches], axis=0)
        queries = jnp.concatenate([q_ref[:, first], q_ref[:, second]], axis=0)
        scores = (
            lax.dot_general(keys, queries, NT, preferred_element_type=F32) * HEAD_SIZE**-0.5 + bias
        )
        peak = jnp.max(scores, axis=0, keepdims=True)
        prob = jnp.exp(scores - peak)
        total = jnp.sum(prob, axis=0, keepdims=True)
        mixed = lax.dot_general(values, prob.astype(BF16), TN, preferred_element_type=F32)
        attn = (mixed / total).T.astype(BF16)
        for ref in (out_ref, *sends):
            ref[:, first] = attn[:tok]
            ref[:, second] = attn[tok:]
    width = sends[0].shape[1] - wide
    for s, ref in enumerate(sends):
        ref[:, wide:] = res_ref[:, pl.ds(chunk_offset(e ^ (2 * s), m, width), width)]


def project_kernel(a2, a3, a1, a0, own_ref, par_ref, o0, o1, o2, o3, hold):
    m = mp_index()
    half, wide = own_ref.shape
    blocks = (a0, a1, a2, a3)
    attn = jnp.concatenate([a[:, :wide] for a in blocks], axis=0)
    rest = jnp.concatenate([a[:, wide:] for a in blocks], axis=0)
    hold[:, :half] = lax.dot_general(attn, own_ref[...], NT, preferred_element_type=F32)
    hold[:, half:] = lax.dot_general(attn, par_ref[...], NT, preferred_element_type=F32)
    width = o0.shape[1]
    for j, out in enumerate((o0, o1, o2, o3)):
        chunk = hold[:, pl.ds(pl.multiple_of((m ^ j) * width, width), width)]
        out[...] = chunk + rest.astype(F32) if j == 0 else chunk.astype(BF16)


def combine_kernel(r2, r3, r1, r0, out, t0, t1, t2, t3):
    tok = t0.shape[0]
    stream = (
        r0[...] + r1[...].astype(F32) + r2[...].astype(F32) + r3[...].astype(F32)
    ).astype(BF16)
    out[...] = stream
    for s, part in enumerate((t0, t1, t2, t3)):
        part[...] = stream[s * tok : (s + 1) * tok]


def qkv_kernel(x0, x1, x2, x3, gain_ref, own_ref, par_ref, o0, o1, o2, o3, hold):
    e, m = seq_index(), mp_index()
    width = x0.shape[1]
    half = 2 * width
    tok = o0.shape[0]
    for j, part in enumerate((x0, x1, x2, x3)):
        k = m ^ j
        gain = gain_ref[:, pl.ds(chunk_offset(e, k, width), width)]
        hold[:, pl.ds(pl.multiple_of(k * width, width), width)] = (
            part[...].astype(F32) * gain
        ).astype(BF16)
    product = jnp.dot(hold[:, :half], own_ref[...], preferred_element_type=F32) + jnp.dot(
        hold[:, half:], par_ref[...], preferred_element_type=F32
    )
    for s, out in enumerate((o0, o1, o2, o3)):
        out[...] = product[s * tok : (s + 1) * tok].astype(out.dtype)


def pack_kernel(t0, t1, t2, t3, out_ref):
    width = t0.shape[1]
    for s, part in enumerate((t0, t1, t2, t3)):
        out_ref[:, s * width : (s + 1) * width] = part[...]


def finish_kernel(p0, p1, p2, p3, y2, y3, y1, y0, qkv_ref, stream_ref):
    e, m = seq_index(), mp_index()
    width = p0.shape[1] // 4
    squares = jnp.zeros((p0.shape[0], width), F32)
    for j, part in enumerate((p0, p1, p2, p3)):
        for s in range(4):
            block = part[:, s * width : (s + 1) * width]
            wide = block.astype(F32)
            squares = squares + wide * wide
            stream_ref[:, pl.ds(chunk_offset(e ^ (2 * s), m ^ j, width), width)] = block
    mean_square = jnp.sum(squares, axis=1, keepdims=True) / stream_ref.shape[1]
    total = y0[...] + y1[...].astype(F32) + y2[...].astype(F32) + y3[...].astype(F32)
    qkv_ref[...] = (total * lax.rsqrt(mean_square + 1e-06)).astype(BF16)


def call(kernel, out_shape, args, scratch=(), flops=0, moved=1 << 20):
    vmem = pl.BlockSpec(memory_space=pltpu.VMEM)
    return pl.pallas_call(
        kernel,
        out_shape=out_shape,
        in_specs=[vmem] * len(args),
        out_specs=jax.tree.map(lambda _: vmem, out_shape),
        scratch_shapes=list(scratch),
        compiler_params=pltpu.CompilerParams(vmem_limit_bytes=24 << 20),
        cost_estimate=pl.CostEstimate(flops=flops, bytes_accessed=moved, transcendentals=0),
    )(*args)


def swap(value, axes, bits):
    count = lax.axis_size(axes)
    return lax.ppermute(value, axes, [(i, i ^ bits) for i in range(count)])


def on_block(
    fresh_queries,
    fresh_keys,
    fresh_values,
    cache,
    pool_root,
    branch_owner,
    branch_len,
    branch_root,
    request_branch,
    token_request,
    residual,
    wo_t,
    norm_gain,
    w_qkv,
):
    tok, wide = fresh_queries.shape
    width = wo_t.shape[0] // 2
    columns = w_qkv.shape[1]
    sds = jax.ShapeDtypeStruct
    mp = ("x", "c")

    wo_pair = swap(wo_t, "y", 1)
    small = (pool_root, branch_owner, branch_len, branch_root, request_branch, token_request)
    wo_pair, small = lax.optimization_barrier((wo_pair, small))
    pool_root, branch_owner, branch_len, branch_root, request_branch, token_request = small
    along = [cache] + [swap(cache, "z", s) for s in range(1, 4)]
    beside = swap(cache, "y", 1)

    holders = pool_root.shape[0]
    requests, token_branch = token_branches(request_branch, token_request)
    branch_ids = jnp.arange(branch_root.shape[0], dtype=jnp.int32)
    chosen = token_branch[:, None] == branch_ids[None, :]
    token_root, token_owner, token_length = (
        jnp.sum(jnp.where(chosen, per_branch[None, :], 0), axis=1)
        for per_branch in (branch_root, branch_owner, branch_len)
    )
    positions = jnp.arange(tok, dtype=jnp.int32)
    own_seen = (requests[None, :] == requests[:, None]) & (
        positions[:, None] <= positions[None, :]
    )
    slot_count = cache.shape[1] - pool_root.shape[1]
    slots = jnp.arange(slot_count, dtype=jnp.int32)
    at = jnp.arange(holders, dtype=jnp.int32)
    root_seen = pool_root[:, :, None] == token_root[None, None, :]
    branch_seen = (token_owner[None, None, :] == at[:, None, None]) & (
        slots[None, :, None] < token_length[None, None, :]
    )
    pool_seen = jnp.concatenate([root_seen, branch_seen], axis=1).reshape(-1, tok)
    seen = jnp.concatenate([own_seen, pool_seen], axis=0)
    bias = jnp.where(jnp.concatenate([seen, seen], axis=1), 0.0, HIDDEN).astype(F32)

    local = jnp.concatenate([fresh_queries, fresh_keys, fresh_values], axis=1)
    along[1:], bias, local = lax.optimization_barrier((along[1:], bias, local))
    across = [beside] + [swap(mine, "y", 1) for mine in along[1:]]
    blocks = [block for pair in zip(along, across) for block in pair]
    blocks, wq_later = lax.optimization_barrier((blocks, w_qkv))
    wq_pair = swap(wq_later, "y", 1)
    attn, *sends = call(
        attend_kernel,
        [sds((tok, wide), BF16)] + [sds((tok, wide + width), BF16)] * 4,
        (local, residual, bias, *blocks),
        flops=1 << 26,
    )
    a2, a3, a1 = (swap(sends[s], "z", s) for s in (2, 3, 1))
    sums = call(
        project_kernel,
        [sds((4 * tok, width), F32)] + [sds((4 * tok, width), BF16)] * 3,
        (a2, a3, a1, sends[0], wo_t, wo_pair),
        scratch=[pltpu.VMEM((4 * tok, 4 * width), F32)],
        flops=1 << 27,
    )
    sums = [sums[0]] + [swap(sums[j], mp, j) for j in range(1, 4)]
    made = call(
        combine_kernel,
        [sds((4 * tok, width), BF16)] + [sds((tok, width), BF16)] * 4,
        (sums[2], sums[3], sums[1], sums[0]),
    )
    made, wq_pair = lax.optimization_barrier((made, wq_pair))
    slices = [made[0]] + [swap(made[0], mp, j) for j in range(1, 4)]
    slices, made = lax.optimization_barrier((slices, made))
    home = [made[1]] + [swap(made[1 + s], "z", s) for s in range(1, 4)]
    partial = call(
        qkv_kernel,
        [sds((tok, columns), F32)] + [sds((tok, columns), BF16)] * 3,
        (*slices, norm_gain[None, :], w_qkv, wq_pair),
        scratch=[pltpu.VMEM((4 * tok, 4 * width), BF16)],
        flops=1 << 28,
    )
    y1, y2, y3 = (swap(partial[s], "z", s) for s in (1, 2, 3))
    home, own_partial = lax.optimization_barrier((home, partial[0]))
    packed = call(pack_kernel, sds((tok, 4 * width), BF16), tuple(home))
    pieces = [packed] + [swap(packed, mp, j) for j in range(1, 4)]
    qkv_next, stream = call(
        finish_kernel,
        [sds((tok, columns), BF16), sds(residual.shape, BF16)],
        (*pieces, y2, y3, y1, own_partial),
    )
    return attn, stream, qkv_next


def absorb(running, query_rows, key_row_block, value_rows, visible, score_scale):
    peak_old, total, mixed = running
    scores = (
        jnp.einsum("tkgd,rkd->tkgr", query_rows, key_row_block, preferred_element_type=jnp.float32)
        * score_scale
    )
    seen = visible[:, None, None, :]
    peak_new = jnp.maximum(peak_old, jnp.max(jnp.where(seen, scores, -jnp.inf), axis=-1))
    factor = jnp.exp(peak_old - peak_new)
    weights_full = jnp.where(seen, jnp.exp(scores - peak_new[..., None]), 0.0)
    total = total * factor + jnp.sum(weights_full, axis=-1)
    mixed = mixed * factor[..., None] + jnp.einsum(
        "tkgr,rkd->tkgd",
        weights_full.astype(jnp.bfloat16),
        value_rows,
        preferred_element_type=jnp.float32,
    )
    return (peak_new, total, mixed)


def on_device(
    fresh_queries,
    fresh_keys,
    fresh_values,
    cache,
    pool_root,
    branch_owner,
    branch_len,
    branch_root,
    request_branch,
    token_request,
    residual,
    wo_t,
    norm_gain,
    w_qkv,
):
    seq_count = lax.axis_size("seq")
    root_count = seq_count // 4
    tok_rows = fresh_queries.shape[0]
    kv_local = fresh_keys.shape[1] // HEAD_SIZE
    query_groups = QUERY_HEADS // KEY_VALUE_HEADS
    score_scale = HEAD_SIZE ** (-0.5)
    slot_count = cache.shape[1] - pool_root.shape[1]
    owner_ids = jnp.arange(seq_count, dtype=jnp.int32)
    tags = cache_tags(pool_root, branch_owner, branch_len, root_count, slot_count, owner_ids)
    requests, token_branch = token_branches(request_branch, token_request)
    branch_ids = jnp.arange(branch_root.shape[0], dtype=jnp.int32)
    token_root = jnp.sum(
        jnp.where(token_branch[:, None] == branch_ids[None, :], branch_root[None, :], 0), axis=1
    )
    query_rows = fresh_queries.reshape(tok_rows, kv_local, query_groups, HEAD_SIZE)
    incoming_keys = fresh_keys.reshape(tok_rows, kv_local, HEAD_SIZE)
    incoming_values = fresh_values.reshape(tok_rows, kv_local, HEAD_SIZE)
    positions = jnp.arange(tok_rows, dtype=jnp.int32)
    own_visible = (requests[None, :] == requests[:, None]) & (
        positions[None, :] <= positions[:, None]
    )
    start_state = (
        jnp.full((tok_rows, kv_local, query_groups), -jnp.inf, jnp.float32),
        jnp.zeros((tok_rows, kv_local, query_groups), jnp.float32),
        jnp.zeros((tok_rows, kv_local, query_groups, HEAD_SIZE), jnp.float32),
    )
    state = absorb(
        start_state, query_rows, incoming_keys, incoming_values, own_visible, score_scale
    )
    piece = lax.all_gather(cache, "seq", axis=1, tiled=True)
    rows = piece.shape[1]
    block = 512 if rows > 512 and rows % 512 == 0 else rows
    key_blocks = piece[0].reshape(rows // block, block, kv_local, HEAD_SIZE)
    value_blocks = piece[1].reshape(rows // block, block, kv_local, HEAD_SIZE)
    tag_blocks = tags.reshape(rows // block, block)

    def one_block(running, parts):
        key_row_block, value_rows, tag_rows = parts
        visible = (tag_rows[None, :] == token_root[:, None]) | (
            tag_rows[None, :] == root_count + token_branch[:, None]
        )
        updated = absorb(running, query_rows, key_row_block, value_rows, visible, score_scale)
        return (updated, None)

    state, unused = lax.scan(one_block, state, (key_blocks, value_blocks, tag_blocks))
    peak_final, total_final, mixed_final = state
    attn = (
        (mixed_final / total_final[..., None])
        .reshape(tok_rows, kv_local * query_groups * HEAD_SIZE)
        .astype(jnp.bfloat16)
    )
    partial_value = lax.dot_general(
        attn,
        lax.all_gather(wo_t, "seq", axis=0, tiled=True),
        (((1,), (1,)), ((), ())),
        preferred_element_type=jnp.float32,
    )
    summed = lax.psum(partial_value.astype(jnp.bfloat16), "mp").astype(jnp.float32)
    stream = (residual.astype(jnp.float32) + summed).astype(jnp.bfloat16)
    widened = stream.astype(jnp.float32)
    mean_square = jnp.mean(widened * widened, axis=-1, keepdims=True)
    normed = (widened * lax.rsqrt(mean_square + 1e-06) * norm_gain[None, :]).astype(jnp.bfloat16)
    qkv_sum = jnp.dot(
        normed, lax.all_gather(w_qkv, "seq", axis=0, tiled=True), preferred_element_type=jnp.float32
    )
    return (attn, stream, qkv_sum.astype(jnp.bfloat16))


def solution(mesh):
    small = mesh.shape["seq"] == 8 and mesh.shape["mp"] == 4
    seq, mp = "seq", "mp"
    if small:
        mesh = Mesh(mesh.devices.reshape(4, 2, 2, 2), ("z", "y", "x", "c"))
        seq, mp = ("z", "y"), ("x", "c")
    return jax.shard_map(
        on_block if small else on_device,
        mesh=mesh,
        in_specs=(
            P(seq, mp),
            P(seq, mp),
            P(seq, mp),
            P(None, seq, mp),
            P(),
            P(),
            P(),
            P(),
            P(seq, None),
            P(seq, None),
            P(seq, None),
            P(seq, mp),
            P(),
            P(seq, mp),
        ),
        out_specs=(P(seq, mp), P(seq, None), P(seq, mp)),
        check_vma=False,
    )
```

```python
import jax
import jax.numpy as jnp
from jax import lax
from jax.experimental import pallas as pl
from jax.experimental.pallas import tpu as pltpu
from jax.sharding import Mesh
from jax.sharding import PartitionSpec as P

QUERY_HEADS = 16
KEY_VALUE_HEADS = 8
HEAD_SIZE = 128
NT = (((1,), (1,)), ((), ()))
TN = (((0,), (0,)), ((), ()))
F32 = jnp.float32
HIDDEN = -1e30
BF16 = jnp.bfloat16


def cache_tags(pool_root, branch_owner, branch_len, root_count, slot_count, owner_ids):
    branch_count = branch_owner.shape[0]
    branch_ids = jnp.arange(branch_count, dtype=jnp.int32)
    owned = jnp.sum(
        jnp.where(branch_owner[None, :] == owner_ids[:, None], branch_ids[None, :], 0), axis=1
    )
    owned_length = jnp.sum(
        jnp.where(branch_ids[None, :] == owned[:, None], branch_len[None, :], 0), axis=1
    )
    slot_ids = jnp.arange(slot_count, dtype=jnp.int32)
    branch_tags = jnp.where(
        slot_ids[None, :] < owned_length[:, None], root_count + owned[:, None], -1
    )
    return jnp.concatenate([pool_root, branch_tags], axis=1).reshape(-1)


def token_branches(request_branch, token_request):
    requests = token_request[0]
    local_branches = request_branch[0]
    request_ids = jnp.arange(local_branches.shape[0], dtype=jnp.int32)
    token_branch = jnp.sum(
        jnp.where(requests[:, None] == request_ids[None, :], local_branches[None, :], 0), axis=1
    )
    return requests, token_branch


def head_lanes(h):
    return slice(h * HEAD_SIZE, (h + 1) * HEAD_SIZE)


def seq_index():
    return 2 * lax.axis_index("z") + lax.axis_index("y")


def chunk_offset(e, k, width):
    return pl.multiple_of((e ^ (k // 2)) * (2 * width) + (k % 2) * width, width)


def mp_index():
    return 2 * lax.axis_index("x") + lax.axis_index("c")


def attend_kernel(local_ref, res_ref, bias_ref, *refs):
    caches, out_ref, sends = refs[:-5], refs[-5], refs[-4:]
    e, m = seq_index(), mp_index()
    tok, wide = out_ref.shape
    kv = caches[0].shape[2]
    q_ref, kf_ref, vf_ref = (
        local_ref.at[:, :wide],
        local_ref.at[:, wide : wide + kv],
        local_ref.at[:, wide + kv :],
    )
    rows = caches[0].shape[1]
    bias = jnp.concatenate(
        [bias_ref[:tok]]
        + [
            bias_ref[pl.ds(pl.multiple_of(tok + (e ^ s) * rows, rows), rows), :]
            for s in range(len(caches))
        ],
        axis=0,
    )
    for k in range(kf_ref.shape[1] // HEAD_SIZE):
        lanes, first, second = head_lanes(k), head_lanes(2 * k), head_lanes(2 * k + 1)
        keys = jnp.concatenate([kf_ref[:, lanes]] + [c[0, :, lanes] for c in caches], axis=0)
        values = jnp.concatenate([vf_ref[:, lanes]] + [c[1, :, lanes] for c in caches], axis=0)
        queries = jnp.concatenate([q_ref[:, first], q_ref[:, second]], axis=0)
        scores = (
            lax.dot_general(keys, queries, NT, preferred_element_type=F32) * HEAD_SIZE**-0.5 + bias
        )
        peak = jnp.max(scores, axis=0, keepdims=True)
        prob = jnp.exp(scores - peak)
        total = jnp.sum(prob, axis=0, keepdims=True)
        mixed = lax.dot_general(values, prob.astype(BF16), TN, preferred_element_type=F32)
        attn = (mixed / total).T.astype(BF16)
        for ref in (out_ref, *sends):
            ref[:, first] = attn[:tok]
            ref[:, second] = attn[tok:]
    width = sends[0].shape[1] - wide
    for s, ref in enumerate(sends):
        ref[:, wide:] = res_ref[:, pl.ds(chunk_offset(e ^ (2 * s), m, width), width)]


def project_kernel(a2, a3, a1, a0, own_ref, par_ref, o0, o1, o2, o3, hold):
    m = mp_index()
    half, wide = own_ref.shape
    blocks = (a0, a1, a2, a3)
    attn = jnp.concatenate([a[:, :wide] for a in blocks], axis=0)
    rest = jnp.concatenate([a[:, wide:] for a in blocks], axis=0)
    hold[:, :half] = lax.dot_general(attn, own_ref[...], NT, preferred_element_type=F32)
    hold[:, half:] = lax.dot_general(attn, par_ref[...], NT, preferred_element_type=F32)
    width = o0.shape[1]
    for j, out in enumerate((o0, o1, o2, o3)):
        chunk = hold[:, pl.ds(pl.multiple_of((m ^ j) * width, width), width)]
        out[...] = chunk + rest.astype(F32) if j == 0 else chunk.astype(BF16)


def combine_kernel(r2, r3, r1, r0, out, t2, t3):
    tok = t2.shape[0]
    stream = (
        r0[...] + r1[...].astype(F32) + r2[...].astype(F32) + r3[...].astype(F32)
    ).astype(BF16)
    out[...] = stream
    t2[...] = stream[2 * tok : 3 * tok]
    t3[...] = stream[3 * tok :]


def qkv_kernel(x0, x1, x2, x3, gain_ref, own_ref, par_ref, t3, t2, o0, o1, o2, o3, near, packed, hold):
    e, m = seq_index(), mp_index()
    width = x0.shape[1]
    half, columns = own_ref.shape
    tok = o0.shape[0]
    for j, part in enumerate((x0, x1, x2, x3)):
        k = m ^ j
        gain = gain_ref[:, pl.ds(chunk_offset(e, k, width), width)]
        at = pl.multiple_of(k * width, width)
        hold[:, pl.ds(at, width)] = (part[...].astype(F32) * gain).astype(BF16)
        near[:, pl.ds(at, width)] = part[:tok]
        o1[:, pl.ds(pl.multiple_of(columns + at, width), width)] = part[tok : 2 * tok]
    packed[:, :width] = t2[...]
    packed[:, width:] = t3[...]
    product = jnp.dot(hold[:, :half], own_ref[...], preferred_element_type=F32) + jnp.dot(
        hold[:, half:], par_ref[...], preferred_element_type=F32
    )
    for s, out in enumerate((o0, o1, o2, o3)):
        out[:, :columns] = product[s * tok : (s + 1) * tok].astype(out.dtype)


def finish_kernel(p0, p1, p2, p3, y2, y3, y1, y0, near, qkv_ref, stream_ref):
    e, m = seq_index(), mp_index()
    tok, columns = qkv_ref.shape
    width = p0.shape[1] // 2
    squares = jnp.zeros((tok, width), F32)
    blocks = []
    for k in range(4):
        lanes = slice(k * width, (k + 1) * width)
        blocks.append((chunk_offset(e, k, width), near[:, lanes]))
        lanes = slice(columns + k * width, columns + (k + 1) * width)
        blocks.append((chunk_offset(e ^ 2, k, width), y1[:, lanes]))
    for j, part in enumerate((p0, p1, p2, p3)):
        for i, s in enumerate((2, 3)):
            lanes = slice(i * width, (i + 1) * width)
            blocks.append((chunk_offset(e ^ (2 * s), m ^ j, width), part[:, lanes]))
    for at, block in blocks:
        wide = block.astype(F32)
        squares = squares + wide * wide
        stream_ref[:, pl.ds(at, width)] = block
    mean_square = jnp.sum(squares, axis=1, keepdims=True) / stream_ref.shape[1]
    total = (
        y0[...] + y1[:, :columns].astype(F32) + y2[...].astype(F32) + y3[...].astype(F32)
    )
    qkv_ref[...] = (total * lax.rsqrt(mean_square + 1e-06)).astype(BF16)


def call(kernel, out_shape, args, scratch=(), flops=0, moved=1 << 20):
    vmem = pl.BlockSpec(memory_space=pltpu.VMEM)
    return pl.pallas_call(
        kernel,
        out_shape=out_shape,
        in_specs=[vmem] * len(args),
        out_specs=jax.tree.map(lambda _: vmem, out_shape),
        scratch_shapes=list(scratch),
        compiler_params=pltpu.CompilerParams(vmem_limit_bytes=24 << 20),
        cost_estimate=pl.CostEstimate(flops=flops, bytes_accessed=moved, transcendentals=0),
    )(*args)


def swap(value, axes, bits):
    count = lax.axis_size(axes)
    return lax.ppermute(value, axes, [(i, i ^ bits) for i in range(count)])


def on_block(
    fresh_queries,
    fresh_keys,
    fresh_values,
    cache,
    pool_root,
    branch_owner,
    branch_len,
    branch_root,
    request_branch,
    token_request,
    residual,
    wo_t,
    norm_gain,
    w_qkv,
):
    tok, wide = fresh_queries.shape
    width = wo_t.shape[0] // 2
    columns = w_qkv.shape[1]
    sds = jax.ShapeDtypeStruct
    mp = ("x", "c")

    along = [cache] + [swap(cache, "z", s) for s in range(1, 4)]
    beside = swap(cache, "y", 1)

    holders = pool_root.shape[0]
    requests, token_branch = token_branches(request_branch, token_request)
    branch_ids = jnp.arange(branch_root.shape[0], dtype=jnp.int32)
    chosen = token_branch[:, None] == branch_ids[None, :]
    token_root, token_owner, token_length = (
        jnp.sum(jnp.where(chosen, per_branch[None, :], 0), axis=1)
        for per_branch in (branch_root, branch_owner, branch_len)
    )
    positions = jnp.arange(tok, dtype=jnp.int32)
    own_seen = (requests[None, :] == requests[:, None]) & (
        positions[:, None] <= positions[None, :]
    )
    slot_count = cache.shape[1] - pool_root.shape[1]
    slots = jnp.arange(slot_count, dtype=jnp.int32)
    at = jnp.arange(holders, dtype=jnp.int32)
    root_seen = pool_root[:, :, None] == token_root[None, None, :]
    branch_seen = (token_owner[None, None, :] == at[:, None, None]) & (
        slots[None, :, None] < token_length[None, None, :]
    )
    pool_seen = jnp.concatenate([root_seen, branch_seen], axis=1).reshape(-1, tok)
    seen = jnp.concatenate([own_seen, pool_seen], axis=0)
    bias = jnp.where(jnp.concatenate([seen, seen], axis=1), 0.0, HIDDEN).astype(F32)

    mine = (fresh_queries, fresh_keys, fresh_values)
    wo_pair, mine = lax.optimization_barrier((swap(wo_t, "y", 1), mine))
    local = jnp.concatenate(mine, axis=1)
    along[1:], bias, local = lax.optimization_barrier((along[1:], bias, local))
    across = [beside] + [swap(mine, "y", 1) for mine in along[1:]]
    blocks = [block for pair in zip(along, across) for block in pair]
    blocks, wq_later = lax.optimization_barrier((blocks, w_qkv))
    wq_pair = swap(wq_later, "y", 1)
    attn, *sends = call(
        attend_kernel,
        [sds((tok, wide), BF16)] + [sds((tok, wide + width), BF16)] * 4,
        (local, residual, bias, *blocks),
        flops=1 << 26,
    )
    a2, a3, a1 = (swap(sends[s], "z", s) for s in (2, 3, 1))
    sums = call(
        project_kernel,
        [sds((4 * tok, width), F32)] + [sds((4 * tok, width), BF16)] * 3,
        (a2, a3, a1, sends[0], wo_t, wo_pair),
        scratch=[pltpu.VMEM((4 * tok, 4 * width), F32)],
        flops=1 << 27,
    )
    sums = [sums[0]] + [swap(sums[j], mp, j) for j in range(1, 4)]
    made = call(
        combine_kernel,
        [sds((4 * tok, width), BF16)] + [sds((tok, width), BF16)] * 2,
        (sums[2], sums[3], sums[1], sums[0]),
    )
    made, wq_pair = lax.optimization_barrier((made, wq_pair))
    slices = [made[0]] + [swap(made[0], mp, j) for j in range(1, 4)]
    home = [swap(made[2], "z", 3), swap(made[1], "z", 2)]
    partial = call(
        qkv_kernel,
        [
            sds((tok, columns), F32),
            sds((tok, columns + 4 * width), BF16),
            sds((tok, columns), BF16),
            sds((tok, columns), BF16),
            sds((tok, 4 * width), BF16),
            sds((tok, 2 * width), BF16),
        ],
        (*slices, norm_gain[None, :], w_qkv, wq_pair, *home),
        scratch=[pltpu.VMEM((4 * tok, 4 * width), BF16)],
        flops=1 << 28,
    )
    y1, y2, y3 = (swap(partial[s], "z", s) for s in (1, 2, 3))
    packed = partial[5]
    pieces = [packed] + [swap(packed, mp, j) for j in range(1, 4)]
    qkv_next, stream = call(
        finish_kernel,
        [sds((tok, columns), BF16), sds(residual.shape, BF16)],
        (*pieces, y2, y3, y1, partial[0], partial[4]),
    )
    return attn, stream, qkv_next


def absorb(running, query_rows, key_row_block, value_rows, visible, score_scale):
    peak_old, total, mixed = running
    scores = (
        jnp.einsum("tkgd,rkd->tkgr", query_rows, key_row_block, preferred_element_type=jnp.float32)
        * score_scale
    )
    seen = visible[:, None, None, :]
    peak_new = jnp.maximum(peak_old, jnp.max(jnp.where(seen, scores, -jnp.inf), axis=-1))
    factor = jnp.exp(peak_old - peak_new)
    weights_full = jnp.where(seen, jnp.exp(scores - peak_new[..., None]), 0.0)
    total = total * factor + jnp.sum(weights_full, axis=-1)
    mixed = mixed * factor[..., None] + jnp.einsum(
        "tkgr,rkd->tkgd",
        weights_full.astype(jnp.bfloat16),
        value_rows,
        preferred_element_type=jnp.float32,
    )
    return (peak_new, total, mixed)


def on_device(
    fresh_queries,
    fresh_keys,
    fresh_values,
    cache,
    pool_root,
    branch_owner,
    branch_len,
    branch_root,
    request_branch,
    token_request,
    residual,
    wo_t,
    norm_gain,
    w_qkv,
):
    seq_count = lax.axis_size("seq")
    root_count = seq_count // 4
    tok_rows = fresh_queries.shape[0]
    kv_local = fresh_keys.shape[1] // HEAD_SIZE
    query_groups = QUERY_HEADS // KEY_VALUE_HEADS
    score_scale = HEAD_SIZE ** (-0.5)
    slot_count = cache.shape[1] - pool_root.shape[1]
    owner_ids = jnp.arange(seq_count, dtype=jnp.int32)
    tags = cache_tags(pool_root, branch_owner, branch_len, root_count, slot_count, owner_ids)
    requests, token_branch = token_branches(request_branch, token_request)
    branch_ids = jnp.arange(branch_root.shape[0], dtype=jnp.int32)
    token_root = jnp.sum(
        jnp.where(token_branch[:, None] == branch_ids[None, :], branch_root[None, :], 0), axis=1
    )
    query_rows = fresh_queries.reshape(tok_rows, kv_local, query_groups, HEAD_SIZE)
    incoming_keys = fresh_keys.reshape(tok_rows, kv_local, HEAD_SIZE)
    incoming_values = fresh_values.reshape(tok_rows, kv_local, HEAD_SIZE)
    positions = jnp.arange(tok_rows, dtype=jnp.int32)
    own_visible = (requests[None, :] == requests[:, None]) & (
        positions[None, :] <= positions[:, None]
    )
    start_state = (
        jnp.full((tok_rows, kv_local, query_groups), -jnp.inf, jnp.float32),
        jnp.zeros((tok_rows, kv_local, query_groups), jnp.float32),
        jnp.zeros((tok_rows, kv_local, query_groups, HEAD_SIZE), jnp.float32),
    )
    state = absorb(
        start_state, query_rows, incoming_keys, incoming_values, own_visible, score_scale
    )
    piece = lax.all_gather(cache, "seq", axis=1, tiled=True)
    rows = piece.shape[1]
    block = 512 if rows > 512 and rows % 512 == 0 else rows
    key_blocks = piece[0].reshape(rows // block, block, kv_local, HEAD_SIZE)
    value_blocks = piece[1].reshape(rows // block, block, kv_local, HEAD_SIZE)
    tag_blocks = tags.reshape(rows // block, block)

    def one_block(running, parts):
        key_row_block, value_rows, tag_rows = parts
        visible = (tag_rows[None, :] == token_root[:, None]) | (
            tag_rows[None, :] == root_count + token_branch[:, None]
        )
        updated = absorb(running, query_rows, key_row_block, value_rows, visible, score_scale)
        return (updated, None)

    state, unused = lax.scan(one_block, state, (key_blocks, value_blocks, tag_blocks))
    peak_final, total_final, mixed_final = state
    attn = (
        (mixed_final / total_final[..., None])
        .reshape(tok_rows, kv_local * query_groups * HEAD_SIZE)
        .astype(jnp.bfloat16)
    )
    partial_value = lax.dot_general(
        attn,
        lax.all_gather(wo_t, "seq", axis=0, tiled=True),
        (((1,), (1,)), ((), ())),
        preferred_element_type=jnp.float32,
    )
    summed = lax.psum(partial_value.astype(jnp.bfloat16), "mp").astype(jnp.float32)
    stream = (residual.astype(jnp.float32) + summed).astype(jnp.bfloat16)
    widened = stream.astype(jnp.float32)
    mean_square = jnp.mean(widened * widened, axis=-1, keepdims=True)
    normed = (widened * lax.rsqrt(mean_square + 1e-06) * norm_gain[None, :]).astype(jnp.bfloat16)
    qkv_sum = jnp.dot(
        normed, lax.all_gather(w_qkv, "seq", axis=0, tiled=True), preferred_element_type=jnp.float32
    )
    return (attn, stream, qkv_sum.astype(jnp.bfloat16))


def solution(mesh):
    small = mesh.shape["seq"] == 8 and mesh.shape["mp"] == 4
    seq, mp = "seq", "mp"
    if small:
        mesh = Mesh(mesh.devices.reshape(4, 2, 2, 2), ("z", "y", "x", "c"))
        seq, mp = ("z", "y"), ("x", "c")
    return jax.shard_map(
        on_block if small else on_device,
        mesh=mesh,
        in_specs=(
            P(seq, mp),
            P(seq, mp),
            P(seq, mp),
            P(None, seq, mp),
            P(),
            P(),
            P(),
            P(),
            P(seq, None),
            P(seq, None),
            P(seq, None),
            P(seq, mp),
            P(),
            P(seq, mp),
        ),
        out_specs=(P(seq, mp), P(seq, None), P(seq, mp)),
        check_vma=False,
    )
```

```python
import jax
import jax.numpy as jnp
from jax import lax
from jax.experimental import pallas as pl
from jax.experimental.pallas import tpu as pltpu
from jax.sharding import Mesh
from jax.sharding import PartitionSpec as P

QUERY_HEADS = 16
KEY_VALUE_HEADS = 8
HEAD_SIZE = 128
NT = (((1,), (1,)), ((), ()))
TN = (((0,), (0,)), ((), ()))
F32 = jnp.float32
HIDDEN = -1e30
BF16 = jnp.bfloat16


def cache_tags(pool_root, branch_owner, branch_len, root_count, slot_count, owner_ids):
    branch_count = branch_owner.shape[0]
    branch_ids = jnp.arange(branch_count, dtype=jnp.int32)
    owned = jnp.sum(
        jnp.where(branch_owner[None, :] == owner_ids[:, None], branch_ids[None, :], 0), axis=1
    )
    owned_length = jnp.sum(
        jnp.where(branch_ids[None, :] == owned[:, None], branch_len[None, :], 0), axis=1
    )
    slot_ids = jnp.arange(slot_count, dtype=jnp.int32)
    branch_tags = jnp.where(
        slot_ids[None, :] < owned_length[:, None], root_count + owned[:, None], -1
    )
    return jnp.concatenate([pool_root, branch_tags], axis=1).reshape(-1)


def token_branches(request_branch, token_request):
    requests = token_request[0]
    local_branches = request_branch[0]
    request_ids = jnp.arange(local_branches.shape[0], dtype=jnp.int32)
    token_branch = jnp.sum(
        jnp.where(requests[:, None] == request_ids[None, :], local_branches[None, :], 0), axis=1
    )
    return requests, token_branch


def head_lanes(h):
    return slice(h * HEAD_SIZE, (h + 1) * HEAD_SIZE)


def seq_index():
    return 2 * lax.axis_index("z") + lax.axis_index("y")


def chunk_offset(e, k, width):
    return pl.multiple_of((e ^ (k // 2)) * (2 * width) + (k % 2) * width, width)


def mp_index():
    return 2 * lax.axis_index("x") + lax.axis_index("c")


def attend_kernel(local_ref, res_ref, bias_ref, *refs):
    caches, out_ref, sends = refs[:-5], refs[-5], refs[-4:]
    e, m = seq_index(), mp_index()
    tok, wide = out_ref.shape
    kv = caches[0].shape[2]
    q_ref, kf_ref, vf_ref = (
        local_ref.at[:, :wide],
        local_ref.at[:, wide : wide + kv],
        local_ref.at[:, wide + kv :],
    )
    rows = caches[0].shape[1]
    bias = jnp.concatenate(
        [bias_ref[:tok]]
        + [
            bias_ref[pl.ds(pl.multiple_of(tok + (e ^ s) * rows, rows), rows), :]
            for s in range(len(caches))
        ],
        axis=0,
    )
    for k in range(kf_ref.shape[1] // HEAD_SIZE):
        lanes, first, second = head_lanes(k), head_lanes(2 * k), head_lanes(2 * k + 1)
        keys = jnp.concatenate([kf_ref[:, lanes]] + [c[0, :, lanes] for c in caches], axis=0)
        values = jnp.concatenate([vf_ref[:, lanes]] + [c[1, :, lanes] for c in caches], axis=0)
        queries = jnp.concatenate([q_ref[:, first], q_ref[:, second]], axis=0)
        scores = (
            lax.dot_general(keys, queries, NT, preferred_element_type=F32) * HEAD_SIZE**-0.5 + bias
        )
        peak = jnp.max(scores, axis=0, keepdims=True)
        prob = jnp.exp(scores - peak)
        total = jnp.sum(prob, axis=0, keepdims=True)
        mixed = lax.dot_general(values, prob.astype(BF16), TN, preferred_element_type=F32)
        attn = (mixed / total).T.astype(BF16)
        for ref in (out_ref, *sends):
            ref[:, first] = attn[:tok]
            ref[:, second] = attn[tok:]
    width = sends[0].shape[1] - wide
    for s, ref in enumerate(sends):
        ref[:, wide:] = res_ref[:, pl.ds(chunk_offset(e ^ (2 * s), m, width), width)]


def project_kernel(a2, a3, a1, a0, own_ref, par_ref, o0, o1, o2, o3, hold):
    m = mp_index()
    half, wide = own_ref.shape
    blocks = (a0, a1, a2, a3)
    attn = jnp.concatenate([a[:, :wide] for a in blocks], axis=0)
    rest = jnp.concatenate([a[:, wide:] for a in blocks], axis=0)
    hold[:, :half] = lax.dot_general(attn, own_ref[...], NT, preferred_element_type=F32)
    hold[:, half:] = lax.dot_general(attn, par_ref[...], NT, preferred_element_type=F32)
    width = o0.shape[1]
    for j, out in enumerate((o0, o1, o2, o3)):
        chunk = hold[:, pl.ds(pl.multiple_of((m ^ j) * width, width), width)]
        out[...] = chunk + rest.astype(F32) if j == 0 else chunk.astype(BF16)


def combine_kernel(r2, r3, r1, r0, out, t2, t3):
    tok = t2.shape[0]
    stream = (
        r0[...] + r1[...].astype(F32) + r2[...].astype(F32) + r3[...].astype(F32)
    ).astype(BF16)
    out[...] = stream
    t2[...] = stream[2 * tok : 3 * tok]
    t3[...] = stream[3 * tok :]


def qkv_kernel(x0, x1, x2, x3, gain_ref, own_ref, par_ref, t3, t2, o0, o1, o2, o3, near, packed, hold):
    e, m = seq_index(), mp_index()
    width = x0.shape[1]
    half, columns = own_ref.shape
    tok = o0.shape[0]
    for j, part in enumerate((x0, x1, x2, x3)):
        k = m ^ j
        gain = gain_ref[:, pl.ds(chunk_offset(e, k, width), width)]
        at = pl.multiple_of(k * width, width)
        hold[:, pl.ds(at, width)] = (part[...].astype(F32) * gain).astype(BF16)
        near[:, pl.ds(at, width)] = part[:tok]
        o1[:, pl.ds(pl.multiple_of(columns + at, width), width)] = part[tok : 2 * tok]
    packed[:, :width] = t2[...]
    packed[:, width:] = t3[...]
    product = jnp.dot(hold[:, :half], own_ref[...], preferred_element_type=F32) + jnp.dot(
        hold[:, half:], par_ref[...], preferred_element_type=F32
    )
    for s, out in enumerate((o0, o1, o2, o3)):
        out[:, :columns] = product[s * tok : (s + 1) * tok].astype(out.dtype)


def finish_kernel(p0, p1, p2, p3, y2, y3, y1, y0, near, qkv_ref, stream_ref):
    e, m = seq_index(), mp_index()
    tok, columns = qkv_ref.shape
    width = p0.shape[1] // 2
    squares = jnp.zeros((tok, width), F32)
    blocks = []
    for k in range(4):
        lanes = slice(k * width, (k + 1) * width)
        blocks.append((chunk_offset(e, k, width), near[:, lanes]))
        lanes = slice(columns + k * width, columns + (k + 1) * width)
        blocks.append((chunk_offset(e ^ 2, k, width), y1[:, lanes]))
    for j, part in enumerate((p0, p1, p2, p3)):
        for i, s in enumerate((2, 3)):
            lanes = slice(i * width, (i + 1) * width)
            blocks.append((chunk_offset(e ^ (2 * s), m ^ j, width), part[:, lanes]))
    for at, block in blocks:
        wide = block.astype(F32)
        squares = squares + wide * wide
        stream_ref[:, pl.ds(at, width)] = block
    mean_square = jnp.sum(squares, axis=1, keepdims=True) / stream_ref.shape[1]
    total = (
        y0[...] + y1[:, :columns].astype(F32) + y2[...].astype(F32) + y3[...].astype(F32)
    )
    qkv_ref[...] = (total * lax.rsqrt(mean_square + 1e-06)).astype(BF16)


def call(kernel, out_shape, args, scratch=(), flops=0, moved=1 << 20):
    vmem = pl.BlockSpec(memory_space=pltpu.VMEM)
    return pl.pallas_call(
        kernel,
        out_shape=out_shape,
        in_specs=[vmem] * len(args),
        out_specs=jax.tree.map(lambda _: vmem, out_shape),
        scratch_shapes=list(scratch),
        compiler_params=pltpu.CompilerParams(vmem_limit_bytes=24 << 20),
        cost_estimate=pl.CostEstimate(flops=flops, bytes_accessed=moved, transcendentals=0),
    )(*args)


def swap(value, axes, bits):
    count = lax.axis_size(axes)
    return lax.ppermute(value, axes, [(i, i ^ bits) for i in range(count)])


def on_block(
    fresh_queries,
    fresh_keys,
    fresh_values,
    cache,
    pool_root,
    branch_owner,
    branch_len,
    branch_root,
    request_branch,
    token_request,
    residual,
    wo_t,
    norm_gain,
    w_qkv,
):
    tok, wide = fresh_queries.shape
    width = wo_t.shape[0] // 2
    columns = w_qkv.shape[1]
    sds = jax.ShapeDtypeStruct
    mp = ("x", "c")

    along = [cache] + [swap(cache, "z", s) for s in range(1, 4)]
    beside = swap(cache, "y", 1)

    holders = pool_root.shape[0]
    requests, token_branch = token_branches(request_branch, token_request)
    branch_ids = jnp.arange(branch_root.shape[0], dtype=jnp.int32)
    chosen = token_branch[:, None] == branch_ids[None, :]
    token_root, token_owner, token_length = (
        jnp.sum(jnp.where(chosen, per_branch[None, :], 0), axis=1)
        for per_branch in (branch_root, branch_owner, branch_len)
    )
    positions = jnp.arange(tok, dtype=jnp.int32)
    own_seen = (requests[None, :] == requests[:, None]) & (
        positions[:, None] <= positions[None, :]
    )
    slot_count = cache.shape[1] - pool_root.shape[1]
    slots = jnp.arange(slot_count, dtype=jnp.int32)
    at = jnp.arange(holders, dtype=jnp.int32)
    root_seen = pool_root[:, :, None] == token_root[None, None, :]
    branch_seen = (token_owner[None, None, :] == at[:, None, None]) & (
        slots[None, :, None] < token_length[None, None, :]
    )
    pool_seen = jnp.concatenate([root_seen, branch_seen], axis=1).reshape(-1, tok)
    seen = jnp.concatenate([own_seen, pool_seen], axis=0)
    bias = jnp.where(jnp.concatenate([seen, seen], axis=1), 0.0, HIDDEN).astype(F32)

    local = jnp.concatenate([fresh_queries, fresh_keys, fresh_values], axis=1)
    along[1:], bias, local = lax.optimization_barrier((along[1:], bias, local))
    across = [beside] + [swap(mine, "y", 1) for mine in along[1:]]
    blocks = [block for pair in zip(along, across) for block in pair]
    wo_pair = swap(wo_t, "y", 1)
    blocks, wo_pair, wq_later = lax.optimization_barrier((blocks, wo_pair, w_qkv))
    wq_pair = swap(wq_later, "y", 1)
    attn, *sends = call(
        attend_kernel,
        [sds((tok, wide), BF16)] + [sds((tok, wide + width), BF16)] * 4,
        (local, residual, bias, *blocks),
        flops=1 << 26,
    )
    a2, a3, a1 = (swap(sends[s], "z", s) for s in (2, 3, 1))
    sums = call(
        project_kernel,
        [sds((4 * tok, width), F32)] + [sds((4 * tok, width), BF16)] * 3,
        (a2, a3, a1, sends[0], wo_t, wo_pair),
        scratch=[pltpu.VMEM((4 * tok, 4 * width), F32)],
        flops=1 << 27,
    )
    sums = [sums[0]] + [swap(sums[j], mp, j) for j in range(1, 4)]
    made = call(
        combine_kernel,
        [sds((4 * tok, width), BF16)] + [sds((tok, width), BF16)] * 2,
        (sums[2], sums[3], sums[1], sums[0]),
    )
    made, wq_pair = lax.optimization_barrier((made, wq_pair))
    slices = [made[0]] + [swap(made[0], mp, j) for j in range(1, 4)]
    home = [swap(made[2], "z", 3), swap(made[1], "z", 2)]
    partial = call(
        qkv_kernel,
        [
            sds((tok, columns), F32),
            sds((tok, columns + 4 * width), BF16),
            sds((tok, columns), BF16),
            sds((tok, columns), BF16),
            sds((tok, 4 * width), BF16),
            sds((tok, 2 * width), BF16),
        ],
        (*slices, norm_gain[None, :], w_qkv, wq_pair, *home),
        scratch=[pltpu.VMEM((4 * tok, 4 * width), BF16)],
        flops=1 << 28,
    )
    y1, y2, y3 = (swap(partial[s], "z", s) for s in (1, 2, 3))
    packed = partial[5]
    pieces = [packed] + [swap(packed, mp, j) for j in range(1, 4)]
    qkv_next, stream = call(
        finish_kernel,
        [sds((tok, columns), BF16), sds(residual.shape, BF16)],
        (*pieces, y2, y3, y1, partial[0], partial[4]),
    )
    return attn, stream, qkv_next


def absorb(running, query_rows, key_row_block, value_rows, visible, score_scale):
    peak_old, total, mixed = running
    scores = (
        jnp.einsum("tkgd,rkd->tkgr", query_rows, key_row_block, preferred_element_type=jnp.float32)
        * score_scale
    )
    seen = visible[:, None, None, :]
    peak_new = jnp.maximum(peak_old, jnp.max(jnp.where(seen, scores, -jnp.inf), axis=-1))
    factor = jnp.exp(peak_old - peak_new)
    weights_full = jnp.where(seen, jnp.exp(scores - peak_new[..., None]), 0.0)
    total = total * factor + jnp.sum(weights_full, axis=-1)
    mixed = mixed * factor[..., None] + jnp.einsum(
        "tkgr,rkd->tkgd",
        weights_full.astype(jnp.bfloat16),
        value_rows,
        preferred_element_type=jnp.float32,
    )
    return (peak_new, total, mixed)


def on_device(
    fresh_queries,
    fresh_keys,
    fresh_values,
    cache,
    pool_root,
    branch_owner,
    branch_len,
    branch_root,
    request_branch,
    token_request,
    residual,
    wo_t,
    norm_gain,
    w_qkv,
):
    seq_count = lax.axis_size("seq")
    root_count = seq_count // 4
    tok_rows = fresh_queries.shape[0]
    kv_local = fresh_keys.shape[1] // HEAD_SIZE
    query_groups = QUERY_HEADS // KEY_VALUE_HEADS
    score_scale = HEAD_SIZE ** (-0.5)
    slot_count = cache.shape[1] - pool_root.shape[1]
    owner_ids = jnp.arange(seq_count, dtype=jnp.int32)
    tags = cache_tags(pool_root, branch_owner, branch_len, root_count, slot_count, owner_ids)
    requests, token_branch = token_branches(request_branch, token_request)
    branch_ids = jnp.arange(branch_root.shape[0], dtype=jnp.int32)
    token_root = jnp.sum(
        jnp.where(token_branch[:, None] == branch_ids[None, :], branch_root[None, :], 0), axis=1
    )
    query_rows = fresh_queries.reshape(tok_rows, kv_local, query_groups, HEAD_SIZE)
    incoming_keys = fresh_keys.reshape(tok_rows, kv_local, HEAD_SIZE)
    incoming_values = fresh_values.reshape(tok_rows, kv_local, HEAD_SIZE)
    positions = jnp.arange(tok_rows, dtype=jnp.int32)
    own_visible = (requests[None, :] == requests[:, None]) & (
        positions[None, :] <= positions[:, None]
    )
    start_state = (
        jnp.full((tok_rows, kv_local, query_groups), -jnp.inf, jnp.float32),
        jnp.zeros((tok_rows, kv_local, query_groups), jnp.float32),
        jnp.zeros((tok_rows, kv_local, query_groups, HEAD_SIZE), jnp.float32),
    )
    state = absorb(
        start_state, query_rows, incoming_keys, incoming_values, own_visible, score_scale
    )
    piece = lax.all_gather(cache, "seq", axis=1, tiled=True)
    rows = piece.shape[1]
    block = 512 if rows > 512 and rows % 512 == 0 else rows
    key_blocks = piece[0].reshape(rows // block, block, kv_local, HEAD_SIZE)
    value_blocks = piece[1].reshape(rows // block, block, kv_local, HEAD_SIZE)
    tag_blocks = tags.reshape(rows // block, block)

    def one_block(running, parts):
        key_row_block, value_rows, tag_rows = parts
        visible = (tag_rows[None, :] == token_root[:, None]) | (
            tag_rows[None, :] == root_count + token_branch[:, None]
        )
        updated = absorb(running, query_rows, key_row_block, value_rows, visible, score_scale)
        return (updated, None)

    state, unused = lax.scan(one_block, state, (key_blocks, value_blocks, tag_blocks))
    peak_final, total_final, mixed_final = state
    attn = (
        (mixed_final / total_final[..., None])
        .reshape(tok_rows, kv_local * query_groups * HEAD_SIZE)
        .astype(jnp.bfloat16)
    )
    partial_value = lax.dot_general(
        attn,
        lax.all_gather(wo_t, "seq", axis=0, tiled=True),
        (((1,), (1,)), ((), ())),
        preferred_element_type=jnp.float32,
    )
    summed = lax.psum(partial_value.astype(jnp.bfloat16), "mp").astype(jnp.float32)
    stream = (residual.astype(jnp.float32) + summed).astype(jnp.bfloat16)
    widened = stream.astype(jnp.float32)
    mean_square = jnp.mean(widened * widened, axis=-1, keepdims=True)
    normed = (widened * lax.rsqrt(mean_square + 1e-06) * norm_gain[None, :]).astype(jnp.bfloat16)
    qkv_sum = jnp.dot(
        normed, lax.all_gather(w_qkv, "seq", axis=0, tiled=True), preferred_element_type=jnp.float32
    )
    return (attn, stream, qkv_sum.astype(jnp.bfloat16))


def solution(mesh):
    small = mesh.shape["seq"] == 8 and mesh.shape["mp"] == 4
    seq, mp = "seq", "mp"
    if small:
        mesh = Mesh(mesh.devices.reshape(4, 2, 2, 2), ("z", "y", "x", "c"))
        seq, mp = ("z", "y"), ("x", "c")
    return jax.shard_map(
        on_block if small else on_device,
        mesh=mesh,
        in_specs=(
            P(seq, mp),
            P(seq, mp),
            P(seq, mp),
            P(None, seq, mp),
            P(),
            P(),
            P(),
            P(),
            P(seq, None),
            P(seq, None),
            P(seq, None),
            P(seq, mp),
            P(),
            P(seq, mp),
        ),
        out_specs=(P(seq, mp), P(seq, None), P(seq, mp)),
        check_vma=False,
    )
```

```python
import jax
import jax.numpy as jnp
from jax import lax
from jax.experimental import pallas as pl
from jax.experimental.pallas import tpu as pltpu
from jax.sharding import Mesh
from jax.sharding import PartitionSpec as P

QUERY_HEADS = 16
KEY_VALUE_HEADS = 8
HEAD_SIZE = 128
NT = (((1,), (1,)), ((), ()))
TN = (((0,), (0,)), ((), ()))
F32 = jnp.float32
HIDDEN = -1e30
BF16 = jnp.bfloat16


def cache_tags(pool_root, branch_owner, branch_len, root_count, slot_count, owner_ids):
    branch_count = branch_owner.shape[0]
    branch_ids = jnp.arange(branch_count, dtype=jnp.int32)
    owned = jnp.sum(
        jnp.where(branch_owner[None, :] == owner_ids[:, None], branch_ids[None, :], 0), axis=1
    )
    owned_length = jnp.sum(
        jnp.where(branch_ids[None, :] == owned[:, None], branch_len[None, :], 0), axis=1
    )
    slot_ids = jnp.arange(slot_count, dtype=jnp.int32)
    branch_tags = jnp.where(
        slot_ids[None, :] < owned_length[:, None], root_count + owned[:, None], -1
    )
    return jnp.concatenate([pool_root, branch_tags], axis=1).reshape(-1)


def token_branches(request_branch, token_request):
    requests = token_request[0]
    local_branches = request_branch[0]
    request_ids = jnp.arange(local_branches.shape[0], dtype=jnp.int32)
    token_branch = jnp.sum(
        jnp.where(requests[:, None] == request_ids[None, :], local_branches[None, :], 0), axis=1
    )
    return requests, token_branch


def head_lanes(h):
    return slice(h * HEAD_SIZE, (h + 1) * HEAD_SIZE)


def seq_index():
    return 2 * lax.axis_index("z") + lax.axis_index("y")


def chunk_offset(e, k, width):
    return pl.multiple_of((e ^ (k // 2)) * (2 * width) + (k % 2) * width, width)


def mp_index():
    return 2 * lax.axis_index("x") + lax.axis_index("c")


def join_kernel(z1, z2, z3, out_ref):
    for i, part in enumerate((z1, z2, z3)):
        out_ref[2 * i : 2 * i + 2] = part[...]


def attend_kernel(local_ref, res_ref, bias_ref, *refs):
    own, beside, z1, z2, z3, moved, out_ref, *sends = refs
    caches = (own, beside, z1, moved.at[:2], z2, moved.at[2:4], z3, moved.at[4:])
    e, m = seq_index(), mp_index()
    tok, wide = out_ref.shape
    kv = caches[0].shape[2]
    q_ref, kf_ref, vf_ref = (
        local_ref.at[:, :wide],
        local_ref.at[:, wide : wide + kv],
        local_ref.at[:, wide + kv :],
    )
    rows = caches[0].shape[1]
    bias = jnp.concatenate(
        [bias_ref[:tok]]
        + [
            bias_ref[pl.ds(pl.multiple_of(tok + (e ^ s) * rows, rows), rows), :]
            for s in range(len(caches))
        ],
        axis=0,
    )
    for k in range(kf_ref.shape[1] // HEAD_SIZE):
        lanes, first, second = head_lanes(k), head_lanes(2 * k), head_lanes(2 * k + 1)
        keys = jnp.concatenate([kf_ref[:, lanes]] + [c[0, :, lanes] for c in caches], axis=0)
        values = jnp.concatenate([vf_ref[:, lanes]] + [c[1, :, lanes] for c in caches], axis=0)
        queries = jnp.concatenate([q_ref[:, first], q_ref[:, second]], axis=0)
        scores = (
            lax.dot_general(keys, queries, NT, preferred_element_type=F32) * HEAD_SIZE**-0.5 + bias
        )
        peak = jnp.max(scores, axis=0, keepdims=True)
        prob = jnp.exp(scores - peak)
        total = jnp.sum(prob, axis=0, keepdims=True)
        mixed = lax.dot_general(values, prob.astype(BF16), TN, preferred_element_type=F32)
        attn = (mixed / total).T.astype(BF16)
        for ref in (out_ref, *sends):
            ref[:, first] = attn[:tok]
            ref[:, second] = attn[tok:]
    width = sends[0].shape[1] - wide
    for s, ref in enumerate(sends):
        ref[:, wide:] = res_ref[:, pl.ds(chunk_offset(e ^ (2 * s), m, width), width)]


def project_kernel(a2, a3, a1, a0, own_ref, par_ref, o0, o1, o2, o3, hold):
    m = mp_index()
    half, wide = own_ref.shape
    blocks = (a0, a1, a2, a3)
    attn = jnp.concatenate([a[:, :wide] for a in blocks], axis=0)
    rest = jnp.concatenate([a[:, wide:] for a in blocks], axis=0)
    hold[:, :half] = lax.dot_general(attn, own_ref[...], NT, preferred_element_type=F32)
    hold[:, half:] = lax.dot_general(attn, par_ref[...], NT, preferred_element_type=F32)
    width = o0.shape[1]
    for j, out in enumerate((o0, o1, o2, o3)):
        chunk = hold[:, pl.ds(pl.multiple_of((m ^ j) * width, width), width)]
        out[...] = chunk + rest.astype(F32) if j == 0 else chunk.astype(BF16)


def combine_kernel(r2, r3, r1, r0, out, t2, t3):
    tok = t2.shape[0]
    stream = (
        r0[...] + r1[...].astype(F32) + r2[...].astype(F32) + r3[...].astype(F32)
    ).astype(BF16)
    out[...] = stream
    t2[...] = stream[2 * tok : 3 * tok]
    t3[...] = stream[3 * tok :]


def qkv_kernel(x0, x1, x2, x3, gain_ref, own_ref, par_ref, t3, t2, o0, o1, o2, o3, near, packed, hold):
    e, m = seq_index(), mp_index()
    width = x0.shape[1]
    half, columns = own_ref.shape
    tok = o0.shape[0]
    for j, part in enumerate((x0, x1, x2, x3)):
        k = m ^ j
        gain = gain_ref[:, pl.ds(chunk_offset(e, k, width), width)]
        at = pl.multiple_of(k * width, width)
        hold[:, pl.ds(at, width)] = (part[...].astype(F32) * gain).astype(BF16)
        near[:, pl.ds(at, width)] = part[:tok]
        o1[:, pl.ds(pl.multiple_of(columns + at, width), width)] = part[tok : 2 * tok]
    packed[:, :width] = t2[...]
    packed[:, width:] = t3[...]
    product = jnp.dot(hold[:, :half], own_ref[...], preferred_element_type=F32) + jnp.dot(
        hold[:, half:], par_ref[...], preferred_element_type=F32
    )
    for s, out in enumerate((o0, o1, o2, o3)):
        out[:, :columns] = product[s * tok : (s + 1) * tok].astype(out.dtype)


def finish_kernel(p0, p1, p2, p3, y2, y3, y1, y0, near, qkv_ref, stream_ref):
    e, m = seq_index(), mp_index()
    tok, columns = qkv_ref.shape
    width = p0.shape[1] // 2
    squares = jnp.zeros((tok, width), F32)
    blocks = []
    for k in range(4):
        lanes = slice(k * width, (k + 1) * width)
        blocks.append((chunk_offset(e, k, width), near[:, lanes]))
        lanes = slice(columns + k * width, columns + (k + 1) * width)
        blocks.append((chunk_offset(e ^ 2, k, width), y1[:, lanes]))
    for j, part in enumerate((p0, p1, p2, p3)):
        for i, s in enumerate((2, 3)):
            lanes = slice(i * width, (i + 1) * width)
            blocks.append((chunk_offset(e ^ (2 * s), m ^ j, width), part[:, lanes]))
    for at, block in blocks:
        wide = block.astype(F32)
        squares = squares + wide * wide
        stream_ref[:, pl.ds(at, width)] = block
    mean_square = jnp.sum(squares, axis=1, keepdims=True) / stream_ref.shape[1]
    total = (
        y0[...] + y1[:, :columns].astype(F32) + y2[...].astype(F32) + y3[...].astype(F32)
    )
    qkv_ref[...] = (total * lax.rsqrt(mean_square + 1e-06)).astype(BF16)


def call(kernel, out_shape, args, scratch=(), flops=0, moved=1 << 20):
    vmem = pl.BlockSpec(memory_space=pltpu.VMEM)
    return pl.pallas_call(
        kernel,
        out_shape=out_shape,
        in_specs=[vmem] * len(args),
        out_specs=jax.tree.map(lambda _: vmem, out_shape),
        scratch_shapes=list(scratch),
        compiler_params=pltpu.CompilerParams(vmem_limit_bytes=24 << 20),
        cost_estimate=pl.CostEstimate(flops=flops, bytes_accessed=moved, transcendentals=0),
    )(*args)


def swap(value, axes, bits):
    count = lax.axis_size(axes)
    return lax.ppermute(value, axes, [(i, i ^ bits) for i in range(count)])


def on_block(
    fresh_queries,
    fresh_keys,
    fresh_values,
    cache,
    pool_root,
    branch_owner,
    branch_len,
    branch_root,
    request_branch,
    token_request,
    residual,
    wo_t,
    norm_gain,
    w_qkv,
):
    tok, wide = fresh_queries.shape
    width = wo_t.shape[0] // 2
    columns = w_qkv.shape[1]
    sds = jax.ShapeDtypeStruct
    mp = ("x", "c")

    along = [cache] + [swap(cache, "z", s) for s in range(1, 4)]
    beside = swap(cache, "y", 1)

    holders = pool_root.shape[0]
    requests, token_branch = token_branches(request_branch, token_request)
    branch_ids = jnp.arange(branch_root.shape[0], dtype=jnp.int32)
    chosen = token_branch[:, None] == branch_ids[None, :]
    token_root, token_owner, token_length = (
        jnp.sum(jnp.where(chosen, per_branch[None, :], 0), axis=1)
        for per_branch in (branch_root, branch_owner, branch_len)
    )
    positions = jnp.arange(tok, dtype=jnp.int32)
    own_seen = (requests[None, :] == requests[:, None]) & (
        positions[:, None] <= positions[None, :]
    )
    slot_count = cache.shape[1] - pool_root.shape[1]
    slots = jnp.arange(slot_count, dtype=jnp.int32)
    at = jnp.arange(holders, dtype=jnp.int32)
    root_seen = pool_root[:, :, None] == token_root[None, None, :]
    branch_seen = (token_owner[None, None, :] == at[:, None, None]) & (
        slots[None, :, None] < token_length[None, None, :]
    )
    pool_seen = jnp.concatenate([root_seen, branch_seen], axis=1).reshape(-1, tok)
    seen = jnp.concatenate([own_seen, pool_seen], axis=0)
    bias = jnp.where(jnp.concatenate([seen, seen], axis=1), 0.0, HIDDEN).astype(F32)

    local = jnp.concatenate([fresh_queries, fresh_keys, fresh_values], axis=1)
    along[1:], bias, local = lax.optimization_barrier((along[1:], bias, local))
    joined = call(
        join_kernel, sds((3 * cache.shape[0],) + cache.shape[1:], BF16), tuple(along[1:])
    )
    blocks = [cache, beside, *along[1:], swap(joined, "y", 1)]
    wo_pair = swap(wo_t, "y", 1)
    blocks, wo_pair, wq_later = lax.optimization_barrier((blocks, wo_pair, w_qkv))
    wq_pair = swap(wq_later, "y", 1)
    attn, *sends = call(
        attend_kernel,
        [sds((tok, wide), BF16)] + [sds((tok, wide + width), BF16)] * 4,
        (local, residual, bias, *blocks),
        flops=1 << 26,
    )
    a2, a3, a1 = (swap(sends[s], "z", s) for s in (2, 3, 1))
    sums = call(
        project_kernel,
        [sds((4 * tok, width), F32)] + [sds((4 * tok, width), BF16)] * 3,
        (a2, a3, a1, sends[0], wo_t, wo_pair),
        scratch=[pltpu.VMEM((4 * tok, 4 * width), F32)],
        flops=1 << 27,
    )
    sums = [sums[0]] + [swap(sums[j], mp, j) for j in range(1, 4)]
    made = call(
        combine_kernel,
        [sds((4 * tok, width), BF16)] + [sds((tok, width), BF16)] * 2,
        (sums[2], sums[3], sums[1], sums[0]),
    )
    made, wq_pair = lax.optimization_barrier((made, wq_pair))
    slices = [made[0]] + [swap(made[0], mp, j) for j in range(1, 4)]
    home = [swap(made[2], "z", 3), swap(made[1], "z", 2)]
    partial = call(
        qkv_kernel,
        [
            sds((tok, columns), F32),
            sds((tok, columns + 4 * width), BF16),
            sds((tok, columns), BF16),
            sds((tok, columns), BF16),
            sds((tok, 4 * width), BF16),
            sds((tok, 2 * width), BF16),
        ],
        (*slices, norm_gain[None, :], w_qkv, wq_pair, *home),
        scratch=[pltpu.VMEM((4 * tok, 4 * width), BF16)],
        flops=1 << 28,
    )
    y1, y2, y3 = (swap(partial[s], "z", s) for s in (1, 2, 3))
    packed = partial[5]
    pieces = [packed] + [swap(packed, mp, j) for j in range(1, 4)]
    qkv_next, stream = call(
        finish_kernel,
        [sds((tok, columns), BF16), sds(residual.shape, BF16)],
        (*pieces, y2, y3, y1, partial[0], partial[4]),
    )
    return attn, stream, qkv_next


def absorb(running, query_rows, key_row_block, value_rows, visible, score_scale):
    peak_old, total, mixed = running
    scores = (
        jnp.einsum("tkgd,rkd->tkgr", query_rows, key_row_block, preferred_element_type=jnp.float32)
        * score_scale
    )
    seen = visible[:, None, None, :]
    peak_new = jnp.maximum(peak_old, jnp.max(jnp.where(seen, scores, -jnp.inf), axis=-1))
    factor = jnp.exp(peak_old - peak_new)
    weights_full = jnp.where(seen, jnp.exp(scores - peak_new[..., None]), 0.0)
    total = total * factor + jnp.sum(weights_full, axis=-1)
    mixed = mixed * factor[..., None] + jnp.einsum(
        "tkgr,rkd->tkgd",
        weights_full.astype(jnp.bfloat16),
        value_rows,
        preferred_element_type=jnp.float32,
    )
    return (peak_new, total, mixed)


def on_device(
    fresh_queries,
    fresh_keys,
    fresh_values,
    cache,
    pool_root,
    branch_owner,
    branch_len,
    branch_root,
    request_branch,
    token_request,
    residual,
    wo_t,
    norm_gain,
    w_qkv,
):
    seq_count = lax.axis_size("seq")
    root_count = seq_count // 4
    tok_rows = fresh_queries.shape[0]
    kv_local = fresh_keys.shape[1] // HEAD_SIZE
    query_groups = QUERY_HEADS // KEY_VALUE_HEADS
    score_scale = HEAD_SIZE ** (-0.5)
    slot_count = cache.shape[1] - pool_root.shape[1]
    owner_ids = jnp.arange(seq_count, dtype=jnp.int32)
    tags = cache_tags(pool_root, branch_owner, branch_len, root_count, slot_count, owner_ids)
    requests, token_branch = token_branches(request_branch, token_request)
    branch_ids = jnp.arange(branch_root.shape[0], dtype=jnp.int32)
    token_root = jnp.sum(
        jnp.where(token_branch[:, None] == branch_ids[None, :], branch_root[None, :], 0), axis=1
    )
    query_rows = fresh_queries.reshape(tok_rows, kv_local, query_groups, HEAD_SIZE)
    incoming_keys = fresh_keys.reshape(tok_rows, kv_local, HEAD_SIZE)
    incoming_values = fresh_values.reshape(tok_rows, kv_local, HEAD_SIZE)
    positions = jnp.arange(tok_rows, dtype=jnp.int32)
    own_visible = (requests[None, :] == requests[:, None]) & (
        positions[None, :] <= positions[:, None]
    )
    start_state = (
        jnp.full((tok_rows, kv_local, query_groups), -jnp.inf, jnp.float32),
        jnp.zeros((tok_rows, kv_local, query_groups), jnp.float32),
        jnp.zeros((tok_rows, kv_local, query_groups, HEAD_SIZE), jnp.float32),
    )
    state = absorb(
        start_state, query_rows, incoming_keys, incoming_values, own_visible, score_scale
    )
    piece = lax.all_gather(cache, "seq", axis=1, tiled=True)
    rows = piece.shape[1]
    block = 512 if rows > 512 and rows % 512 == 0 else rows
    key_blocks = piece[0].reshape(rows // block, block, kv_local, HEAD_SIZE)
    value_blocks = piece[1].reshape(rows // block, block, kv_local, HEAD_SIZE)
    tag_blocks = tags.reshape(rows // block, block)

    def one_block(running, parts):
        key_row_block, value_rows, tag_rows = parts
        visible = (tag_rows[None, :] == token_root[:, None]) | (
            tag_rows[None, :] == root_count + token_branch[:, None]
        )
        updated = absorb(running, query_rows, key_row_block, value_rows, visible, score_scale)
        return (updated, None)

    state, unused = lax.scan(one_block, state, (key_blocks, value_blocks, tag_blocks))
    peak_final, total_final, mixed_final = state
    attn = (
        (mixed_final / total_final[..., None])
        .reshape(tok_rows, kv_local * query_groups * HEAD_SIZE)
        .astype(jnp.bfloat16)
    )
    partial_value = lax.dot_general(
        attn,
        lax.all_gather(wo_t, "seq", axis=0, tiled=True),
        (((1,), (1,)), ((), ())),
        preferred_element_type=jnp.float32,
    )
    summed = lax.psum(partial_value.astype(jnp.bfloat16), "mp").astype(jnp.float32)
    stream = (residual.astype(jnp.float32) + summed).astype(jnp.bfloat16)
    widened = stream.astype(jnp.float32)
    mean_square = jnp.mean(widened * widened, axis=-1, keepdims=True)
    normed = (widened * lax.rsqrt(mean_square + 1e-06) * norm_gain[None, :]).astype(jnp.bfloat16)
    qkv_sum = jnp.dot(
        normed, lax.all_gather(w_qkv, "seq", axis=0, tiled=True), preferred_element_type=jnp.float32
    )
    return (attn, stream, qkv_sum.astype(jnp.bfloat16))


def solution(mesh):
    small = mesh.shape["seq"] == 8 and mesh.shape["mp"] == 4
    seq, mp = "seq", "mp"
    if small:
        mesh = Mesh(mesh.devices.reshape(4, 2, 2, 2), ("z", "y", "x", "c"))
        seq, mp = ("z", "y"), ("x", "c")
    return jax.shard_map(
        on_block if small else on_device,
        mesh=mesh,
        in_specs=(
            P(seq, mp),
            P(seq, mp),
            P(seq, mp),
            P(None, seq, mp),
            P(),
            P(),
            P(),
            P(),
            P(seq, None),
            P(seq, None),
            P(seq, None),
            P(seq, mp),
            P(),
            P(seq, mp),
        ),
        out_specs=(P(seq, mp), P(seq, None), P(seq, mp)),
        check_vma=False,
    )
```
